32 devices in a mesh: parts: 2 (over y), row: 4 (over z), col: 4 (over x, core).
Axes of the slice: x: 2, y: 2, z: 4, core: 2. Of those that a mesh axis runs over, the one named last changes fastest.
Arguments:
- charges: bfloat16 [32, 32, 1024], P(('parts', 'row')), parts along dimension 0, may hold values from -6 to 6
- near_blocks: bfloat16 [32, 1024, 1024], P(('parts', 'row', 'col')), parts along dimension 0, may hold values from -0.09375 to 0.09375
- near_rows: int32 [32], P(('parts', 'row', 'col')), parts along dimension 0, may hold values from 0 to 15, as said below
- near_cols: int32 [32], P(('parts', 'row', 'col')), parts along dimension 0, may hold values from 0 to 15, as said below
- far_u: bfloat16 [768, 16, 1024], P(('parts', 'row', 'col')), parts along dimension 0, may hold values from -0.3125 to 0.3125
- far_v: bfloat16 [768, 16, 1024], P(('parts', 'row', 'col')), parts along dimension 0, may hold values from -0.1875 to 0.1875
- far_rows: int32 [768], P(('parts', 'row', 'col')), parts along dimension 0, may hold values from 0 to 15, as said below
- far_cols: int32 [768], P(('parts', 'row', 'col')), parts along dimension 0, may hold values from 0 to 15, as said below
Outputs:
- potential: float32 [32, 32, 1024], P(('parts', 'row'), None, 'col'), parts along dimension 0
The draws below stay inside these ranges and needn't reach their ends.
There are 2 independent parts, one for each index of `parts`. The reference program is written for one: setup_inputs(seed, part) draws one part's arguments, and reference() takes and returns one part's arrays. A program takes and returns all parts, laid end to end along the dimension named above; each array names one. Nothing has to cross between parts.
Inputs may be any that keep to these rules, and one draw needn't show every extreme that they name: `near_rows`: entry e lies in row group g = e // 4: its cluster is one of g * 4 to (g + 1) * 4 - 1. `near_cols`: entry e lies in row group g = e // 4: its cluster is one of g * 4 to (g + 1) * 4 - 1. `far_rows`: entry e has its row cluster in row group g = e // 96, that is one of g * 4 to (g + 1) * 4 - 1. `far_cols`: a column cluster never lies in its entry's own row group; of the 24 entries of one device at most 8 have column clusters in one row group, and some device reaches 8; a pair of clusters may occur in several entries, whose terms add.
All inputs are finite; a program needn't handle non-finite values.
Results may differ from the reference program's by a relative error of at most 0.0026.
Values may be sent and summed in bfloat16 or wider, within the bound.
No kernel may reach another device: no remote copies, remote signals or barrier semaphores. Data moves between devices by JAX's collectives and lax.ppermute only.
A program may use at most 128 MiB of HBM per device.

```python
import jax
import jax.numpy as jnp
from jax import lax

S = 1024
EXC = 32
RANK = 16
CL_ROW = 4
NEAR_DEV = 1
FAR_DEV = 24
NCL = 16
NEAR_TOTAL = 16
FAR_TOTAL = 384
CAP = 8
N_ROW = 4
N_COL = 4


def draw_near_rows(key, part):
    key = jax.random.fold_in(key, 11)
    entry = jnp.arange(NEAR_TOTAL)
    group = entry // (N_COL * NEAR_DEV)
    return (group * CL_ROW + jax.random.randint(key, (NEAR_TOTAL,), 0, CL_ROW)).astype(jnp.int32)


def draw_near_cols(key, part):
    key = jax.random.fold_in(key, 12)
    entry = jnp.arange(NEAR_TOTAL)
    group = entry // (N_COL * NEAR_DEV)
    return (group * CL_ROW + jax.random.randint(key, (NEAR_TOTAL,), 0, CL_ROW)).astype(jnp.int32)


def draw_far_rows(key, part):
    key = jax.random.fold_in(key, 13)
    entry = jnp.arange(FAR_TOTAL)
    group = entry // (N_COL * FAR_DEV)
    return (group * CL_ROW + jax.random.randint(key, (FAR_TOTAL,), 0, CL_ROW)).astype(jnp.int32)


def draw_far_cols(key, part):
    key = jax.random.fold_in(key, 14)
    key_hot, key_prio, key_mix, key_pick = jax.random.split(key, 4)
    device_count = N_ROW * N_COL
    table_size = N_ROW * CAP
    hottest = jax.random.randint(key_hot, (), 0, N_ROW)
    groups = jnp.arange(device_count) // N_COL
    table_owner = jnp.arange(table_size) // CAP
    priority = jax.random.randint(key_prio, (device_count, table_size), 1, 1 << 20)
    priority = jnp.where(table_owner[None, :] == hottest, 0, priority)
    priority = jnp.where(table_owner[None, :] == groups[:, None], 1 << 21, priority)
    scores = priority * table_size + jnp.arange(table_size)[None, :]
    chosen = jnp.argsort(scores, axis=1)[:, :FAR_DEV]
    owners = chosen // CAP
    mixing = jax.random.randint(key_mix, (device_count, FAR_DEV), 0, 1 << 20) * FAR_DEV + jnp.arange(FAR_DEV)[None, :]
    shuffle = jnp.argsort(mixing, axis=1)
    owners = jnp.take_along_axis(owners, shuffle, axis=1)
    within = jax.random.randint(key_pick, (device_count, FAR_DEV), 0, CL_ROW)
    return (owners * CL_ROW + within).reshape(-1).astype(jnp.int32)


def block_levels(key, extent, shards, least, largest):
    def one(dim, parts):
        draws = jax.random.uniform(jax.random.fold_in(jax.random.fold_in(key, 6), dim), (parts,), jnp.float32, least / len(shards), largest / len(shards))
        return jnp.repeat(jnp.exp(draws), extent[dim] // parts).reshape((-1,) + (1,) * (len(extent) - dim - 1))

    loudness = one(*shards[0])
    for cut in shards[1:]:
        loudness = loudness * one(*cut)
    return loudness


def centred(key, extent, scale, most, cuts=(), kind=jnp.bfloat16):
    array = jax.random.normal(key, extent, jnp.float32) * scale
    if len(cuts) > 0:
        array = block_levels(key, extent, cuts, -0.22, 0.18) * array
    return jnp.clip(array, min=-most, max=most).astype(kind)


def setup_inputs(seed: int = 0, part: int = 0) -> dict:
    streams_of = jax.random.split(jax.random.key(seed), 9)
    part_splits = jax.random.split(jax.random.fold_in(streams_of[8], part), 9)
    return {
        "charges": centred(part_splits[0], (NCL, EXC, S), 1.0, 6.0, ((0, 4),)),
        "near_blocks": centred(part_splits[1], (NEAR_TOTAL, S, S), (S * 4) ** -0.5, 0.09375, ((0, 16),)),
        "near_rows": draw_near_rows(jax.random.fold_in(jax.random.fold_in(streams_of[8], part), 71), part),
        "near_cols": draw_near_cols(jax.random.fold_in(jax.random.fold_in(streams_of[8], part), 71), part),
        "far_u": centred(part_splits[4], (FAR_TOTAL, RANK, S), (RANK * FAR_DEV) ** -0.5, 0.3125, ((0, 16),)),
        "far_v": centred(part_splits[5], (FAR_TOTAL, RANK, S), S ** -0.5, 0.1875, ((0, 16),)),
        "far_rows": draw_far_rows(jax.random.fold_in(jax.random.fold_in(streams_of[8], part), 71), part),
        "far_cols": draw_far_cols(jax.random.fold_in(jax.random.fold_in(streams_of[8], part), 71), part),
    }


def reference(charges, near_blocks, near_rows, near_cols, far_u, far_v, far_rows, far_cols):
    potential = jnp.zeros(charges.shape, jnp.float32)

    def near_step(total, item):
        block, row_id, col_id = item
        weight = jnp.where(row_id == col_id, 0.5, 1.0).astype(jnp.float32)
        forward = jnp.dot(charges[col_id], block.T, preferred_element_type=jnp.float32)
        mirror = jnp.dot(charges[row_id], block, preferred_element_type=jnp.float32)
        total = total.at[row_id].add(weight * forward)
        total = total.at[col_id].add(weight * mirror)
        return total, None

    potential, _ = lax.scan(near_step, potential, (near_blocks, near_rows, near_cols))

    def far_step(total, item):
        left, right, row_id, col_id = item
        coef = jnp.dot(charges[col_id], right.T, preferred_element_type=jnp.float32).astype(jnp.bfloat16)
        coef_t = jnp.dot(charges[row_id], left.T, preferred_element_type=jnp.float32).astype(jnp.bfloat16)
        total = total.at[row_id].add(jnp.dot(coef, left, preferred_element_type=jnp.float32))
        total = total.at[col_id].add(jnp.dot(coef_t, right, preferred_element_type=jnp.float32))
        return total, None

    potential, _ = lax.scan(far_step, potential, (far_u, far_v, far_rows, far_cols))
    return potential
```

```python
import jax
import jax.numpy as jnp
from jax import lax
from jax.experimental import pallas as pl
from jax.experimental.pallas import tpu as pltpu
from jax.sharding import PartitionSpec as P

F32 = jnp.float32
BF16 = jnp.bfloat16
SMEM = pl.BlockSpec(memory_space=pltpu.SMEM)
VMEM = pl.BlockSpec(memory_space=pltpu.VMEM)


def dot(a, b):
    return jnp.dot(a, b, preferred_element_type=F32)


def dot_t(a, b):
    return lax.dot_general(a, b, (((1,), (1,)), ((), ())), preferred_element_type=F32)


def params():
    return pltpu.CompilerParams(vmem_limit_bytes=48 * 1024 * 1024)


def each(count, step):
    if count <= 4:
        for i in range(count):
            step(i)
    else:
        lax.fori_loop(0, count, lambda i, c: (step(i), c)[1], 0)


def lane_ids(ids_ref, rank):
    count = ids_ref.shape[0]
    lane = lax.broadcasted_iota(jnp.int32, (1, count * rank), 1) // rank
    out = jnp.full((1, count * rank), -1, jnp.int32)
    for b in range(count):
        out = jnp.where(lane == b, ids_ref[b], out)
    return out


def mirror_kernel(clusters, exc, rank, others, at_ref, rows_ref, cols_ref, x_ref, u_ref, v_ref, send_ref, keep_ref, mask_ref):
    group = at_ref[0]
    place = at_ref[1]
    half = lax.rem(place, 2)
    width = keep_ref.shape[2]
    row_lane = lane_ids(rows_ref, rank)
    col_lane = lane_ids(cols_ref, rank)
    every = dot_t(x_ref[...], u_ref[...])
    coef = jnp.zeros((exc, every.shape[1]), F32)
    for c in range(clusters):
        coef += jnp.where(row_lane == group * clusters + c, every[c * exc : (c + 1) * exc], 0.0)
    coef = coef.astype(BF16).astype(F32)
    span = clusters * exc

    def one(i):
        other = group ^ (i + 1)
        for c in range(clusters):
            mask_ref[c * exc : (c + 1) * exc, :] = jnp.where(
                col_lane == other * clusters + c, coef, 0.0
            ).astype(BF16)
        rows = pl.ds(i * span if isinstance(i, int) else pl.multiple_of(i * span, span), span)
        for q in range(keep_ref.shape[0]):
            for side in range(2):
                at = (2 * q + side) * width
                part = dot(mask_ref[...], v_ref[:, at : at + width])

                @pl.when(half == side)
                def _():
                    keep_ref[q, rows, :] = part

                @pl.when(half != side)
                def _():
                    send_ref[q, rows, :] = part.astype(BF16)

    each(others, one)


def near_kernel(clusters, exc, at_ref, rows_ref, cols_ref, x_ref, n_ref, out_ref):
    first = at_ref[0] * clusters
    out_ref[...] = jnp.zeros_like(out_ref)
    for b in range(n_ref.shape[0]):
        row = rows_ref[b] - first
        col = cols_ref[b] - first
        weight = jnp.where(row == col, 0.5, 1.0).astype(F32)
        out_ref[row] += weight * dot_t(x_ref[col], n_ref[b])
        out_ref[col] += weight * dot(x_ref[row], n_ref[b])


def forward_kernel(clusters, exc, rank, others, at_ref, rows_ref, cols_ref, u_ref, v_ref, near_ref, *refs):
    pieces = refs[: 2 * others]
    own_ref = refs[2 * others]
    sends = refs[2 * others + 1 : -1]
    part_ref = refs[-1]
    group = at_ref[0]
    place = at_ref[1]
    half = lax.rem(place, 2)
    width = own_ref.shape[1]
    row_lane = lane_ids(rows_ref, rank)
    col_lane = lane_ids(cols_ref, rank)
    some = clusters // 2
    coef = jnp.zeros((exc, u_ref.shape[0]), F32)
    for i in range(others):
        other = group ^ (i + 1)
        for side in range(2):
            every = dot_t(pieces[2 * i + side][...], v_ref[...])
            first = other * clusters + jnp.where(half == side, 0, 1) * some
            for c in range(some):
                coef += jnp.where(col_lane == first + c, every[c * exc : (c + 1) * exc], 0.0)
    coef = coef.astype(BF16).astype(F32)
    masked = jnp.concatenate(
        [jnp.where(row_lane == group * clusters + c, coef, 0.0) for c in range(clusters)], axis=0
    ).astype(BF16)
    for q in range(len(sends) + 1):
        cols = slice(q * width, (q + 1) * width)
        part_ref[q] = dot(masked, u_ref[:, cols]) + near_ref[:, cols]
    own_ref[...] = part_ref[place]
    for m in range(1, len(sends) + 1):
        sends[m - 1][...] = part_ref[place ^ m].astype(BF16)


def swap(value, axis, size, step):
    return lax.ppermute(value, axis, [(i, i ^ step) for i in range(size)])


def body(charges, near_blocks, near_rows, near_cols, far_u, far_v, far_rows, far_cols):
    clusters, exc, panels = charges.shape
    entries, rank, _ = far_u.shape
    row_count = lax.axis_size("row")
    col_count = lax.axis_size("col")
    others = row_count - 1
    pairs = col_count // 2
    width = panels // col_count
    span = clusters * exc
    some = span // 2
    place = lax.axis_index("col")
    at = jnp.stack([lax.axis_index("row"), place])
    x = charges.reshape(span, panels)
    u = far_u.reshape(entries * rank, panels)
    v = far_v.reshape(entries * rank, panels)

    mine = lax.dynamic_slice_in_dim(x, lax.rem(place, 2) * some, some, 0)
    got = [swap(mine, "row", row_count, d) for d in range(1, row_count)]

    send, keep = pl.pallas_call(
        lambda *refs: mirror_kernel(clusters, exc, rank, others, *refs),
        in_specs=[SMEM, SMEM, SMEM, VMEM, VMEM, VMEM],
        out_specs=[VMEM, VMEM],
        out_shape=[
            jax.ShapeDtypeStruct((pairs, others * span, width), BF16),
            jax.ShapeDtypeStruct((pairs, others * span, width), F32),
        ],
        scratch_shapes=[pltpu.VMEM((span, entries * rank), BF16)],
        compiler_params=params(),
        name="mirror",
    )(at, far_rows, far_cols, x, u, v)
    from_core = swap(send, "col", col_count, 1)

    near = pl.pallas_call(
        lambda *refs: near_kernel(clusters, exc, *refs),
        in_specs=[SMEM, SMEM, SMEM, VMEM, VMEM],
        out_specs=VMEM,
        out_shape=jax.ShapeDtypeStruct((clusters, exc, panels), F32),
        compiler_params=params(),
        name="near",
    )(at, near_rows, near_cols, charges, near_blocks).reshape(span, panels)

    other_half = [swap(piece, "col", col_count, 1) for piece in got]

    pair_sum = keep + from_core.astype(F32)
    my_pair = place // 2

    def chunk(q):
        return lax.dynamic_index_in_dim(pair_sum, q, 0, keepdims=False)

    mirror = chunk(my_pair)
    for m in range(1, pairs):
        mirror = mirror + swap(chunk(my_pair ^ m).astype(BF16), "col", col_count, 2 * m).astype(F32)
    mirror = mirror.astype(BF16)
    from_rows = [
        swap(mirror[(d - 1) * span : d * span], "row", row_count, d) for d in range(1, row_count)
    ]

    pieces = []
    for a, b in zip(got, other_half):
        pieces += [a, b]
    own, *sends = pl.pallas_call(
        lambda *refs: forward_kernel(clusters, exc, rank, others, *refs),
        in_specs=[SMEM, SMEM, SMEM] + [VMEM] * (3 + 2 * others),
        out_specs=[VMEM] * col_count,
        out_shape=[jax.ShapeDtypeStruct((span, width), F32)]
        + [jax.ShapeDtypeStruct((span, width), BF16)] * (col_count - 1),
        scratch_shapes=[pltpu.VMEM((col_count, span, width), F32)],
        compiler_params=params(),
        name="forward",
    )(at, far_rows, far_cols, u, v, near, *pieces)
    total = own
    for m in range(1, col_count):
        total = total + swap(sends[m - 1], "col", col_count, m).astype(F32)
    for term in from_rows:
        total = total + term.astype(F32)
    return total.reshape(clusters, exc, width)


def solution(mesh):
    placed = (
        P(("parts", "row"), None, None),
        P(("parts", "row", "col"), None, None),
        P(("parts", "row", "col")),
        P(("parts", "row", "col")),
        P(("parts", "row", "col"), None, None),
        P(("parts", "row", "col"), None, None),
        P(("parts", "row", "col")),
        P(("parts", "row", "col")),
    )
    return jax.shard_map(
        body,
        mesh=mesh,
        in_specs=placed,
        out_specs=P(("parts", "row"), None, "col"),
        check_vma=False,
    )
```

```python
import jax
import jax.numpy as jnp
from jax import lax
from jax.experimental import pallas as pl
from jax.experimental.pallas import tpu as pltpu
from jax.sharding import PartitionSpec as P

F32 = jnp.float32
BF16 = jnp.bfloat16
SMEM = pl.BlockSpec(memory_space=pltpu.SMEM)
ANY = pl.BlockSpec(memory_space=pltpu.HBM)
VMEM = pl.BlockSpec(memory_space=pltpu.VMEM)


def dot(a, b):
    return jnp.dot(a, b, preferred_element_type=F32)


def dot_t(a, b):
    return lax.dot_general(a, b, (((1,), (1,)), ((), ())), preferred_element_type=F32)


def params():
    return pltpu.CompilerParams(vmem_limit_bytes=48 * 1024 * 1024)


def each(count, step):
    if count <= 4:
        for i in range(count):
            step(i)
    else:
        lax.fori_loop(0, count, lambda i, c: (step(i), c)[1], 0)


def lane_ids(ids_ref, rank):
    count = ids_ref.shape[0]
    lane = lax.broadcasted_iota(jnp.int32, (1, count * rank), 1) // rank
    out = jnp.full((1, count * rank), -1, jnp.int32)
    for b in range(count):
        out = jnp.where(lane == b, ids_ref[b], out)
    return out


def mirror_kernel(
    clusters, exc, rank, others, rows_hbm, cols_hbm, x_hbm, u_hbm, v_hbm, send_ref, keep_ref, lanes_ref,
    rows_ref, cols_ref, x_ref, u_ref, v_ref, mask_ref, sems,
):
    copies = [
        pltpu.make_async_copy(src, dst, sems.at[i])
        for i, (src, dst) in enumerate(
            [(rows_hbm, rows_ref), (cols_hbm, cols_ref), (x_hbm, x_ref), (u_hbm, u_ref), (v_hbm, v_ref)]
        )
    ]
    for copy in copies:
        copy.start()
    group = lax.axis_index("row")
    half = lax.rem(lax.axis_index("col"), 2)
    width = keep_ref.shape[2]
    copies[0].wait()
    copies[1].wait()
    row_lane = lane_ids(rows_ref, rank)
    col_lane = lane_ids(cols_ref, rank)
    lanes_ref[0:1, :] = row_lane
    lanes_ref[1:2, :] = col_lane
    copies[2].wait()
    copies[3].wait()
    every = dot_t(x_ref[...], u_ref[...])
    coef = jnp.zeros((exc, every.shape[1]), F32)
    for c in range(clusters):
        coef += jnp.where(row_lane == group * clusters + c, every[c * exc : (c + 1) * exc], 0.0)
    coef = coef.astype(BF16).astype(F32)
    span = clusters * exc
    copies[4].wait()

    def one(i):
        other = group ^ (i + 1)
        for c in range(clusters):
            mask_ref[c * exc : (c + 1) * exc, :] = jnp.where(
                col_lane == other * clusters + c, coef, 0.0
            ).astype(BF16)
        rows = pl.ds(i * span if isinstance(i, int) else pl.multiple_of(i * span, span), span)
        for q in range(keep_ref.shape[0]):
            for side in range(2):
                at = (2 * q + side) * width
                part = dot(mask_ref[...], v_ref[:, at : at + width])

                @pl.when(half == side)
                def _():
                    keep_ref[q, rows, :] = part

                @pl.when(half != side)
                def _():
                    send_ref[q, rows, :] = part.astype(BF16)

    each(others, one)


def near_kernel(clusters, exc, rows_ref, cols_ref, x_ref, n_ref, out_ref):
    first = lax.axis_index("row") * clusters
    out_ref[...] = jnp.zeros_like(out_ref)
    for b in range(n_ref.shape[0]):
        row = rows_ref[b] - first
        col = cols_ref[b] - first
        weight = jnp.where(row == col, 0.5, 1.0).astype(F32)
        out_ref[row] += weight * dot_t(x_ref[col], n_ref[b])
        out_ref[col] += weight * dot(x_ref[row], n_ref[b])


def forward_kernel(clusters, exc, others, lanes_ref, u_ref, v_ref, near_ref, *refs):
    count = 2 * others - 1
    pieces = refs[:count]
    own_ref = refs[count]
    sends = refs[count + 1 : -1]
    part_ref = refs[-1]
    group = lax.axis_index("row")
    place = lax.axis_index("col")
    half = lax.rem(place, 2)
    width = own_ref.shape[1]
    row_lane = lanes_ref[0:1, :]
    col_lane = lanes_ref[1:2, :]
    some = clusters // 2
    coef = jnp.zeros((exc, u_ref.shape[0]), F32)
    for n, piece in enumerate(pieces):
        every = dot_t(piece[...], v_ref[...])
        if n == 0:
            first = (group ^ 1) * clusters
        else:
            first = (group ^ (2 + (n - 1) // 2)) * clusters + (half if n % 2 == 1 else 1 - half) * some
        for c in range(piece.shape[0] // exc):
            coef += jnp.where(col_lane == first + c, every[c * exc : (c + 1) * exc], 0.0)
    coef = coef.astype(BF16).astype(F32)
    masked = jnp.concatenate(
        [jnp.where(row_lane == group * clusters + c, coef, 0.0) for c in range(clusters)], axis=0
    ).astype(BF16)
    for q in range(len(sends) + 1):
        cols = slice(q * width, (q + 1) * width)
        part_ref[q] = dot(masked, u_ref[:, cols]) + near_ref[:, cols]
    own_ref[...] = part_ref[place]
    for m in range(1, len(sends) + 1):
        sends[m - 1][...] = part_ref[place ^ m].astype(BF16)


def swap(value, axis, size, step):
    return lax.ppermute(value, axis, [(i, i ^ step) for i in range(size)])


def stage(work):
    shapes = jax.eval_shape(work)
    inside = lax.axis_index("row") < lax.axis_size("row")
    return lax.cond(inside, work, lambda: jax.tree.map(lambda a: jnp.zeros(a.shape, a.dtype), shapes))


def body(charges, near_blocks, near_rows, near_cols, far_u, far_v, far_rows, far_cols):
    clusters, exc, panels = charges.shape
    entries, rank, _ = far_u.shape
    row_count = lax.axis_size("row")
    col_count = lax.axis_size("col")
    others = row_count - 1
    pairs = col_count // 2
    width = panels // col_count
    span = clusters * exc
    some = span // 2
    place = lax.axis_index("col")
    x = charges.reshape(span, panels)
    u = far_u.reshape(entries * rank, panels)
    v = far_v.reshape(entries * rank, panels)

    whole = swap(x, "row", row_count, 1)
    mine = lax.dynamic_slice_in_dim(x, lax.rem(place, 2) * some, some, 0)
    got = [swap(mine, "row", row_count, d) for d in range(2, row_count)]

    def local():
        send, keep, lanes = pl.pallas_call(
            lambda *refs: mirror_kernel(clusters, exc, rank, others, *refs),
            in_specs=[ANY] * 5,
            out_specs=[VMEM] * 3,
            out_shape=[
                jax.ShapeDtypeStruct((pairs, others * span, width), BF16),
                jax.ShapeDtypeStruct((pairs, others * span, width), F32),
                jax.ShapeDtypeStruct((8, entries * rank), jnp.int32),
            ],
            scratch_shapes=[
                pltpu.SMEM(far_rows.shape, jnp.int32),
                pltpu.SMEM(far_cols.shape, jnp.int32),
                pltpu.VMEM(x.shape, BF16),
                pltpu.VMEM(u.shape, BF16),
                pltpu.VMEM(v.shape, BF16),
                pltpu.VMEM((span, entries * rank), BF16),
                pltpu.SemaphoreType.DMA((5,)),
            ],
            compiler_params=params(),
            name="mirror",
        )(far_rows, far_cols, x, u, v)
        from_core = swap(send, "col", col_count, 1)
        pair_sum = keep + from_core.astype(F32)

        def chunk(m):
            return lax.dynamic_index_in_dim(pair_sum, place // 2 ^ m, 0, keepdims=False)

        leaving = [chunk(m).astype(BF16) for m in range(1, pairs)]
        *leaving, x_near = lax.optimization_barrier((*leaving, charges))
        near = pl.pallas_call(
            lambda *refs: near_kernel(clusters, exc, *refs),
            in_specs=[SMEM, SMEM, VMEM, VMEM],
            out_specs=VMEM,
            out_shape=jax.ShapeDtypeStruct((clusters, exc, panels), F32),
            compiler_params=params(),
            name="near",
        )(near_rows, near_cols, x_near, near_blocks).reshape(span, panels)
        mirror = chunk(0)
        for m, part in enumerate(leaving):
            mirror = mirror + swap(part, "col", col_count, 2 * m + 2).astype(F32)
        mirror = mirror.astype(BF16)
        return [mirror[i * span : (i + 1) * span] for i in range(others)], near, lanes

    mirror, near, lanes = stage(local)
    whole, *got, lanes = lax.optimization_barrier((whole, *got, lanes))
    other_half = [swap(piece, "col", col_count, 1) for piece in got]
    from_rows = [swap(part, "row", row_count, i + 1) for i, part in enumerate(mirror)]

    pieces = [whole]
    for a, b in zip(got, other_half):
        pieces += [a, b]

    def forward():
        own, *sends = pl.pallas_call(
            lambda *refs: forward_kernel(clusters, exc, others, *refs),
            in_specs=[VMEM] * (4 + len(pieces)),
            out_specs=[VMEM] * col_count,
            out_shape=[jax.ShapeDtypeStruct((span, width), F32)]
            + [jax.ShapeDtypeStruct((span, width), BF16)] * (col_count - 1),
            scratch_shapes=[pltpu.VMEM((col_count, span, width), F32)],
            compiler_params=params(),
            name="forward",
        )(lanes, u, v, near, *pieces)
        for m in range(1, col_count):
            own = own + swap(sends[m - 1], "col", col_count, m).astype(F32)
        return own

    total = stage(forward)
    for term in from_rows:
        total = total + term.astype(F32)
    return total.reshape(clusters, exc, width)


def solution(mesh):
    placed = (
        P(("parts", "row"), None, None),
        P(("parts", "row", "col"), None, None),
        P(("parts", "row", "col")),
        P(("parts", "row", "col")),
        P(("parts", "row", "col"), None, None),
        P(("parts", "row", "col"), None, None),
        P(("parts", "row", "col")),
        P(("parts", "row", "col")),
    )
    return jax.shard_map(
        body,
        mesh=mesh,
        in_specs=placed,
        out_specs=P(("parts", "row"), None, "col"),
        check_vma=False,
    )
```

```python
import jax
import jax.numpy as jnp
from jax import lax
from jax.experimental import pallas as pl
from jax.experimental.pallas import tpu as pltpu
from jax.sharding import PartitionSpec as P

F32 = jnp.float32
BF16 = jnp.bfloat16
SMEM = pl.BlockSpec(memory_space=pltpu.SMEM)
ANY = pl.BlockSpec(memory_space=pltpu.HBM)
VMEM = pl.BlockSpec(memory_space=pltpu.VMEM)


def dot(a, b):
    return jnp.dot(a, b, preferred_element_type=F32)


def dot_t(a, b):
    return lax.dot_general(a, b, (((1,), (1,)), ((), ())), preferred_element_type=F32)


def params():
    return pltpu.CompilerParams(vmem_limit_bytes=48 * 1024 * 1024)


def each(count, step):
    if count <= 4:
        for i in range(count):
            step(i)
    else:
        lax.fori_loop(0, count, lambda i, c: (step(i), c)[1], 0)


def lane_ids(ids_ref, rank):
    count = ids_ref.shape[0]
    lane = lax.broadcasted_iota(jnp.int32, (1, count * rank), 1) // rank
    out = jnp.full((1, count * rank), -1, jnp.int32)
    for b in range(count):
        out = jnp.where(lane == b, ids_ref[b], out)
    return out


def split_columns(half, keep_ref, send_ref, rows, product):
    width = keep_ref.shape[2]
    for q in range(keep_ref.shape[0]):
        for side in range(2):
            at = (2 * q + side) * width
            part = product(slice(at, at + width))

            @pl.when(half == side)
            def _():
                keep_ref[q, rows, :] = part

            @pl.when(half != side)
            def _():
                send_ref[q, rows, :] = part.astype(BF16)


def mirror_kernel(
    clusters, exc, rank, others, rows_hbm, cols_hbm, x_hbm, u_hbm, v_hbm,
    send_ref, keep_ref, lanes_ref, u_ref, v_ref,
    rows_ref, cols_ref, x_ref, mask_ref, sems,
):
    copies = [
        pltpu.make_async_copy(src, dst, sems.at[i])
        for i, (src, dst) in enumerate(
            [(rows_hbm, rows_ref), (cols_hbm, cols_ref), (x_hbm, x_ref), (u_hbm, u_ref), (v_hbm, v_ref)]
        )
    ]
    for copy in copies:
        copy.start()
    group = lax.axis_index("row")
    half = lax.rem(lax.axis_index("col"), 2)
    copies[0].wait()
    copies[1].wait()
    row_lane = lane_ids(rows_ref, rank)
    col_lane = lane_ids(cols_ref, rank)
    lanes_ref[0:1, :] = row_lane
    lanes_ref[1:2, :] = col_lane
    copies[2].wait()
    copies[3].wait()
    every = dot_t(x_ref[...], u_ref[...])
    coef = jnp.zeros((exc, every.shape[1]), F32)
    for c in range(clusters):
        coef += jnp.where(row_lane == group * clusters + c, every[c * exc : (c + 1) * exc], 0.0)
    coef = coef.astype(BF16).astype(F32)
    span = clusters * exc
    copies[4].wait()
    batch = mask_ref.shape[0] // span

    def one(step):
        for i in range(batch):
            other = group ^ (step * batch + i + 1)
            for c in range(clusters):
                at = (i * clusters + c) * exc
                mask_ref[at : at + exc, :] = jnp.where(
                    col_lane == other * clusters + c, coef, 0.0
                ).astype(BF16)
        size = batch * span
        rows = pl.ds(step * size if isinstance(step, int) else pl.multiple_of(step * size, size), size)
        split_columns(half, keep_ref, send_ref, rows, lambda cols: dot(mask_ref[...], v_ref[:, cols]))

    each(others // batch, one)


def near_kernel(clusters, exc, rows_ref, cols_ref, x_ref, n_ref, out_ref):
    first = lax.axis_index("row") * clusters
    out_ref[...] = jnp.zeros_like(out_ref)
    for b in range(n_ref.shape[0]):
        row = rows_ref[b] - first
        col = cols_ref[b] - first
        weight = jnp.where(row == col, 0.5, 1.0).astype(F32)
        out_ref[row] += weight * dot_t(x_ref[col], n_ref[b])
        out_ref[col] += weight * dot(x_ref[row], n_ref[b])


def forward_kernel(clusters, exc, others, lanes_ref, u_ref, v_ref, near_ref, *refs):
    pieces = refs[:others]
    send_ref, keep_ref = refs[others:]
    group = lax.axis_index("row")
    half = lax.rem(lax.axis_index("col"), 2)
    row_lane = lanes_ref[0:1, :]
    col_lane = lanes_ref[1:2, :]
    coef = jnp.zeros((exc, u_ref.shape[0]), F32)
    batch = others if others <= 4 else 1
    for n in range(0, others, batch):
        every = dot_t(jnp.concatenate([p[...] for p in pieces[n : n + batch]], axis=0), v_ref[...])
        for i in range(batch):
            away = n + i + 1
            if away > 1:
                away = away + half if away % 2 == 0 else away - half
            first = (group ^ away) * clusters
            for c in range(clusters):
                at = (i * clusters + c) * exc
                coef += jnp.where(col_lane == first + c, every[at : at + exc], 0.0)
    coef = coef.astype(BF16).astype(F32)
    masked = jnp.concatenate(
        [jnp.where(row_lane == group * clusters + c, coef, 0.0) for c in range(clusters)], axis=0
    ).astype(BF16)
    rows = slice(None)
    split_columns(
        half, keep_ref, send_ref, rows, lambda cols: dot(masked, u_ref[:, cols]) + near_ref[:, cols]
    )


def swap(value, axis, size, step):
    return lax.ppermute(value, axis, [(i, i ^ step) for i in range(size)])


def stage(work):
    shapes = jax.eval_shape(work)
    inside = lax.axis_index("row") < lax.axis_size("row")
    return lax.cond(inside, work, lambda: jax.tree.map(lambda a: jnp.zeros(a.shape, a.dtype), shapes))


def body(charges, near_blocks, near_rows, near_cols, far_u, far_v, far_rows, far_cols):
    clusters, exc, panels = charges.shape
    entries, rank, _ = far_u.shape
    row_count = lax.axis_size("row")
    col_count = lax.axis_size("col")
    others = row_count - 1
    pairs = col_count // 2
    width = panels // col_count
    span = clusters * exc
    batch = others if others <= 4 else 1
    place = lax.axis_index("col")
    x = charges.reshape(span, panels)
    u = far_u.reshape(entries * rank, panels)
    v = far_v.reshape(entries * rank, panels)

    def shares(count):
        return [
            jax.ShapeDtypeStruct((pairs, count * span, width), BF16),
            jax.ShapeDtypeStruct((pairs, count * span, width), F32),
        ]

    def pair_sum(send, keep):
        total = keep + swap(send, "col", col_count, 1).astype(F32)

        def chunk(m):
            return lax.dynamic_index_in_dim(total, place // 2 ^ m, 0, keepdims=False)

        return chunk(0), [chunk(m).astype(BF16) for m in range(1, pairs)]

    def col_sum(total, leaving):
        for m, part in enumerate(leaving):
            total = total + swap(part, "col", col_count, 2 * m + 2).astype(F32)
        return total

    whole = swap(x, "row", row_count, 1)
    got = []
    for d in range(2, row_count, 2):
        perm = [
            (r * col_count + c, (r ^ (d + c % 2)) * col_count + c)
            for r in range(row_count)
            for c in range(col_count)
        ]
        got.append(lax.ppermute(x, ("row", "col"), perm))

    def local():
        send, keep, lanes, u_held, v_held = pl.pallas_call(
            lambda *refs: mirror_kernel(clusters, exc, rank, others, *refs),
            in_specs=[ANY] * 5,
            out_specs=[VMEM] * 5,
            out_shape=shares(others)
            + [
                jax.ShapeDtypeStruct((8, entries * rank), jnp.int32),
                jax.ShapeDtypeStruct(u.shape, BF16),
                jax.ShapeDtypeStruct(v.shape, BF16),
            ],
            scratch_shapes=[
                pltpu.SMEM(far_rows.shape, jnp.int32),
                pltpu.SMEM(far_cols.shape, jnp.int32),
                pltpu.VMEM(x.shape, BF16),
                pltpu.VMEM((batch * span, entries * rank), BF16),
                pltpu.SemaphoreType.DMA((5,)),
            ],
            compiler_params=params(),
            cost_estimate=pl.CostEstimate(flops=1024, bytes_accessed=1024, transcendentals=0),
            name="mirror",
        )(far_rows, far_cols, x, u, v)
        mirror, leaving = pair_sum(send, keep)
        *leaving, x_near = lax.optimization_barrier((*leaving, charges))
        near = pl.pallas_call(
            lambda *refs: near_kernel(clusters, exc, *refs),
            in_specs=[SMEM, SMEM, VMEM, VMEM],
            out_specs=VMEM,
            out_shape=jax.ShapeDtypeStruct((clusters, exc, panels), F32),
            compiler_params=params(),
            cost_estimate=pl.CostEstimate(flops=1024, bytes_accessed=1024, transcendentals=0),
            name="near",
        )(near_rows, near_cols, x_near, near_blocks).reshape(span, panels)
        mirror = col_sum(mirror, leaving).astype(BF16)
        return [mirror[i * span : (i + 1) * span] for i in range(others)], near, lanes, u_held, v_held

    mirror, near, lanes, u_held, v_held = stage(local)
    whole, *got, lanes = lax.optimization_barrier((whole, *got, lanes))
    pieces = [whole]
    for piece in got:
        pieces += [piece, swap(piece, "col", col_count, 1)]
    from_rows = [swap(part, "row", row_count, i + 1) for i, part in enumerate(mirror)]

    def forward():
        send, keep = pl.pallas_call(
            lambda *refs: forward_kernel(clusters, exc, others, *refs),
            in_specs=[VMEM] * (4 + others),
            out_specs=[VMEM] * 2,
            out_shape=shares(1),
            compiler_params=params(),
            cost_estimate=pl.CostEstimate(flops=1024, bytes_accessed=1024, transcendentals=0),
            name="forward",
        )(lanes, u_held, v_held, near, *pieces)
        return col_sum(*pair_sum(send, keep))

    total = stage(forward)
    for term in from_rows:
        total = total + term.astype(F32)
    return total.reshape(clusters, exc, width)


def solution(mesh):
    placed = (
        P(("parts", "row"), None, None),
        P(("parts", "row", "col"), None, None),
        P(("parts", "row", "col")),
        P(("parts", "row", "col")),
        P(("parts", "row", "col"), None, None),
        P(("parts", "row", "col"), None, None),
        P(("parts", "row", "col")),
        P(("parts", "row", "col")),
    )
    return jax.shard_map(
        body,
        mesh=mesh,
        in_specs=placed,
        out_specs=P(("parts", "row"), None, "col"),
        check_vma=False,
    )
```

```python
import jax
import jax.numpy as jnp
from jax import lax
from jax.experimental import pallas as pl
from jax.experimental.pallas import tpu as pltpu
from jax.sharding import PartitionSpec as P

F32 = jnp.float32
BF16 = jnp.bfloat16
SMEM = pl.BlockSpec(memory_space=pltpu.SMEM)
ANY = pl.BlockSpec(memory_space=pltpu.HBM)
VMEM = pl.BlockSpec(memory_space=pltpu.VMEM)


def dot(a, b):
    return jnp.dot(a, b, preferred_element_type=F32)


def dot_t(a, b):
    return lax.dot_general(a, b, (((1,), (1,)), ((), ())), preferred_element_type=F32)


def params(others):
    return pltpu.CompilerParams(vmem_limit_bytes=(12 if others <= 4 else 48) * 1024 * 1024)


def each(count, step):
    if count <= 4:
        for i in range(count):
            step(i)
    else:
        lax.fori_loop(0, count, lambda i, c: (step(i), c)[1], 0)


def lane_ids(ids_ref, rank):
    count = ids_ref.shape[0]
    lane = lax.broadcasted_iota(jnp.int32, (1, count * rank), 1) // rank
    out = jnp.full((1, count * rank), -1, jnp.int32)
    for b in range(count):
        out = jnp.where(lane == b, ids_ref[b], out)
    return out


def split_columns(half, keep_ref, send_ref, rows, product):
    width = keep_ref.shape[2]
    for q in range(keep_ref.shape[0]):
        for side in range(2):
            at = (2 * q + side) * width
            part = product(slice(at, at + width))

            @pl.when(half == side)
            def _():
                keep_ref[q, rows, :] = part

            @pl.when(half != side)
            def _():
                send_ref[q, rows, :] = part.astype(BF16)


def mirror_kernel(
    clusters, exc, rank, others, rows_hbm, cols_hbm, x_hbm, u_hbm, v_hbm,
    send_ref, keep_ref, lanes_ref, u_ref, v_ref,
    rows_ref, cols_ref, x_ref, mask_ref, sems,
):
    copies = [
        pltpu.make_async_copy(src, dst, sems.at[i])
        for i, (src, dst) in enumerate(
            [(rows_hbm, rows_ref), (cols_hbm, cols_ref), (x_hbm, x_ref), (u_hbm, u_ref), (v_hbm, v_ref)]
        )
    ]
    for copy in copies:
        copy.start()
    group = lax.axis_index("row")
    half = lax.rem(lax.axis_index("col"), 2)
    copies[0].wait()
    copies[1].wait()
    row_lane = lane_ids(rows_ref, rank)
    col_lane = lane_ids(cols_ref, rank)
    lanes_ref[0:1, :] = row_lane
    lanes_ref[1:2, :] = col_lane
    copies[2].wait()
    copies[3].wait()
    every = dot_t(x_ref[...], u_ref[...])
    coef = jnp.zeros((exc, every.shape[1]), F32)
    for c in range(clusters):
        coef += jnp.where(row_lane == group * clusters + c, every[c * exc : (c + 1) * exc], 0.0)
    coef = coef.astype(BF16).astype(F32)
    span = clusters * exc
    copies[4].wait()
    batch = mask_ref.shape[0] // span

    def one(step):
        for i in range(batch):
            other = group ^ (step * batch + i + 1)
            for c in range(clusters):
                at = (i * clusters + c) * exc
                mask_ref[at : at + exc, :] = jnp.where(
                    col_lane == other * clusters + c, coef, 0.0
                ).astype(BF16)
        size = batch * span
        rows = pl.ds(step * size if isinstance(step, int) else pl.multiple_of(step * size, size), size)
        split_columns(half, keep_ref, send_ref, rows, lambda cols: dot(mask_ref[...], v_ref[:, cols]))

    each(others // batch, one)


def near_kernel(clusters, exc, rows_ref, cols_ref, x_ref, n_ref, out_ref):
    first = lax.axis_index("row") * clusters
    out_ref[...] = jnp.zeros_like(out_ref)
    for b in range(n_ref.shape[0]):
        row = rows_ref[b] - first
        col = cols_ref[b] - first
        weight = jnp.where(row == col, 0.5, 1.0).astype(F32)
        out_ref[row] += weight * dot_t(x_ref[col], n_ref[b])
        out_ref[col] += weight * dot(x_ref[row], n_ref[b])


def coef_of(clusters, exc, aways, lanes_ref, v_ref, pieces):
    group = lax.axis_index("row")
    col_lane = lanes_ref[1:2, :]
    coef = jnp.zeros((exc, v_ref.shape[0]), F32)
    batch = len(pieces) if len(pieces) <= 4 else 1
    for n in range(0, len(pieces), batch):
        every = dot_t(jnp.concatenate([p[...] for p in pieces[n : n + batch]], axis=0), v_ref[...])
        for i in range(batch):
            first = (group ^ aways[n + i]) * clusters
            for c in range(clusters):
                at = (i * clusters + c) * exc
                coef += jnp.where(col_lane == first + c, every[at : at + exc], 0.0)
    return coef


def early_kernel(clusters, exc, lanes_ref, v_ref, *refs):
    half = lax.rem(lax.axis_index("col"), 2)
    pieces = refs[:-1]
    aways = [1] + [2 * t + half for t in range(1, len(pieces))]
    refs[-1][...] = coef_of(clusters, exc, aways, lanes_ref, v_ref, pieces)


def forward_kernel(clusters, exc, lanes_ref, u_ref, v_ref, near_ref, early_ref, *refs):
    pieces = refs[:-2]
    send_ref, keep_ref = refs[-2:]
    group = lax.axis_index("row")
    half = lax.rem(lax.axis_index("col"), 2)
    aways = [2 * t + 3 - half for t in range(len(pieces))]
    coef = early_ref[...] + coef_of(clusters, exc, aways, lanes_ref, v_ref, pieces)
    coef = coef.astype(BF16).astype(F32)
    row_lane = lanes_ref[0:1, :]
    masked = jnp.concatenate(
        [jnp.where(row_lane == group * clusters + c, coef, 0.0) for c in range(clusters)], axis=0
    ).astype(BF16)
    rows = slice(None)
    split_columns(
        half, keep_ref, send_ref, rows, lambda cols: dot(masked, u_ref[:, cols]) + near_ref[:, cols]
    )


def swap(value, axis, size, step):
    return lax.ppermute(value, axis, [(i, i ^ step) for i in range(size)])


def stage(work):
    shapes = jax.eval_shape(work)
    inside = lax.axis_index("row") < lax.axis_size("row")
    return lax.cond(inside, work, lambda: jax.tree.map(lambda a: jnp.zeros(a.shape, a.dtype), shapes))


def body(charges, near_blocks, near_rows, near_cols, far_u, far_v, far_rows, far_cols):
    clusters, exc, panels = charges.shape
    entries, rank, _ = far_u.shape
    row_count = lax.axis_size("row")
    col_count = lax.axis_size("col")
    others = row_count - 1
    pairs = col_count // 2
    width = panels // col_count
    span = clusters * exc
    batch = others if others <= 4 else 1
    place = lax.axis_index("col")
    x = charges.reshape(span, panels)
    u = far_u.reshape(entries * rank, panels)
    v = far_v.reshape(entries * rank, panels)

    def shares(count):
        return [
            jax.ShapeDtypeStruct((pairs, count * span, width), BF16),
            jax.ShapeDtypeStruct((pairs, count * span, width), F32),
        ]

    def pair_sum(send, keep):
        total = keep + swap(send, "col", col_count, 1).astype(F32)

        def chunk(m):
            return lax.dynamic_index_in_dim(total, place // 2 ^ m, 0, keepdims=False)

        return chunk(0), [chunk(m).astype(BF16) for m in range(1, pairs)]

    def col_sum(total, leaving):
        for m, part in enumerate(leaving):
            total = total + swap(part, "col", col_count, 2 * m + 2).astype(F32)
        return total

    whole = swap(x, "row", row_count, 1)
    got = []
    for d in range(2, row_count, 2):
        perm = [
            (r * col_count + c, (r ^ (d + c % 2)) * col_count + c)
            for r in range(row_count)
            for c in range(col_count)
        ]
        got.append(lax.ppermute(x, ("row", "col"), perm))

    def local():
        send, keep, lanes, u_held, v_held = pl.pallas_call(
            lambda *refs: mirror_kernel(clusters, exc, rank, others, *refs),
            in_specs=[ANY] * 5,
            out_specs=[VMEM] * 5,
            out_shape=shares(others)
            + [
                jax.ShapeDtypeStruct((8, entries * rank), jnp.int32),
                jax.ShapeDtypeStruct(u.shape, BF16),
                jax.ShapeDtypeStruct(v.shape, BF16),
            ],
            scratch_shapes=[
                pltpu.SMEM(far_rows.shape, jnp.int32),
                pltpu.SMEM(far_cols.shape, jnp.int32),
                pltpu.VMEM(x.shape, BF16),
                pltpu.VMEM((batch * span, entries * rank), BF16),
                pltpu.SemaphoreType.DMA((5,)),
            ],
            compiler_params=params(others),
            cost_estimate=pl.CostEstimate(flops=1024, bytes_accessed=1024, transcendentals=0),
            name="mirror",
        )(far_rows, far_cols, x, u, v)
        mirror, leaving = pair_sum(send, keep)
        *leaving, x_near = lax.optimization_barrier((*leaving, charges))
        near = pl.pallas_call(
            lambda *refs: near_kernel(clusters, exc, *refs),
            in_specs=[SMEM, SMEM, VMEM, VMEM],
            out_specs=VMEM,
            out_shape=jax.ShapeDtypeStruct((clusters, exc, panels), F32),
            compiler_params=params(others),
            cost_estimate=pl.CostEstimate(flops=1024, bytes_accessed=1024, transcendentals=0),
            name="near",
        )(near_rows, near_cols, x_near, near_blocks).reshape(span, panels)
        mirror = col_sum(mirror, leaving).astype(BF16)
        return [mirror[i * span : (i + 1) * span] for i in range(others)], near, lanes, u_held, v_held

    mirror, near, lanes, u_held, v_held = stage(local)
    whole, *got, lanes = lax.optimization_barrier((whole, *got, lanes))
    from_rows = [swap(part, "row", row_count, i + 1) for i, part in enumerate(mirror)]

    def forward():
        early = pl.pallas_call(
            lambda *refs: early_kernel(clusters, exc, *refs),
            in_specs=[VMEM] * (3 + len(got)),
            out_specs=VMEM,
            out_shape=jax.ShapeDtypeStruct((exc, entries * rank), F32),
            compiler_params=params(others),
            cost_estimate=pl.CostEstimate(flops=1024, bytes_accessed=1024, transcendentals=0),
            name="early",
        )(lanes, v_held, whole, *got)
        send, keep = pl.pallas_call(
            lambda *refs: forward_kernel(clusters, exc, *refs),
            in_specs=[VMEM] * (5 + len(got)),
            out_specs=[VMEM] * 2,
            out_shape=shares(1),
            compiler_params=params(others),
            cost_estimate=pl.CostEstimate(flops=1024, bytes_accessed=1024, transcendentals=0),
            name="forward",
        )(lanes, u_held, v_held, near, early, *[swap(piece, "col", col_count, 1) for piece in got])
        return col_sum(*pair_sum(send, keep))

    total = stage(forward)
    for term in from_rows:
        total = total + term.astype(F32)
    return total.reshape(clusters, exc, width)


def solution(mesh):
    placed = (
        P(("parts", "row"), None, None),
        P(("parts", "row", "col"), None, None),
        P(("parts", "row", "col")),
        P(("parts", "row", "col")),
        P(("parts", "row", "col"), None, None),
        P(("parts", "row", "col"), None, None),
        P(("parts", "row", "col")),
        P(("parts", "row", "col")),
    )
    return jax.shard_map(
        body,
        mesh=mesh,
        in_specs=placed,
        out_specs=P(("parts", "row"), None, "col"),
        check_vma=False,
    )
```

```python
import jax
import jax.numpy as jnp
from jax import lax
from jax.experimental import pallas as pl
from jax.experimental.pallas import tpu as pltpu
from jax.sharding import PartitionSpec as P

F32 = jnp.float32
BF16 = jnp.bfloat16
SMEM = pl.BlockSpec(memory_space=pltpu.SMEM)
ANY = pl.BlockSpec(memory_space=pltpu.HBM)
VMEM = pl.BlockSpec(memory_space=pltpu.VMEM)


def dot(a, b):
    return jnp.dot(a, b, preferred_element_type=F32)


def dot_t(a, b):
    return lax.dot_general(a, b, (((1,), (1,)), ((), ())), preferred_element_type=F32)


def params(others):
    return pltpu.CompilerParams(vmem_limit_bytes=(12 if others <= 4 else 48) * 1024 * 1024)


def each(count, step):
    if count <= 4:
        for i in range(count):
            step(i)
    else:
        lax.fori_loop(0, count, lambda i, c: (step(i), c)[1], 0)


def lane_ids(ids_ref, rank):
    count = ids_ref.shape[0]
    lane = lax.broadcasted_iota(jnp.int32, (1, count * rank), 1) // rank
    out = jnp.full((1, count * rank), -1, jnp.int32)
    for b in range(count):
        out = jnp.where(lane == b, ids_ref[b], out)
    return out


def split_columns(half, keep_ref, send_ref, rows, product):
    width = keep_ref.shape[2]
    for q in range(keep_ref.shape[0]):
        for side in range(2):
            at = (2 * q + side) * width
            part = product(slice(at, at + width))

            @pl.when(half == side)
            def _():
                keep_ref[q, rows, :] = part

            @pl.when(half != side)
            def _():
                send_ref[q, rows, :] = part.astype(BF16)


def mirror_kernel(
    clusters, exc, rank, others, rows_hbm, cols_hbm, x_hbm, u_hbm, v_hbm,
    send_ref, keep_ref, lanes_ref,
    rows_ref, cols_ref, x_ref, u_ref, v_ref, mask_ref, sems,
):
    copies = [
        pltpu.make_async_copy(src, dst, sems.at[i])
        for i, (src, dst) in enumerate(
            [(rows_hbm, rows_ref), (cols_hbm, cols_ref), (x_hbm, x_ref), (u_hbm, u_ref), (v_hbm, v_ref)]
        )
    ]
    for copy in copies:
        copy.start()
    group = lax.axis_index("row")
    half = lax.rem(lax.axis_index("col"), 2)
    copies[0].wait()
    copies[1].wait()
    row_lane = lane_ids(rows_ref, rank)
    col_lane = lane_ids(cols_ref, rank)
    lanes_ref[0:1, :] = row_lane
    lanes_ref[1:2, :] = col_lane
    copies[2].wait()
    copies[3].wait()
    every = dot_t(x_ref[...], u_ref[...])
    coef = jnp.zeros((exc, every.shape[1]), F32)
    for c in range(clusters):
        coef += jnp.where(row_lane == group * clusters + c, every[c * exc : (c + 1) * exc], 0.0)
    coef = coef.astype(BF16).astype(F32)
    span = clusters * exc
    copies[4].wait()
    batch = mask_ref.shape[0] // span

    def one(step):
        for i in range(batch):
            other = group ^ (step * batch + i + 1)
            for c in range(clusters):
                at = (i * clusters + c) * exc
                mask_ref[at : at + exc, :] = jnp.where(
                    col_lane == other * clusters + c, coef, 0.0
                ).astype(BF16)
        size = batch * span
        rows = pl.ds(step * size if isinstance(step, int) else pl.multiple_of(step * size, size), size)
        split_columns(half, keep_ref, send_ref, rows, lambda cols: dot(mask_ref[...], v_ref[:, cols]))

    each(others // batch, one)


def near_kernel(clusters, exc, rows_ref, cols_ref, x_ref, n_ref, out_ref):
    first = lax.axis_index("row") * clusters
    out_ref[...] = jnp.zeros_like(out_ref)
    for b in range(n_ref.shape[0]):
        row = rows_ref[b] - first
        col = cols_ref[b] - first
        weight = jnp.where(row == col, 0.5, 1.0).astype(F32)
        out_ref[row] += weight * dot_t(x_ref[col], n_ref[b])
        out_ref[col] += weight * dot(x_ref[row], n_ref[b])


def forward_kernel(clusters, exc, others, lanes_ref, u_hbm, v_hbm, near_hbm, *refs):
    sources = refs[:others]
    send_ref, keep_ref, u_ref, v_ref, near_ref, pieces_ref, sems = refs[others:]
    span = clusters * exc
    moves = [(v_hbm, v_ref)]
    moves += [(piece, pieces_ref.at[i * span : (i + 1) * span]) for i, piece in enumerate(sources)]
    moves += [(u_hbm, u_ref), (near_hbm, near_ref)]
    copies = [pltpu.make_async_copy(src, dst, sems.at[i]) for i, (src, dst) in enumerate(moves)]
    for copy in copies:
        copy.start()
    group = lax.axis_index("row")
    half = lax.rem(lax.axis_index("col"), 2)
    row_lane = lanes_ref[0:1, :]
    col_lane = lanes_ref[1:2, :]
    coef = jnp.zeros((exc, u_ref.shape[0]), F32)
    batch = others if others <= 4 else 1
    for copy in copies[:-2]:
        copy.wait()
    for n in range(0, others, batch):
        every = dot_t(pieces_ref[n * span : (n + batch) * span], v_ref[...])
        for i in range(batch):
            away = n + i + 1
            if away > 1:
                away = away + half if away % 2 == 0 else away - half
            first = (group ^ away) * clusters
            for c in range(clusters):
                at = (i * clusters + c) * exc
                coef += jnp.where(col_lane == first + c, every[at : at + exc], 0.0)
    coef = coef.astype(BF16).astype(F32)
    masked = jnp.concatenate(
        [jnp.where(row_lane == group * clusters + c, coef, 0.0) for c in range(clusters)], axis=0
    ).astype(BF16)
    copies[-2].wait()
    copies[-1].wait()
    rows = slice(None)
    split_columns(
        half, keep_ref, send_ref, rows, lambda cols: dot(masked, u_ref[:, cols]) + near_ref[:, cols]
    )


def swap(value, axis, size, step):
    return lax.ppermute(value, axis, [(i, i ^ step) for i in range(size)])


def stage(work):
    shapes = jax.eval_shape(work)
    inside = lax.axis_index("row") < lax.axis_size("row")
    return lax.cond(inside, work, lambda: jax.tree.map(lambda a: jnp.zeros(a.shape, a.dtype), shapes))


def body(charges, near_blocks, near_rows, near_cols, far_u, far_v, far_rows, far_cols):
    clusters, exc, panels = charges.shape
    entries, rank, _ = far_u.shape
    row_count = lax.axis_size("row")
    col_count = lax.axis_size("col")
    others = row_count - 1
    pairs = col_count // 2
    width = panels // col_count
    span = clusters * exc
    batch = others if others <= 4 else 1
    place = lax.axis_index("col")
    x = charges.reshape(span, panels)
    u = far_u.reshape(entries * rank, panels)
    v = far_v.reshape(entries * rank, panels)

    def shares(count):
        return [
            jax.ShapeDtypeStruct((pairs, count * span, width), BF16),
            jax.ShapeDtypeStruct((pairs, count * span, width), F32),
        ]

    def pair_sum(send, keep):
        total = keep + swap(send, "col", col_count, 1).astype(F32)

        def chunk(m):
            return lax.dynamic_index_in_dim(total, place // 2 ^ m, 0, keepdims=False)

        return chunk(0), [chunk(m).astype(BF16) for m in range(1, pairs)]

    def col_sum(total, leaving):
        for m, part in enumerate(leaving):
            total = total + swap(part, "col", col_count, 2 * m + 2).astype(F32)
        return total

    whole = swap(x, "row", row_count, 1)
    got = []
    for d in range(2, row_count, 2):
        perm = [
            (r * col_count + c, (r ^ (d + c % 2)) * col_count + c)
            for r in range(row_count)
            for c in range(col_count)
        ]
        got.append(lax.ppermute(x, ("row", "col"), perm))

    def local():
        send, keep, lanes = pl.pallas_call(
            lambda *refs: mirror_kernel(clusters, exc, rank, others, *refs),
            in_specs=[ANY] * 5,
            out_specs=[VMEM] * 3,
            out_shape=shares(others) + [jax.ShapeDtypeStruct((8, entries * rank), jnp.int32)],
            scratch_shapes=[
                pltpu.SMEM(far_rows.shape, jnp.int32),
                pltpu.SMEM(far_cols.shape, jnp.int32),
                pltpu.VMEM(x.shape, BF16),
                pltpu.VMEM(u.shape, BF16),
                pltpu.VMEM(v.shape, BF16),
                pltpu.VMEM((batch * span, entries * rank), BF16),
                pltpu.SemaphoreType.DMA((5,)),
            ],
            compiler_params=params(others),
            cost_estimate=pl.CostEstimate(flops=1024, bytes_accessed=1024, transcendentals=0),
            name="mirror",
        )(far_rows, far_cols, x, u, v)
        mirror, leaving = pair_sum(send, keep)
        *leaving, x_near = lax.optimization_barrier((*leaving, charges))
        near = pl.pallas_call(
            lambda *refs: near_kernel(clusters, exc, *refs),
            in_specs=[SMEM, SMEM, VMEM, VMEM],
            out_specs=VMEM,
            out_shape=jax.ShapeDtypeStruct((clusters, exc, panels), F32),
            compiler_params=params(others),
            cost_estimate=pl.CostEstimate(flops=1024, bytes_accessed=1024, transcendentals=0),
            name="near",
        )(near_rows, near_cols, x_near, near_blocks).reshape(span, panels)
        mirror = col_sum(mirror, leaving).astype(BF16)
        return [mirror[i * span : (i + 1) * span] for i in range(others)], near, lanes

    mirror, near, lanes = stage(local)
    whole, *got, lanes = lax.optimization_barrier((whole, *got, lanes))
    pieces = [whole]
    for piece in got:
        pieces += [piece, swap(piece, "col", col_count, 1)]
    from_rows = [swap(mirror[d - 1], "row", row_count, d) for d in range(2, row_count)]

    def forward():
        send, keep = pl.pallas_call(
            lambda *refs: forward_kernel(clusters, exc, others, *refs),
            in_specs=[VMEM] + [ANY] * (3 + others),
            out_specs=[VMEM] * 2,
            out_shape=shares(1),
            scratch_shapes=[
                pltpu.VMEM(u.shape, BF16),
                pltpu.VMEM(v.shape, BF16),
                pltpu.VMEM(near.shape, F32),
                pltpu.VMEM((others * span, panels), BF16),
                pltpu.SemaphoreType.DMA((3 + others,)),
            ],
            compiler_params=params(others),
            cost_estimate=pl.CostEstimate(flops=1024, bytes_accessed=1024, transcendentals=0),
            name="forward",
        )(lanes, u, v, near, *pieces)
        own, leaving = pair_sum(send, keep)
        return col_sum(own, leaving) + swap(mirror[0], "row", row_count, 1).astype(F32)

    total = stage(forward)
    for term in from_rows:
        total = total + term.astype(F32)
    return total.reshape(clusters, exc, width)


def solution(mesh):
    placed = (
        P(("parts", "row"), None, None),
        P(("parts", "row", "col"), None, None),
        P(("parts", "row", "col")),
        P(("parts", "row", "col")),
        P(("parts", "row", "col"), None, None),
        P(("parts", "row", "col"), None, None),
        P(("parts", "row", "col")),
        P(("parts", "row", "col")),
    )
    return jax.shard_map(
        body,
        mesh=mesh,
        in_specs=placed,
        out_specs=P(("parts", "row"), None, "col"),
        check_vma=False,
    )
```

```python
import jax
import jax.numpy as jnp
from jax import lax
from jax.experimental import pallas as pl
from jax.experimental.pallas import tpu as pltpu
from jax.sharding import PartitionSpec as P

F32 = jnp.float32
BF16 = jnp.bfloat16
SMEM = pl.BlockSpec(memory_space=pltpu.SMEM)
ANY = pl.BlockSpec(memory_space=pltpu.HBM)
VMEM = pl.BlockSpec(memory_space=pltpu.VMEM)


def dot(a, b):
    return jnp.dot(a, b, preferred_element_type=F32)


def dot_t(a, b):
    return lax.dot_general(a, b, (((1,), (1,)), ((), ())), preferred_element_type=F32)


def params(others):
    return pltpu.CompilerParams(vmem_limit_bytes=(12 if others <= 4 else 48) * 1024 * 1024)


def each(count, step):
    if count <= 4:
        for i in range(count):
            step(i)
    else:
        lax.fori_loop(0, count, lambda i, c: (step(i), c)[1], 0)


def lane_ids(ids_ref, rank):
    count = ids_ref.shape[0]
    lane = lax.broadcasted_iota(jnp.int32, (1, count * rank), 1) // rank
    out = jnp.full((1, count * rank), -1, jnp.int32)
    for b in range(count):
        out = jnp.where(lane == b, ids_ref[b], out)
    return out


def split_columns(half, keep_ref, send_ref, rows, product):
    width = keep_ref.shape[2]
    for q in range(keep_ref.shape[0]):
        for side in range(2):
            at = (2 * q + side) * width
            part = product(slice(at, at + width))

            @pl.when(half == side)
            def _():
                keep_ref[q, rows, :] = part

            @pl.when(half != side)
            def _():
                send_ref[q, rows, :] = part.astype(BF16)


def mirror_kernel(
    clusters, exc, rank, others, rows_hbm, cols_hbm, x_hbm, u_hbm, v_hbm,
    send_ref, keep_ref, lanes_ref,
    rows_ref, cols_ref, x_ref, u_ref, v_ref, mask_ref, sems,
):
    copies = [
        pltpu.make_async_copy(src, dst, sems.at[i])
        for i, (src, dst) in enumerate(
            [(rows_hbm, rows_ref), (cols_hbm, cols_ref), (x_hbm, x_ref), (u_hbm, u_ref), (v_hbm, v_ref)]
        )
    ]
    for copy in copies:
        copy.start()
    group = lax.axis_index("row")
    half = lax.rem(lax.axis_index("col"), 2)
    copies[0].wait()
    copies[1].wait()
    row_lane = lane_ids(rows_ref, rank)
    col_lane = lane_ids(cols_ref, rank)
    lanes_ref[0:1, :] = row_lane
    lanes_ref[1:2, :] = col_lane
    copies[2].wait()
    copies[3].wait()
    every = dot_t(x_ref[...], u_ref[...])
    coef = jnp.zeros((exc, every.shape[1]), F32)
    for c in range(clusters):
        coef += jnp.where(row_lane == group * clusters + c, every[c * exc : (c + 1) * exc], 0.0)
    coef = coef.astype(BF16).astype(F32)
    span = clusters * exc
    copies[4].wait()
    batch = mask_ref.shape[0] // span

    def one(step):
        for i in range(batch):
            other = group ^ (step * batch + i + 1)
            for c in range(clusters):
                at = (i * clusters + c) * exc
                mask_ref[at : at + exc, :] = jnp.where(
                    col_lane == other * clusters + c, coef, 0.0
                ).astype(BF16)
        size = batch * span
        rows = pl.ds(step * size if isinstance(step, int) else pl.multiple_of(step * size, size), size)
        split_columns(half, keep_ref, send_ref, rows, lambda cols: dot(mask_ref[...], v_ref[:, cols]))

    each(others // batch, one)


def near_kernel(clusters, exc, rows_ref, cols_ref, x_ref, n_ref, out_ref):
    first = lax.axis_index("row") * clusters
    out_ref[...] = jnp.zeros_like(out_ref)
    for b in range(n_ref.shape[0]):
        row = rows_ref[b] - first
        col = cols_ref[b] - first
        weight = jnp.where(row == col, 0.5, 1.0).astype(F32)
        out_ref[row] += weight * dot_t(x_ref[col], n_ref[b])
        out_ref[col] += weight * dot(x_ref[row], n_ref[b])


def coef_of(clusters, exc, aways, lanes_ref, v_ref, pieces):
    group = lax.axis_index("row")
    col_lane = lanes_ref[1:2, :]
    coef = jnp.zeros((exc, v_ref.shape[0]), F32)
    batch = len(pieces) if len(pieces) <= 4 else 1
    for n in range(0, len(pieces), batch):
        every = dot_t(jnp.concatenate(pieces[n : n + batch], axis=0), v_ref[...])
        for i in range(batch):
            first = (group ^ aways[n + i]) * clusters
            for c in range(clusters):
                at = (i * clusters + c) * exc
                coef += jnp.where(col_lane == first + c, every[at : at + exc], 0.0)
    return coef


def early_kernel(clusters, exc, count, lanes_ref, *refs):
    sources, (coef_ref, *targets) = refs[: 4 + count], refs[4 + count : 9 + count]
    got_ref, sems = refs[9 + count :]
    span = clusters * exc
    moves = [(sources[0], targets[0])]
    moves += [(src, got_ref.at[i * span : (i + 1) * span]) for i, src in enumerate(sources[4:])]
    moves += list(zip(sources[1:4], targets[1:]))
    copies = [pltpu.make_async_copy(src, dst, sems.at[i]) for i, (src, dst) in enumerate(moves)]
    for copy in copies:
        copy.start()
    half = lax.rem(lax.axis_index("col"), 2)
    for copy in copies[: 1 + count]:
        copy.wait()
    pieces = [got_ref[i * span : (i + 1) * span] for i in range(count)]
    aways = [2 * t + half for t in range(1, count + 1)]
    coef_ref[...] = coef_of(clusters, exc, aways, lanes_ref, targets[0], pieces)
    for copy in copies[1 + count :]:
        copy.wait()


def forward_kernel(clusters, exc, lanes_ref, early_ref, v_ref, u_ref, near_ref, whole_ref, handed_ref, *refs):
    send_ref, keep_ref = refs[-2:]
    group = lax.axis_index("row")
    half = lax.rem(lax.axis_index("col"), 2)
    pieces = [jnp.where(half == 0, whole_ref[...], handed_ref[...])] + [ref[...] for ref in refs[:-2]]
    aways = [1] + [2 * t + 1 - half for t in range(1, len(pieces))]
    coef = early_ref[...] + coef_of(clusters, exc, aways, lanes_ref, v_ref, pieces)
    coef = coef.astype(BF16).astype(F32)
    row_lane = lanes_ref[0:1, :]
    masked = jnp.concatenate(
        [jnp.where(row_lane == group * clusters + c, coef, 0.0) for c in range(clusters)], axis=0
    ).astype(BF16)
    rows = slice(None)
    split_columns(
        half, keep_ref, send_ref, rows, lambda cols: dot(masked, u_ref[:, cols]) + near_ref[:, cols]
    )


def swap(value, axis, size, step):
    return lax.ppermute(value, axis, [(i, i ^ step) for i in range(size)])


def stage(work):
    shapes = jax.eval_shape(work)
    inside = lax.axis_index("row") < lax.axis_size("row")
    return lax.cond(inside, work, lambda: jax.tree.map(lambda a: jnp.zeros(a.shape, a.dtype), shapes))


def body(charges, near_blocks, near_rows, near_cols, far_u, far_v, far_rows, far_cols):
    clusters, exc, panels = charges.shape
    entries, rank, _ = far_u.shape
    row_count = lax.axis_size("row")
    col_count = lax.axis_size("col")
    others = row_count - 1
    pairs = col_count // 2
    width = panels // col_count
    span = clusters * exc
    batch = others if others <= 4 else 1
    place = lax.axis_index("col")
    x = charges.reshape(span, panels)
    u = far_u.reshape(entries * rank, panels)
    v = far_v.reshape(entries * rank, panels)

    def shares(count):
        return [
            jax.ShapeDtypeStruct((pairs, count * span, width), BF16),
            jax.ShapeDtypeStruct((pairs, count * span, width), F32),
        ]

    def pair_sum(send, keep):
        return keep + swap(send, "col", col_count, 1).astype(F32)

    def col_sum(total, between=lambda leaving: leaving):
        def chunk(m):
            return lax.dynamic_index_in_dim(total, place // 2 ^ m, 0, keepdims=False)

        leaving = between([chunk(m).astype(BF16) for m in range(1, pairs)])
        out = chunk(0)
        for m, part in enumerate(leaving):
            out = out + swap(part, "col", col_count, 2 * m + 2).astype(F32)
        return out

    def rows_perm(distance, cores):
        return [
            (r * col_count + c, (r ^ (distance + c % cores)) * col_count + c)
            for r in range(row_count)
            for c in range(0, col_count, 3 - cores)
        ]

    def near_of(x_near):
        return pl.pallas_call(
            lambda *refs: near_kernel(clusters, exc, *refs),
            in_specs=[SMEM, SMEM, VMEM, VMEM],
            out_specs=VMEM,
            out_shape=jax.ShapeDtypeStruct((clusters, exc, panels), F32),
            compiler_params=params(others),
            cost_estimate=pl.CostEstimate(flops=1024, bytes_accessed=1024, transcendentals=0),
            name="near",
        )(near_rows, near_cols, x_near, near_blocks).reshape(span, panels)

    whole = lax.ppermute(x, ("row", "col"), rows_perm(1, 1))
    got = [lax.ppermute(x, ("row", "col"), rows_perm(d, 2)) for d in range(2, row_count, 2)]

    def local():
        send, keep, lanes = pl.pallas_call(
            lambda *refs: mirror_kernel(clusters, exc, rank, others, *refs),
            in_specs=[ANY] * 5,
            out_specs=[VMEM] * 3,
            out_shape=shares(others) + [jax.ShapeDtypeStruct((8, entries * rank), jnp.int32)],
            scratch_shapes=[
                pltpu.SMEM(far_rows.shape, jnp.int32),
                pltpu.SMEM(far_cols.shape, jnp.int32),
                pltpu.VMEM(x.shape, BF16),
                pltpu.VMEM(u.shape, BF16),
                pltpu.VMEM(v.shape, BF16),
                pltpu.VMEM((batch * span, entries * rank), BF16),
                pltpu.SemaphoreType.DMA((5,)),
            ],
            compiler_params=params(others),
            cost_estimate=pl.CostEstimate(flops=1024, bytes_accessed=1024, transcendentals=0),
            name="mirror",
        )(far_rows, far_cols, x, u, v)
        total = pair_sum(send, keep)
        beside = swap(total[:, :span].astype(BF16), "row", row_count, 1)
        held = []

        def with_near(leaving):
            *leaving, x_near = lax.optimization_barrier((*leaving, charges))
            held.append(near_of(x_near))
            return leaving

        mirror = col_sum(total[:, span:], with_near).astype(BF16)
        return [mirror[i * span : (i + 1) * span] for i in range(others - 1)], beside, held[0], lanes

    mirror, beside, near, lanes = stage(local)
    from_rows = [swap(part, "row", row_count, i + 2) for i, part in enumerate(mirror)]
    whole, *got, lanes = lax.optimization_barrier((whole, *got, lanes))

    def forward():
        handed = lax.ppermute(whole, "col", [(c, c + 1) for c in range(0, col_count, 2)])
        other = [swap(piece, "col", col_count, 1) for piece in got]
        early, *fetched = pl.pallas_call(
            lambda *refs: early_kernel(clusters, exc, len(got), *refs),
            in_specs=[VMEM] + [ANY] * (4 + len(got)),
            out_specs=[VMEM] * 5,
            out_shape=[
                jax.ShapeDtypeStruct((exc, entries * rank), F32),
                jax.ShapeDtypeStruct(v.shape, BF16),
                jax.ShapeDtypeStruct(u.shape, BF16),
                jax.ShapeDtypeStruct(near.shape, F32),
                jax.ShapeDtypeStruct(x.shape, BF16),
            ],
            scratch_shapes=[
                pltpu.VMEM((len(got) * span, panels), BF16),
                pltpu.SemaphoreType.DMA((4 + len(got),)),
            ],
            compiler_params=params(others),
            cost_estimate=pl.CostEstimate(flops=1024, bytes_accessed=1024, transcendentals=0),
            name="early",
        )(lanes, v, u, near, whole, *got)
        send, keep = pl.pallas_call(
            lambda *refs: forward_kernel(clusters, exc, *refs),
            in_specs=[VMEM] * (7 + len(other)),
            out_specs=[VMEM] * 2,
            out_shape=shares(1),
            compiler_params=params(others),
            cost_estimate=pl.CostEstimate(flops=1024, bytes_accessed=1024, transcendentals=0),
            name="forward",
        )(lanes, early, *fetched, handed, *other)
        return col_sum(pair_sum(send, keep + beside.astype(F32)))

    total = stage(forward)
    for term in from_rows:
        total = total + term.astype(F32)
    return total.reshape(clusters, exc, width)


def solution(mesh):
    placed = (
        P(("parts", "row"), None, None),
        P(("parts", "row", "col"), None, None),
        P(("parts", "row", "col")),
        P(("parts", "row", "col")),
        P(("parts", "row", "col"), None, None),
        P(("parts", "row", "col"), None, None),
        P(("parts", "row", "col")),
        P(("parts", "row", "col")),
    )
    return jax.shard_map(
        body,
        mesh=mesh,
        in_specs=placed,
        out_specs=P(("parts", "row"), None, "col"),
        check_vma=False,
    )
```

```python
import jax
import jax.numpy as jnp
from jax import lax
from jax.experimental import pallas as pl
from jax.experimental.pallas import tpu as pltpu
from jax.sharding import PartitionSpec as P

F32 = jnp.float32
BF16 = jnp.bfloat16
SMEM = pl.BlockSpec(memory_space=pltpu.SMEM)
ANY = pl.BlockSpec(memory_space=pltpu.HBM)
VMEM = pl.BlockSpec(memory_space=pltpu.VMEM)


def dot(a, b):
    return jnp.dot(a, b, preferred_element_type=F32)


def dot_t(a, b):
    return lax.dot_general(a, b, (((1,), (1,)), ((), ())), preferred_element_type=F32)


def params(others):
    return pltpu.CompilerParams(vmem_limit_bytes=(12 if others <= 4 else 48) * 1024 * 1024)


def each(count, step):
    if count <= 4:
        for i in range(count):
            step(i)
    else:
        lax.fori_loop(0, count, lambda i, c: (step(i), c)[1], 0)


def lane_ids(ids_ref, rank):
    count = ids_ref.shape[0]
    lane = lax.broadcasted_iota(jnp.int32, (1, count * rank), 1) // rank
    out = jnp.full((1, count * rank), -1, jnp.int32)
    for b in range(count):
        out = jnp.where(lane == b, ids_ref[b], out)
    return out


def split_columns(half, keep_ref, send_ref, rows, product):
    width = keep_ref.shape[2]
    for q in range(keep_ref.shape[0]):
        for side in range(2):
            at = (2 * q + side) * width
            part = product(slice(at, at + width))

            @pl.when(half == side)
            def _():
                keep_ref[q, rows, :] = part

            @pl.when(half != side)
            def _():
                send_ref[q, rows, :] = part.astype(BF16)


def mirror_kernel(
    clusters, exc, rank, others, rows_hbm, cols_hbm, x_hbm, u_hbm, v_hbm,
    send_ref, keep_ref, lanes_ref,
    rows_ref, cols_ref, x_ref, u_ref, v_ref, mask_ref, sems,
):
    copies = [
        pltpu.make_async_copy(src, dst, sems.at[i])
        for i, (src, dst) in enumerate(
            [(rows_hbm, rows_ref), (cols_hbm, cols_ref), (x_hbm, x_ref), (u_hbm, u_ref), (v_hbm, v_ref)]
        )
    ]
    for copy in copies:
        copy.start()
    group = lax.axis_index("row")
    half = lax.rem(lax.axis_index("col"), 2)
    copies[0].wait()
    copies[1].wait()
    row_lane = lane_ids(rows_ref, rank)
    col_lane = lane_ids(cols_ref, rank)
    lanes_ref[0:1, :] = row_lane
    lanes_ref[1:2, :] = col_lane
    copies[2].wait()
    copies[3].wait()
    every = dot_t(x_ref[...], u_ref[...])
    coef = jnp.zeros((exc, every.shape[1]), F32)
    for c in range(clusters):
        coef += jnp.where(row_lane == group * clusters + c, every[c * exc : (c + 1) * exc], 0.0)
    coef = coef.astype(BF16).astype(F32)
    span = clusters * exc
    copies[4].wait()
    batch = mask_ref.shape[0] // span

    def one(step):
        for i in range(batch):
            other = group ^ (step * batch + i + 1)
            for c in range(clusters):
                at = (i * clusters + c) * exc
                mask_ref[at : at + exc, :] = jnp.where(
                    col_lane == other * clusters + c, coef, 0.0
                ).astype(BF16)
        size = batch * span
        rows = pl.ds(step * size if isinstance(step, int) else pl.multiple_of(step * size, size), size)
        split_columns(half, keep_ref, send_ref, rows, lambda cols: dot(mask_ref[...], v_ref[:, cols]))

    each(others // batch, one)


def near_kernel(clusters, exc, rows_ref, cols_ref, x_ref, n_ref, out_ref):
    first = lax.axis_index("row") * clusters
    out_ref[...] = jnp.zeros_like(out_ref)
    for b in range(n_ref.shape[0]):
        row = rows_ref[b] - first
        col = cols_ref[b] - first
        weight = jnp.where(row == col, 0.5, 1.0).astype(F32)
        out_ref[row] += weight * dot_t(x_ref[col], n_ref[b])
        out_ref[col] += weight * dot(x_ref[row], n_ref[b])


def coef_of(clusters, exc, aways, lanes_ref, v_ref, pieces):
    group = lax.axis_index("row")
    col_lane = lanes_ref[1:2, :]
    coef = jnp.zeros((exc, v_ref.shape[0]), F32)
    batch = len(pieces) if len(pieces) <= 4 else 1
    for n in range(0, len(pieces), batch):
        every = dot_t(jnp.concatenate(pieces[n : n + batch], axis=0), v_ref[...])
        for i in range(batch):
            first = (group ^ aways[n + i]) * clusters
            for c in range(clusters):
                at = (i * clusters + c) * exc
                coef += jnp.where(col_lane == first + c, every[at : at + exc], 0.0)
    return coef


def early_kernel(clusters, exc, count, lanes_ref, *refs):
    sources, (coef_ref, *targets) = refs[: 3 + count], refs[3 + count : 7 + count]
    pieces_ref, sems = refs[7 + count :]
    span = clusters * exc
    moves = [(sources[0], targets[0])]
    moves += [(src, pieces_ref.at[i * span : (i + 1) * span]) for i, src in enumerate(sources[3:])]
    moves += list(zip(sources[1:3], targets[1:]))
    copies = [pltpu.make_async_copy(src, dst, sems.at[i]) for i, (src, dst) in enumerate(moves)]
    for copy in copies:
        copy.start()
    half = lax.rem(lax.axis_index("col"), 2)
    for copy in copies[: 1 + count]:
        copy.wait()
    pieces = [pieces_ref[i * span : (i + 1) * span] for i in range(count)]
    aways = [1] + [2 * t + half for t in range(1, count)]
    coef_ref[...] = coef_of(clusters, exc, aways, lanes_ref, targets[0], pieces)
    for copy in copies[1 + count :]:
        copy.wait()


def forward_kernel(clusters, exc, lanes_ref, early_ref, v_ref, u_ref, near_ref, *refs):
    send_ref, keep_ref = refs[-2:]
    group = lax.axis_index("row")
    half = lax.rem(lax.axis_index("col"), 2)
    pieces = [ref[...] for ref in refs[:-2]]
    aways = [2 * t + 3 - half for t in range(len(pieces))]
    coef = early_ref[...] + coef_of(clusters, exc, aways, lanes_ref, v_ref, pieces)
    coef = coef.astype(BF16).astype(F32)
    row_lane = lanes_ref[0:1, :]
    masked = jnp.concatenate(
        [jnp.where(row_lane == group * clusters + c, coef, 0.0) for c in range(clusters)], axis=0
    ).astype(BF16)
    rows = slice(None)
    split_columns(
        half, keep_ref, send_ref, rows, lambda cols: dot(masked, u_ref[:, cols]) + near_ref[:, cols]
    )


def swap(value, axis, size, step):
    return lax.ppermute(value, axis, [(i, i ^ step) for i in range(size)])


def stage(work):
    shapes = jax.eval_shape(work)
    inside = lax.axis_index("row") < lax.axis_size("row")
    return lax.cond(inside, work, lambda: jax.tree.map(lambda a: jnp.zeros(a.shape, a.dtype), shapes))


def body(charges, near_blocks, near_rows, near_cols, far_u, far_v, far_rows, far_cols):
    clusters, exc, panels = charges.shape
    entries, rank, _ = far_u.shape
    row_count = lax.axis_size("row")
    col_count = lax.axis_size("col")
    others = row_count - 1
    pairs = col_count // 2
    width = panels // col_count
    span = clusters * exc
    batch = others if others <= 4 else 1
    place = lax.axis_index("col")
    x = charges.reshape(span, panels)
    u = far_u.reshape(entries * rank, panels)
    v = far_v.reshape(entries * rank, panels)

    def shares(count):
        return [
            jax.ShapeDtypeStruct((pairs, count * span, width), BF16),
            jax.ShapeDtypeStruct((pairs, count * span, width), F32),
        ]

    def pair_sum(send, keep):
        return keep + swap(send, "col", col_count, 1).astype(F32)

    def col_sum(total, between=lambda leaving: leaving):
        def chunk(m):
            return lax.dynamic_index_in_dim(total, place // 2 ^ m, 0, keepdims=False)

        leaving = between([chunk(m).astype(BF16) for m in range(1, pairs)])
        out = chunk(0)
        for m, part in enumerate(leaving):
            out = out + swap(part, "col", col_count, 2 * m + 2).astype(F32)
        return out

    def near_of(x_near):
        return pl.pallas_call(
            lambda *refs: near_kernel(clusters, exc, *refs),
            in_specs=[SMEM, SMEM, VMEM, VMEM],
            out_specs=VMEM,
            out_shape=jax.ShapeDtypeStruct((clusters, exc, panels), F32),
            compiler_params=params(others),
            cost_estimate=pl.CostEstimate(flops=1024, bytes_accessed=1024, transcendentals=0),
            name="near",
        )(near_rows, near_cols, x_near, near_blocks).reshape(span, panels)

    whole = swap(x, "row", row_count, 1)
    got = []
    for d in range(2, row_count, 2):
        perm = [
            (r * col_count + c, (r ^ (d + c % 2)) * col_count + c)
            for r in range(row_count)
            for c in range(col_count)
        ]
        got.append(lax.ppermute(x, ("row", "col"), perm))

    def local():
        send, keep, lanes = pl.pallas_call(
            lambda *refs: mirror_kernel(clusters, exc, rank, others, *refs),
            in_specs=[ANY] * 5,
            out_specs=[VMEM] * 3,
            out_shape=shares(others) + [jax.ShapeDtypeStruct((8, entries * rank), jnp.int32)],
            scratch_shapes=[
                pltpu.SMEM(far_rows.shape, jnp.int32),
                pltpu.SMEM(far_cols.shape, jnp.int32),
                pltpu.VMEM(x.shape, BF16),
                pltpu.VMEM(u.shape, BF16),
                pltpu.VMEM(v.shape, BF16),
                pltpu.VMEM((batch * span, entries * rank), BF16),
                pltpu.SemaphoreType.DMA((5,)),
            ],
            compiler_params=params(others),
            cost_estimate=pl.CostEstimate(flops=1024, bytes_accessed=1024, transcendentals=0),
            name="mirror",
        )(far_rows, far_cols, x, u, v)
        total = pair_sum(send, keep)
        held = []

        def with_near(leaving):
            *leaving, x_near = lax.optimization_barrier((*leaving, charges))
            held.append(near_of(x_near))
            return leaving

        mirror = col_sum(total, with_near).astype(BF16)
        return [mirror[i * span : (i + 1) * span] for i in range(others)], held[0], lanes

    mirror, near, lanes = stage(local)
    from_rows = [swap(mirror[d - 1], "row", row_count, d) for d in range(2, row_count)]
    whole, *got, lanes = lax.optimization_barrier((whole, *got, lanes))

    def forward():
        other = [swap(piece, "col", col_count, 1) for piece in got]
        early, *fetched = pl.pallas_call(
            lambda *refs: early_kernel(clusters, exc, 1 + len(got), *refs),
            in_specs=[VMEM] + [ANY] * (4 + len(got)),
            out_specs=[VMEM] * 4,
            out_shape=[
                jax.ShapeDtypeStruct((exc, entries * rank), F32),
                jax.ShapeDtypeStruct(v.shape, BF16),
                jax.ShapeDtypeStruct(u.shape, BF16),
                jax.ShapeDtypeStruct(near.shape, F32),
            ],
            scratch_shapes=[
                pltpu.VMEM(((1 + len(got)) * span, panels), BF16),
                pltpu.SemaphoreType.DMA((4 + len(got),)),
            ],
            compiler_params=params(others),
            cost_estimate=pl.CostEstimate(flops=1024, bytes_accessed=1024, transcendentals=0),
            name="early",
        )(lanes, v, u, near, whole, *got)
        send, keep = pl.pallas_call(
            lambda *refs: forward_kernel(clusters, exc, *refs),
            in_specs=[VMEM] * (5 + len(other)),
            out_specs=[VMEM] * 2,
            out_shape=shares(1),
            compiler_params=params(others),
            cost_estimate=pl.CostEstimate(flops=1024, bytes_accessed=1024, transcendentals=0),
            name="forward",
        )(lanes, early, *fetched, *other)
        return col_sum(pair_sum(send, keep)) + swap(mirror[0], "row", row_count, 1).astype(F32)

    total = stage(forward)
    for term in from_rows:
        total = total + term.astype(F32)
    return total.reshape(clusters, exc, width)


def solution(mesh):
    placed = (
        P(("parts", "row"), None, None),
        P(("parts", "row", "col"), None, None),
        P(("parts", "row", "col")),
        P(("parts", "row", "col")),
        P(("parts", "row", "col"), None, None),
        P(("parts", "row", "col"), None, None),
        P(("parts", "row", "col")),
        P(("parts", "row", "col")),
    )
    return jax.shard_map(
        body,
        mesh=mesh,
        in_specs=placed,
        out_specs=P(("parts", "row"), None, "col"),
        check_vma=False,
    )
```

```python
import jax
import jax.numpy as jnp
from jax import lax
from jax.experimental import pallas as pl
from jax.experimental.pallas import tpu as pltpu
from jax.sharding import PartitionSpec as P

F32 = jnp.float32
BF16 = jnp.bfloat16
SMEM = pl.BlockSpec(memory_space=pltpu.SMEM)
ANY = pl.BlockSpec(memory_space=pltpu.HBM)
VMEM = pl.BlockSpec(memory_space=pltpu.VMEM)


def dot(a, b):
    return jnp.dot(a, b, preferred_element_type=F32)


def dot_t(a, b):
    return lax.dot_general(a, b, (((1,), (1,)), ((), ())), preferred_element_type=F32)


def params(others):
    return pltpu.CompilerParams(vmem_limit_bytes=(12 if others <= 4 else 48) * 1024 * 1024)


def each(count, step):
    if count <= 4:
        for i in range(count):
            step(i)
    else:
        lax.fori_loop(0, count, lambda i, c: (step(i), c)[1], 0)


def lane_ids(ids_ref, rank):
    count = ids_ref.shape[0]
    lane = lax.broadcasted_iota(jnp.int32, (1, count * rank), 1) // rank
    out = jnp.full((1, count * rank), -1, jnp.int32)
    for b in range(count):
        out = jnp.where(lane == b, ids_ref[b], out)
    return out


def split_columns(half, keep_ref, send_ref, rows, product):
    width = keep_ref.shape[2]
    for q in range(keep_ref.shape[0]):
        for side in range(2):
            at = (2 * q + side) * width
            part = product(slice(at, at + width))

            @pl.when(half == side)
            def _():
                keep_ref[q, rows, :] = part

            @pl.when(half != side)
            def _():
                send_ref[q, rows, :] = part.astype(BF16)


def side_columns(half, out_ref, rows, product):
    width = out_ref.shape[2]
    for side in range(2):

        @pl.when(half == side)
        def _():
            for q in range(out_ref.shape[0]):
                at = (2 * q + side) * width
                out_ref[q, rows, :] = product(slice(at, at + width)).astype(out_ref.dtype)


def batches(count, span):
    size = span * (count if count <= 4 else 1)

    def rows_of(step):
        return pl.ds(step * size if isinstance(step, int) else pl.multiple_of(step * size, size), size)

    return size // span, count * span // size, rows_of


def mirror_kernel(
    clusters, exc, rank, others, rows_hbm, cols_hbm, x_hbm, u_hbm, v_hbm,
    send_ref, mask_ref, lanes_ref,
    rows_ref, cols_ref, x_ref, u_ref, v_ref, sems,
):
    copies = [
        pltpu.make_async_copy(src, dst, sems.at[i])
        for i, (src, dst) in enumerate(
            [(rows_hbm, rows_ref), (cols_hbm, cols_ref), (x_hbm, x_ref), (u_hbm, u_ref), (v_hbm, v_ref)]
        )
    ]
    for copy in copies:
        copy.start()
    group = lax.axis_index("row")
    half = lax.rem(lax.axis_index("col"), 2)
    copies[0].wait()
    copies[1].wait()
    row_lane = lane_ids(rows_ref, rank)
    col_lane = lane_ids(cols_ref, rank)
    lanes_ref[0:1, :] = row_lane
    lanes_ref[1:2, :] = col_lane
    copies[2].wait()
    copies[3].wait()
    every = dot_t(x_ref[...], u_ref[...])
    coef = jnp.zeros((exc, every.shape[1]), F32)
    for c in range(clusters):
        coef += jnp.where(row_lane == group * clusters + c, every[c * exc : (c + 1) * exc], 0.0)
    coef = coef.astype(BF16).astype(F32)
    copies[4].wait()
    batch, steps, rows_of = batches(others, clusters * exc)

    def one(step):
        masked = []
        for i in range(batch):
            first = (group ^ (step * batch + i + 1)) * clusters
            masked += [jnp.where(col_lane == first + c, coef, 0.0) for c in range(clusters)]
        rows = rows_of(step)
        mask_ref[rows, :] = jnp.concatenate(masked, axis=0).astype(BF16)
        side_columns(1 - half, send_ref, rows, lambda cols: dot(mask_ref[rows, :], v_ref[:, cols]))

    each(steps, one)


def kept_kernel(clusters, exc, others, mask_ref, v_ref, keep_ref):
    half = lax.rem(lax.axis_index("col"), 2)
    _, steps, rows_of = batches(others, clusters * exc)

    def one(step):
        rows = rows_of(step)
        side_columns(half, keep_ref, rows, lambda cols: dot(mask_ref[rows, :], v_ref[:, cols]))

    each(steps, one)


def near_kernel(clusters, exc, rows_ref, cols_ref, x_ref, n_ref, out_ref):
    first = lax.axis_index("row") * clusters
    out_ref[...] = jnp.zeros_like(out_ref)
    for b in range(n_ref.shape[0]):
        row = rows_ref[b] - first
        col = cols_ref[b] - first
        weight = jnp.where(row == col, 0.5, 1.0).astype(F32)
        out_ref[row] += weight * dot_t(x_ref[col], n_ref[b])
        out_ref[col] += weight * dot(x_ref[row], n_ref[b])


def coef_of(clusters, exc, aways, lanes_ref, v_ref, pieces):
    group = lax.axis_index("row")
    col_lane = lanes_ref[1:2, :]
    coef = jnp.zeros((exc, v_ref.shape[0]), F32)
    batch = len(pieces) if len(pieces) <= 4 else 1
    for n in range(0, len(pieces), batch):
        every = dot_t(jnp.concatenate(pieces[n : n + batch], axis=0), v_ref[...])
        for i in range(batch):
            first = (group ^ aways[n + i]) * clusters
            for c in range(clusters):
                at = (i * clusters + c) * exc
                coef += jnp.where(col_lane == first + c, every[at : at + exc], 0.0)
    return coef


def early_kernel(clusters, exc, count, lanes_ref, *refs):
    sources, (coef_ref, *targets) = refs[: 3 + count], refs[3 + count : 7 + count]
    pieces_ref, sems = refs[7 + count :]
    span = clusters * exc
    moves = [(sources[0], targets[0])]
    moves += [(src, pieces_ref.at[i * span : (i + 1) * span]) for i, src in enumerate(sources[3:])]
    moves += list(zip(sources[1:3], targets[1:]))
    copies = [pltpu.make_async_copy(src, dst, sems.at[i]) for i, (src, dst) in enumerate(moves)]
    for copy in copies:
        copy.start()
    half = lax.rem(lax.axis_index("col"), 2)
    for copy in copies[: 1 + count]:
        copy.wait()
    pieces = [pieces_ref[i * span : (i + 1) * span] for i in range(count)]
    aways = [2 * t + half for t in range(1, count + 1)]
    coef_ref[...] = coef_of(clusters, exc, aways, lanes_ref, targets[0], pieces)
    for copy in copies[1 + count :]:
        copy.wait()


def forward_kernel(clusters, exc, lanes_ref, early_ref, v_ref, u_ref, near_ref, whole_ref, handed_ref, *refs):
    send_ref, keep_ref = refs[-2:]
    group = lax.axis_index("row")
    half = lax.rem(lax.axis_index("col"), 2)
    pieces = [jnp.where(half == 0, whole_ref[...], handed_ref[...])] + [ref[...] for ref in refs[:-2]]
    aways = [1] + [2 * t + 1 - half for t in range(1, len(pieces))]
    coef = early_ref[...] + coef_of(clusters, exc, aways, lanes_ref, v_ref, pieces)
    coef = coef.astype(BF16).astype(F32)
    row_lane = lanes_ref[0:1, :]
    masked = jnp.concatenate(
        [jnp.where(row_lane == group * clusters + c, coef, 0.0) for c in range(clusters)], axis=0
    ).astype(BF16)
    rows = slice(None)
    split_columns(
        half, keep_ref, send_ref, rows, lambda cols: dot(masked, u_ref[:, cols]) + near_ref[:, cols]
    )


def swap(value, axis, size, step):
    return lax.ppermute(value, axis, [(i, i ^ step) for i in range(size)])


def stage(work):
    shapes = jax.eval_shape(work)
    inside = lax.axis_index("row") < lax.axis_size("row")
    return lax.cond(inside, work, lambda: jax.tree.map(lambda a: jnp.zeros(a.shape, a.dtype), shapes))


def body(charges, near_blocks, near_rows, near_cols, far_u, far_v, far_rows, far_cols):
    clusters, exc, panels = charges.shape
    entries, rank, _ = far_u.shape
    row_count = lax.axis_size("row")
    col_count = lax.axis_size("col")
    others = row_count - 1
    pairs = col_count // 2
    width = panels // col_count
    span = clusters * exc
    place = lax.axis_index("col")
    x = charges.reshape(span, panels)
    u = far_u.reshape(entries * rank, panels)
    v = far_v.reshape(entries * rank, panels)

    def shares(count):
        return [
            jax.ShapeDtypeStruct((pairs, count * span, width), BF16),
            jax.ShapeDtypeStruct((pairs, count * span, width), F32),
        ]

    def pair_sum(send, keep):
        return keep + swap(send, "col", col_count, 1).astype(F32)

    def col_sum(total, between=lambda leaving: leaving):
        def chunk(m):
            return lax.dynamic_index_in_dim(total, place // 2 ^ m, 0, keepdims=False)

        leaving = between([chunk(m).astype(BF16) for m in range(1, pairs)])
        out = chunk(0)
        for m, part in enumerate(leaving):
            out = out + swap(part, "col", col_count, 2 * m + 2).astype(F32)
        return out

    def near_of(x_near):
        return pl.pallas_call(
            lambda *refs: near_kernel(clusters, exc, *refs),
            in_specs=[SMEM, SMEM, VMEM, VMEM],
            out_specs=VMEM,
            out_shape=jax.ShapeDtypeStruct((clusters, exc, panels), F32),
            compiler_params=params(others),
            cost_estimate=pl.CostEstimate(flops=1024, bytes_accessed=1024, transcendentals=0),
            name="near",
        )(near_rows, near_cols, x_near, near_blocks).reshape(span, panels)

    def rows_perm(distance):
        return [
            (r * col_count + c, (r ^ distance(c % 2)) * col_count + c)
            for r in range(row_count)
            for c in range(col_count)
        ]

    whole = lax.ppermute(x, ("row", "col"), rows_perm(lambda core: 1 - core))
    got = [lax.ppermute(x, ("row", "col"), rows_perm(lambda core: d + core)) for d in range(2, row_count, 2)]

    def local():
        send, mask, lanes = pl.pallas_call(
            lambda *refs: mirror_kernel(clusters, exc, rank, others, *refs),
            in_specs=[ANY] * 5,
            out_specs=[VMEM] * 3,
            out_shape=[
                shares(others)[0],
                jax.ShapeDtypeStruct((others * span, entries * rank), BF16),
                jax.ShapeDtypeStruct((8, entries * rank), jnp.int32),
            ],
            scratch_shapes=[
                pltpu.SMEM(far_rows.shape, jnp.int32),
                pltpu.SMEM(far_cols.shape, jnp.int32),
                pltpu.VMEM(x.shape, BF16),
                pltpu.VMEM(u.shape, BF16),
                pltpu.VMEM(v.shape, BF16),
                pltpu.SemaphoreType.DMA((5,)),
            ],
            compiler_params=params(others),
            cost_estimate=pl.CostEstimate(flops=1024, bytes_accessed=1024, transcendentals=0),
            name="mirror",
        )(far_rows, far_cols, x, u, v)
        keep = pl.pallas_call(
            lambda *refs: kept_kernel(clusters, exc, others, *refs),
            in_specs=[VMEM] * 2,
            out_specs=VMEM,
            out_shape=shares(others)[1],
            compiler_params=params(others),
            cost_estimate=pl.CostEstimate(flops=1024, bytes_accessed=1024, transcendentals=0),
            name="kept",
        )(mask, v)
        total = pair_sum(send, keep)
        held = []

        def with_near(leaving):
            *leaving, x_near = lax.optimization_barrier((*leaving, charges))
            held.append(near_of(x_near))
            return leaving

        mirror = col_sum(total, with_near).astype(BF16)
        return [mirror[i * span : (i + 1) * span] for i in range(others)], held[0], lanes

    mirror, near, lanes = stage(local)
    from_rows = [swap(mirror[d - 1], "row", row_count, d) for d in range(2, row_count)]
    *got, lanes = lax.optimization_barrier((*got, lanes))
    whole, *got = lax.optimization_barrier((whole, *got))

    def forward():
        handed = swap(whole, "col", col_count, 1)
        other = [swap(piece, "col", col_count, 1) for piece in got]
        early, *fetched = pl.pallas_call(
            lambda *refs: early_kernel(clusters, exc, len(got), *refs),
            in_specs=[VMEM] + [ANY] * (3 + len(got)),
            out_specs=[VMEM] * 4,
            out_shape=[
                jax.ShapeDtypeStruct((exc, entries * rank), F32),
                jax.ShapeDtypeStruct(v.shape, BF16),
                jax.ShapeDtypeStruct(u.shape, BF16),
                jax.ShapeDtypeStruct(near.shape, F32),
            ],
            scratch_shapes=[
                pltpu.VMEM((len(got) * span, panels), BF16),
                pltpu.SemaphoreType.DMA((3 + len(got),)),
            ],
            compiler_params=params(others),
            cost_estimate=pl.CostEstimate(flops=1024, bytes_accessed=1024, transcendentals=0),
            name="early",
        )(lanes, v, u, near, *got)
        send, keep = pl.pallas_call(
            lambda *refs: forward_kernel(clusters, exc, *refs),
            in_specs=[VMEM] * (7 + len(other)),
            out_specs=[VMEM] * 2,
            out_shape=shares(1),
            compiler_params=params(others),
            cost_estimate=pl.CostEstimate(flops=1024, bytes_accessed=1024, transcendentals=0),
            name="forward",
        )(lanes, early, *fetched, whole, handed, *other)
        return col_sum(pair_sum(send, keep)) + swap(mirror[0], "row", row_count, 1).astype(F32)

    total = stage(forward)
    for term in from_rows:
        total = total + term.astype(F32)
    return total.reshape(clusters, exc, width)


def solution(mesh):
    placed = (
        P(("parts", "row"), None, None),
        P(("parts", "row", "col"), None, None),
        P(("parts", "row", "col")),
        P(("parts", "row", "col")),
        P(("parts", "row", "col"), None, None),
        P(("parts", "row", "col"), None, None),
        P(("parts", "row", "col")),
        P(("parts", "row", "col")),
    )
    return jax.shard_map(
        body,
        mesh=mesh,
        in_specs=placed,
        out_specs=P(("parts", "row"), None, "col"),
        check_vma=False,
    )
```

```python
import jax
import jax.numpy as jnp
from jax import lax
from jax.experimental import pallas as pl
from jax.experimental.pallas import tpu as pltpu
from jax.sharding import PartitionSpec as P

F32 = jnp.float32
BF16 = jnp.bfloat16
SMEM = pl.BlockSpec(memory_space=pltpu.SMEM)
ANY = pl.BlockSpec(memory_space=pltpu.HBM)
VMEM = pl.BlockSpec(memory_space=pltpu.VMEM)


def dot(a, b):
    return jnp.dot(a, b, preferred_element_type=F32)


def dot_t(a, b):
    return lax.dot_general(a, b, (((1,), (1,)), ((), ())), preferred_element_type=F32)


def params(others):
    return pltpu.CompilerParams(vmem_limit_bytes=(12 if others <= 4 else 48) * 1024 * 1024)


def each(count, step):
    if count <= 4:
        for i in range(count):
            step(i)
    else:
        lax.fori_loop(0, count, lambda i, c: (step(i), c)[1], 0)


def lane_ids(ids_ref, rank):
    count = ids_ref.shape[0]
    lane = lax.broadcasted_iota(jnp.int32, (1, count * rank), 1) // rank
    out = jnp.full((1, count * rank), -1, jnp.int32)
    for b in range(count):
        out = jnp.where(lane == b, ids_ref[b], out)
    return out


def split_columns(half, keep_ref, send_ref, rows, product):
    width = keep_ref.shape[2]
    for q in range(keep_ref.shape[0]):
        for side in range(2):
            at = (2 * q + side) * width
            part = product(slice(at, at + width))

            @pl.when(half == side)
            def _():
                keep_ref[q, rows, :] = part

            @pl.when(half != side)
            def _():
                send_ref[q, rows, :] = part.astype(BF16)


def side_columns(half, out_ref, rows, product):
    width = out_ref.shape[2]
    for side in range(2):

        @pl.when(half == side)
        def _():
            for q in range(out_ref.shape[0]):
                at = (2 * q + side) * width
                out_ref[q, rows, :] = product(slice(at, at + width)).astype(out_ref.dtype)


def batches(count, span):
    size = span * (count if count <= 4 else 1)

    def rows_of(step):
        return pl.ds(step * size if isinstance(step, int) else pl.multiple_of(step * size, size), size)

    return size // span, count * span // size, rows_of


def mirror_kernel(
    clusters, exc, rank, others, rows_hbm, cols_hbm, x_hbm, u_hbm, v_hbm,
    send_ref, mask_ref, lanes_ref,
    rows_ref, cols_ref, x_ref, u_ref, v_ref, sems,
):
    copies = [
        pltpu.make_async_copy(src, dst, sems.at[i])
        for i, (src, dst) in enumerate(
            [(rows_hbm, rows_ref), (cols_hbm, cols_ref), (x_hbm, x_ref), (u_hbm, u_ref), (v_hbm, v_ref)]
        )
    ]
    for copy in copies:
        copy.start()
    group = lax.axis_index("row")
    half = lax.rem(lax.axis_index("col"), 2)
    copies[0].wait()
    copies[1].wait()
    row_lane = lane_ids(rows_ref, rank)
    col_lane = lane_ids(cols_ref, rank)
    lanes_ref[0:1, :] = row_lane
    lanes_ref[1:2, :] = col_lane
    copies[2].wait()
    copies[3].wait()
    every = dot_t(x_ref[...], u_ref[...])
    coef = jnp.zeros((exc, every.shape[1]), F32)
    for c in range(clusters):
        coef += jnp.where(row_lane == group * clusters + c, every[c * exc : (c + 1) * exc], 0.0)
    coef = coef.astype(BF16).astype(F32)
    copies[4].wait()
    batch, steps, rows_of = batches(others, clusters * exc)

    def one(step):
        masked = []
        for i in range(batch):
            first = (group ^ (step * batch + i + 1)) * clusters
            masked += [jnp.where(col_lane == first + c, coef, 0.0) for c in range(clusters)]
        rows = rows_of(step)
        mask_ref[rows, :] = jnp.concatenate(masked, axis=0).astype(BF16)
        side_columns(1 - half, send_ref, rows, lambda cols: dot(mask_ref[rows, :], v_ref[:, cols]))

    each(steps, one)


def kept_kernel(clusters, exc, others, mask_ref, v_ref, keep_ref):
    half = lax.rem(lax.axis_index("col"), 2)
    _, steps, rows_of = batches(others, clusters * exc)

    def one(step):
        rows = rows_of(step)
        side_columns(half, keep_ref, rows, lambda cols: dot(mask_ref[rows, :], v_ref[:, cols]))

    each(steps, one)


def near_kernel(clusters, exc, rows_ref, cols_ref, x_ref, n_ref, out_ref):
    first = lax.axis_index("row") * clusters
    out_ref[...] = jnp.zeros_like(out_ref)
    for b in range(n_ref.shape[0]):
        row = rows_ref[b] - first
        col = cols_ref[b] - first
        weight = jnp.where(row == col, 0.5, 1.0).astype(F32)
        out_ref[row] += weight * dot_t(x_ref[col], n_ref[b])
        out_ref[col] += weight * dot(x_ref[row], n_ref[b])


def coef_of(clusters, exc, aways, lanes_ref, v_ref, pieces):
    group = lax.axis_index("row")
    col_lane = lanes_ref[1:2, :]
    coef = jnp.zeros((exc, v_ref.shape[0]), F32)
    batch = len(pieces) if len(pieces) <= 4 else 1
    for n in range(0, len(pieces), batch):
        every = dot_t(jnp.concatenate(pieces[n : n + batch], axis=0), v_ref[...])
        for i in range(batch):
            first = (group ^ aways[n + i]) * clusters
            for c in range(clusters):
                at = (i * clusters + c) * exc
                coef += jnp.where(col_lane == first + c, every[at : at + exc], 0.0)
    return coef


def early_kernel(clusters, exc, count, lanes_ref, *refs):
    sources, (coef_ref, *targets) = refs[: 3 + count], refs[3 + count : 7 + count]
    pieces_ref, sems = refs[7 + count :]
    span = clusters * exc
    moves = [(sources[0], targets[0])]
    moves += [(src, pieces_ref.at[i * span : (i + 1) * span]) for i, src in enumerate(sources[3:])]
    moves += list(zip(sources[1:3], targets[1:]))
    copies = [pltpu.make_async_copy(src, dst, sems.at[i]) for i, (src, dst) in enumerate(moves)]
    for copy in copies:
        copy.start()
    half = lax.rem(lax.axis_index("col"), 2)
    for copy in copies[: 1 + count]:
        copy.wait()
    pieces = [pieces_ref[i * span : (i + 1) * span] for i in range(count)]
    aways = [1] + [2 * t + half for t in range(1, count)]
    coef_ref[...] = coef_of(clusters, exc, aways, lanes_ref, targets[0], pieces)
    for copy in copies[1 + count :]:
        copy.wait()


def forward_kernel(clusters, exc, lanes_ref, early_ref, v_ref, u_ref, near_ref, *refs):
    send_ref, keep_ref = refs[-2:]
    group = lax.axis_index("row")
    half = lax.rem(lax.axis_index("col"), 2)
    pieces = [ref[...] for ref in refs[:-2]]
    aways = [2 * t + 3 - half for t in range(len(pieces))]
    coef = early_ref[...] + coef_of(clusters, exc, aways, lanes_ref, v_ref, pieces)
    coef = coef.astype(BF16).astype(F32)
    row_lane = lanes_ref[0:1, :]
    masked = jnp.concatenate(
        [jnp.where(row_lane == group * clusters + c, coef, 0.0) for c in range(clusters)], axis=0
    ).astype(BF16)
    rows = slice(None)
    split_columns(
        half, keep_ref, send_ref, rows, lambda cols: dot(masked, u_ref[:, cols]) + near_ref[:, cols]
    )


def swap(value, axis, size, step):
    return lax.ppermute(value, axis, [(i, i ^ step) for i in range(size)])


def stage(work):
    shapes = jax.eval_shape(work)
    inside = lax.axis_index("row") < lax.axis_size("row")
    return lax.cond(inside, work, lambda: jax.tree.map(lambda a: jnp.zeros(a.shape, a.dtype), shapes))


def body(charges, near_blocks, near_rows, near_cols, far_u, far_v, far_rows, far_cols):
    clusters, exc, panels = charges.shape
    entries, rank, _ = far_u.shape
    row_count = lax.axis_size("row")
    col_count = lax.axis_size("col")
    others = row_count - 1
    pairs = col_count // 2
    width = panels // col_count
    span = clusters * exc
    place = lax.axis_index("col")
    x = charges.reshape(span, panels)
    u = far_u.reshape(entries * rank, panels)
    v = far_v.reshape(entries * rank, panels)

    def shares(count):
        return [
            jax.ShapeDtypeStruct((pairs, count * span, width), BF16),
            jax.ShapeDtypeStruct((pairs, count * span, width), F32),
        ]

    def pair_sum(send, keep):
        return keep + swap(send, "col", col_count, 1).astype(F32)

    def col_sum(total, between=lambda leaving: leaving):
        def chunk(m):
            return lax.dynamic_index_in_dim(total, place // 2 ^ m, 0, keepdims=False)

        leaving = between([chunk(m).astype(BF16) for m in range(1, pairs)])
        out = chunk(0)
        for m, part in enumerate(leaving):
            out = out + swap(part, "col", col_count, 2 * m + 2).astype(F32)
        return out

    def near_of(x_near):
        return pl.pallas_call(
            lambda *refs: near_kernel(clusters, exc, *refs),
            in_specs=[SMEM, SMEM, VMEM, VMEM],
            out_specs=VMEM,
            out_shape=jax.ShapeDtypeStruct((clusters, exc, panels), F32),
            compiler_params=params(others),
            cost_estimate=pl.CostEstimate(flops=1024, bytes_accessed=1024, transcendentals=0),
            name="near",
        )(near_rows, near_cols, x_near, near_blocks).reshape(span, panels)

    def rows_perm(distance):
        return [
            (r * col_count + c, (r ^ (distance + c % 2)) * col_count + c)
            for r in range(row_count)
            for c in range(col_count)
        ]

    whole = swap(x, "row", row_count, 1)
    got = [lax.ppermute(x, ("row", "col"), rows_perm(d)) for d in range(2, row_count, 2)]

    def local():
        send, mask, lanes = pl.pallas_call(
            lambda *refs: mirror_kernel(clusters, exc, rank, others, *refs),
            in_specs=[ANY] * 5,
            out_specs=[VMEM] * 3,
            out_shape=[
                shares(others)[0],
                jax.ShapeDtypeStruct((others * span, entries * rank), BF16),
                jax.ShapeDtypeStruct((8, entries * rank), jnp.int32),
            ],
            scratch_shapes=[
                pltpu.SMEM(far_rows.shape, jnp.int32),
                pltpu.SMEM(far_cols.shape, jnp.int32),
                pltpu.VMEM(x.shape, BF16),
                pltpu.VMEM(u.shape, BF16),
                pltpu.VMEM(v.shape, BF16),
                pltpu.SemaphoreType.DMA((5,)),
            ],
            compiler_params=params(others),
            cost_estimate=pl.CostEstimate(flops=1024, bytes_accessed=1024, transcendentals=0),
            name="mirror",
        )(far_rows, far_cols, x, u, v)
        keep = pl.pallas_call(
            lambda *refs: kept_kernel(clusters, exc, others, *refs),
            in_specs=[VMEM] * 2,
            out_specs=VMEM,
            out_shape=shares(others)[1],
            compiler_params=params(others),
            cost_estimate=pl.CostEstimate(flops=1024, bytes_accessed=1024, transcendentals=0),
            name="kept",
        )(mask, v)
        total = pair_sum(send, keep)
        held = []

        def with_near(leaving):
            *leaving, x_near = lax.optimization_barrier((*leaving, charges))
            held.append(near_of(x_near))
            return leaving

        mirror = col_sum(total, with_near).astype(BF16)
        return [mirror[i * span : (i + 1) * span] for i in range(others)], held[0], lanes

    mirror, near, lanes = stage(local)
    from_rows = [swap(mirror[d - 1], "row", row_count, d) for d in range(2, row_count)]
    *got, lanes = lax.optimization_barrier((*got, lanes))
    whole, *got = lax.optimization_barrier((whole, *got))

    def forward():
        other = [swap(piece, "col", col_count, 1) for piece in got]
        early, *fetched = pl.pallas_call(
            lambda *refs: early_kernel(clusters, exc, 1 + len(got), *refs),
            in_specs=[VMEM] + [ANY] * (4 + len(got)),
            out_specs=[VMEM] * 4,
            out_shape=[
                jax.ShapeDtypeStruct((exc, entries * rank), F32),
                jax.ShapeDtypeStruct(v.shape, BF16),
                jax.ShapeDtypeStruct(u.shape, BF16),
                jax.ShapeDtypeStruct(near.shape, F32),
            ],
            scratch_shapes=[
                pltpu.VMEM(((1 + len(got)) * span, panels), BF16),
                pltpu.SemaphoreType.DMA((4 + len(got),)),
            ],
            compiler_params=params(others),
            cost_estimate=pl.CostEstimate(flops=1024, bytes_accessed=1024, transcendentals=0),
            name="early",
        )(lanes, v, u, near, whole, *got)
        send, keep = pl.pallas_call(
            lambda *refs: forward_kernel(clusters, exc, *refs),
            in_specs=[VMEM] * (5 + len(other)),
            out_specs=[VMEM] * 2,
            out_shape=shares(1),
            compiler_params=params(others),
            cost_estimate=pl.CostEstimate(flops=1024, bytes_accessed=1024, transcendentals=0),
            name="forward",
        )(lanes, early, *fetched, *other)
        return col_sum(pair_sum(send, keep)) + swap(mirror[0], "row", row_count, 1).astype(F32)

    total = stage(forward)
    for term in from_rows:
        total = total + term.astype(F32)
    return total.reshape(clusters, exc, width)


def solution(mesh):
    placed = (
        P(("parts", "row"), None, None),
        P(("parts", "row", "col"), None, None),
        P(("parts", "row", "col")),
        P(("parts", "row", "col")),
        P(("parts", "row", "col"), None, None),
        P(("parts", "row", "col"), None, None),
        P(("parts", "row", "col")),
        P(("parts", "row", "col")),
    )
    return jax.shard_map(
        body,
        mesh=mesh,
        in_specs=placed,
        out_specs=P(("parts", "row"), None, "col"),
        check_vma=False,
    )
```

```python
import jax
import jax.numpy as jnp
from jax import lax
from jax.experimental import pallas as pl
from jax.experimental.pallas import tpu as pltpu
from jax.sharding import PartitionSpec as P

F32 = jnp.float32
BF16 = jnp.bfloat16
SMEM = pl.BlockSpec(memory_space=pltpu.SMEM)
ANY = pl.BlockSpec(memory_space=pltpu.HBM)
VMEM = pl.BlockSpec(memory_space=pltpu.VMEM)


def dot(a, b):
    return jnp.dot(a, b, preferred_element_type=F32)


def dot_t(a, b):
    return lax.dot_general(a, b, (((1,), (1,)), ((), ())), preferred_element_type=F32)


def params(others):
    return pltpu.CompilerParams(vmem_limit_bytes=(12 if others <= 4 else 48) * 1024 * 1024)


def each(count, step):
    if count <= 4:
        for i in range(count):
            step(i)
    else:
        lax.fori_loop(0, count, lambda i, c: (step(i), c)[1], 0)


def lane_ids(ids_ref, rank):
    count = ids_ref.shape[0]
    lane = lax.broadcasted_iota(jnp.int32, (1, count * rank), 1) // rank
    out = jnp.full((1, count * rank), -1, jnp.int32)
    for b in range(count):
        out = jnp.where(lane == b, ids_ref[b], out)
    return out


def split_columns(half, keep_ref, send_ref, rows, product):
    width = keep_ref.shape[2]
    for q in range(keep_ref.shape[0]):
        for side in range(2):
            at = (2 * q + side) * width
            part = product(slice(at, at + width))

            @pl.when(half == side)
            def _():
                keep_ref[q, rows, :] = part

            @pl.when(half != side)
            def _():
                send_ref[q, rows, :] = part.astype(BF16)


def side_columns(half, out_ref, rows, product):
    width = out_ref.shape[2]
    for side in range(2):

        @pl.when(half == side)
        def _():
            for q in range(out_ref.shape[0]):
                at = (2 * q + side) * width
                out_ref[q, rows, :] = product(slice(at, at + width)).astype(out_ref.dtype)


def batches(count, span):
    size = span * (count if count <= 4 else 1)

    def rows_of(step):
        return pl.ds(step * size if isinstance(step, int) else pl.multiple_of(step * size, size), size)

    return size // span, count * span // size, rows_of


def mirror_kernel(
    clusters, exc, rank, others, rows_hbm, cols_hbm, x_hbm, u_hbm, v_hbm,
    send_ref, mask_ref, lanes_ref,
    rows_ref, cols_ref, x_ref, u_ref, v_ref, sems,
):
    copies = [
        pltpu.make_async_copy(src, dst, sems.at[i])
        for i, (src, dst) in enumerate(
            [(u_hbm, u_ref), (x_hbm, x_ref), (rows_hbm, rows_ref), (cols_hbm, cols_ref), (v_hbm, v_ref)]
        )
    ]
    for copy in copies:
        copy.start()
    group = lax.axis_index("row")
    half = lax.rem(lax.axis_index("col"), 2)
    copies[2].wait()
    copies[3].wait()
    row_lane = lane_ids(rows_ref, rank)
    col_lane = lane_ids(cols_ref, rank)
    lanes_ref[0:1, :] = row_lane
    lanes_ref[1:2, :] = col_lane
    copies[0].wait()
    copies[1].wait()
    every = dot_t(x_ref[...], u_ref[...])
    coef = jnp.zeros((exc, every.shape[1]), F32)
    for c in range(clusters):
        coef += jnp.where(row_lane == group * clusters + c, every[c * exc : (c + 1) * exc], 0.0)
    coef = coef.astype(BF16).astype(F32)
    copies[4].wait()
    batch, steps, rows_of = batches(others, clusters * exc)

    def one(step):
        masked = []
        for i in range(batch):
            first = (group ^ (step * batch + i + 1)) * clusters
            masked += [jnp.where(col_lane == first + c, coef, 0.0) for c in range(clusters)]
        rows = rows_of(step)
        mask_ref[rows, :] = jnp.concatenate(masked, axis=0).astype(BF16)
        side_columns(1 - half, send_ref, rows, lambda cols: dot(mask_ref[rows, :], v_ref[:, cols]))

    each(steps, one)


def kept_kernel(clusters, exc, others, mask_ref, v_ref, keep_ref):
    half = lax.rem(lax.axis_index("col"), 2)
    _, steps, rows_of = batches(others, clusters * exc)

    def one(step):
        rows = rows_of(step)
        side_columns(half, keep_ref, rows, lambda cols: dot(mask_ref[rows, :], v_ref[:, cols]))

    each(steps, one)


def near_kernel(clusters, exc, rows_ref, cols_ref, x_ref, n_ref, out_ref):
    first = lax.axis_index("row") * clusters
    out_ref[...] = jnp.zeros_like(out_ref)
    for b in range(n_ref.shape[0]):
        row = rows_ref[b] - first
        col = cols_ref[b] - first
        weight = jnp.where(row == col, 0.5, 1.0).astype(F32)
        out_ref[row] += weight * dot_t(x_ref[col], n_ref[b])
        out_ref[col] += weight * dot(x_ref[row], n_ref[b])


def coef_of(clusters, exc, aways, lanes_ref, v_ref, pieces):
    group = lax.axis_index("row")
    col_lane = lanes_ref[1:2, :]
    coef = jnp.zeros((exc, v_ref.shape[0]), F32)
    batch = len(pieces) if len(pieces) <= 4 else 1
    for n in range(0, len(pieces), batch):
        every = dot_t(jnp.concatenate(pieces[n : n + batch], axis=0), v_ref[...])
        for i in range(batch):
            first = (group ^ aways[n + i]) * clusters
            for c in range(clusters):
                at = (i * clusters + c) * exc
                coef += jnp.where(col_lane == first + c, every[at : at + exc], 0.0)
    return coef


def early_kernel(clusters, exc, count, lanes_ref, *refs):
    sources, (coef_ref, *targets) = refs[: 3 + count], refs[3 + count : 7 + count]
    pieces_ref, sems = refs[7 + count :]
    span = clusters * exc
    moves = [(sources[0], targets[0])]
    moves += [(src, pieces_ref.at[i * span : (i + 1) * span]) for i, src in enumerate(sources[3:])]
    moves += list(zip(sources[1:3], targets[1:]))
    copies = [pltpu.make_async_copy(src, dst, sems.at[i]) for i, (src, dst) in enumerate(moves)]
    for copy in copies:
        copy.start()
    half = lax.rem(lax.axis_index("col"), 2)
    for copy in copies[: 1 + count]:
        copy.wait()
    pieces = [pieces_ref[i * span : (i + 1) * span] for i in range(count)]
    aways = [1] + [2 * t + half for t in range(1, count)]
    coef_ref[...] = coef_of(clusters, exc, aways, lanes_ref, targets[0], pieces)
    for copy in copies[1 + count :]:
        copy.wait()


def forward_kernel(clusters, exc, lanes_ref, early_ref, v_ref, u_ref, near_ref, *refs):
    send_ref, keep_ref = refs[-2:]
    group = lax.axis_index("row")
    half = lax.rem(lax.axis_index("col"), 2)
    pieces = [ref[...] for ref in refs[:-2]]
    aways = [2 * t + 3 - half for t in range(len(pieces))]
    coef = early_ref[...] + coef_of(clusters, exc, aways, lanes_ref, v_ref, pieces)
    coef = coef.astype(BF16).astype(F32)
    row_lane = lanes_ref[0:1, :]
    masked = jnp.concatenate(
        [jnp.where(row_lane == group * clusters + c, coef, 0.0) for c in range(clusters)], axis=0
    ).astype(BF16)
    rows = slice(None)
    split_columns(
        half, keep_ref, send_ref, rows, lambda cols: dot(masked, u_ref[:, cols]) + near_ref[:, cols]
    )


def swap(value, axis, size, step):
    return lax.ppermute(value, axis, [(i, i ^ step) for i in range(size)])


def stage(work):
    shapes = jax.eval_shape(work)
    inside = lax.axis_index("row") < lax.axis_size("row")
    return lax.cond(inside, work, lambda: jax.tree.map(lambda a: jnp.zeros(a.shape, a.dtype), shapes))


def body(charges, near_blocks, near_rows, near_cols, far_u, far_v, far_rows, far_cols):
    clusters, exc, panels = charges.shape
    entries, rank, _ = far_u.shape
    row_count = lax.axis_size("row")
    col_count = lax.axis_size("col")
    others = row_count - 1
    pairs = col_count // 2
    width = panels // col_count
    span = clusters * exc
    place = lax.axis_index("col")
    x = charges.reshape(span, panels)
    u = far_u.reshape(entries * rank, panels)
    v = far_v.reshape(entries * rank, panels)

    def shares(count):
        return [
            jax.ShapeDtypeStruct((pairs, count * span, width), BF16),
            jax.ShapeDtypeStruct((pairs, count * span, width), F32),
        ]

    def pair_sum(send, keep):
        return keep + swap(send, "col", col_count, 1).astype(F32)

    def chunks(total):
        def chunk(m):
            return lax.dynamic_index_in_dim(total, place // 2 ^ m, 0, keepdims=False)

        return chunk(0), [chunk(m).astype(BF16) for m in range(1, pairs)]

    def col_sum(out, leaving):
        for m, part in enumerate(leaving):
            out = out + swap(part, "col", col_count, 2 * m + 2).astype(F32)
        return out

    def near_of(x_near):
        return pl.pallas_call(
            lambda *refs: near_kernel(clusters, exc, *refs),
            in_specs=[SMEM, SMEM, VMEM, VMEM],
            out_specs=VMEM,
            out_shape=jax.ShapeDtypeStruct((clusters, exc, panels), F32),
            compiler_params=params(others),
            cost_estimate=pl.CostEstimate(flops=1024, bytes_accessed=1024, transcendentals=0),
            name="near",
        )(near_rows, near_cols, x_near, near_blocks).reshape(span, panels)

    def rows_perm(distance):
        return [
            (r * col_count + c, (r ^ (distance + c % 2)) * col_count + c)
            for r in range(row_count)
            for c in range(col_count)
        ]

    whole = swap(x, "row", row_count, 1)
    got = [lax.ppermute(x, ("row", "col"), rows_perm(d)) for d in range(2, row_count, 2)]

    def local():
        send, mask, lanes = pl.pallas_call(
            lambda *refs: mirror_kernel(clusters, exc, rank, others, *refs),
            in_specs=[ANY] * 5,
            out_specs=[VMEM] * 3,
            out_shape=[
                shares(others)[0],
                jax.ShapeDtypeStruct((others * span, entries * rank), BF16),
                jax.ShapeDtypeStruct((8, entries * rank), jnp.int32),
            ],
            scratch_shapes=[
                pltpu.SMEM(far_rows.shape, jnp.int32),
                pltpu.SMEM(far_cols.shape, jnp.int32),
                pltpu.VMEM(x.shape, BF16),
                pltpu.VMEM(u.shape, BF16),
                pltpu.VMEM(v.shape, BF16),
                pltpu.SemaphoreType.DMA((5,)),
            ],
            compiler_params=params(others),
            cost_estimate=pl.CostEstimate(flops=1024, bytes_accessed=1024, transcendentals=0),
            name="mirror",
        )(far_rows, far_cols, x, u, v)
        keep = pl.pallas_call(
            lambda *refs: kept_kernel(clusters, exc, others, *refs),
            in_specs=[VMEM] * 2,
            out_specs=VMEM,
            out_shape=shares(others)[1],
            compiler_params=params(others),
            cost_estimate=pl.CostEstimate(flops=1024, bytes_accessed=1024, transcendentals=0),
            name="kept",
        )(mask, v)
        total = pair_sum(send, keep)
        far, leaving = chunks(total[:, span:])
        *leaving, x_near = lax.optimization_barrier((*leaving, charges))
        near = near_of(x_near)
        far = col_sum(far, leaving).astype(BF16)
        return chunks(total[:, :span]), [far[i * span : (i + 1) * span] for i in range(others - 1)], near, lanes

    (one, one_leaving), far, near, lanes = stage(local)
    from_rows = [swap(part, "row", row_count, i + 2) for i, part in enumerate(far)]
    whole, *got, lanes = lax.optimization_barrier((whole, *got, lanes))

    def forward():
        other = [swap(piece, "col", col_count, 1) for piece in got]
        early, *fetched = pl.pallas_call(
            lambda *refs: early_kernel(clusters, exc, 1 + len(got), *refs),
            in_specs=[VMEM] + [ANY] * (4 + len(got)),
            out_specs=[VMEM] * 4,
            out_shape=[
                jax.ShapeDtypeStruct((exc, entries * rank), F32),
                jax.ShapeDtypeStruct(v.shape, BF16),
                jax.ShapeDtypeStruct(u.shape, BF16),
                jax.ShapeDtypeStruct(near.shape, F32),
            ],
            scratch_shapes=[
                pltpu.VMEM(((1 + len(got)) * span, panels), BF16),
                pltpu.SemaphoreType.DMA((4 + len(got),)),
            ],
            compiler_params=params(others),
            cost_estimate=pl.CostEstimate(flops=1024, bytes_accessed=1024, transcendentals=0),
            name="early",
        )(lanes, v, u, near, whole, *got)
        send, keep = pl.pallas_call(
            lambda *refs: forward_kernel(clusters, exc, *refs),
            in_specs=[VMEM] * (5 + len(other)),
            out_specs=[VMEM] * 2,
            out_shape=shares(1),
            compiler_params=params(others),
            cost_estimate=pl.CostEstimate(flops=1024, bytes_accessed=1024, transcendentals=0),
            name="forward",
        )(lanes, early, *fetched, *other)
        joined = col_sum(one, one_leaving).astype(BF16)
        return col_sum(*chunks(pair_sum(send, keep))) + swap(joined, "row", row_count, 1).astype(F32)

    total = stage(forward)
    for term in from_rows:
        total = total + term.astype(F32)
    return total.reshape(clusters, exc, width)


def solution(mesh):
    placed = (
        P(("parts", "row"), None, None),
        P(("parts", "row", "col"), None, None),
        P(("parts", "row", "col")),
        P(("parts", "row", "col")),
        P(("parts", "row", "col"), None, None),
        P(("parts", "row", "col"), None, None),
        P(("parts", "row", "col")),
        P(("parts", "row", "col")),
    )
    return jax.shard_map(
        body,
        mesh=mesh,
        in_specs=placed,
        out_specs=P(("parts", "row"), None, "col"),
        check_vma=False,
    )
```

```python
import jax
import jax.numpy as jnp
from jax import lax
from jax.experimental import pallas as pl
from jax.experimental.pallas import tpu as pltpu
from jax.sharding import PartitionSpec as P

F32 = jnp.float32
BF16 = jnp.bfloat16
SMEM = pl.BlockSpec(memory_space=pltpu.SMEM)
ANY = pl.BlockSpec(memory_space=pltpu.HBM)
VMEM = pl.BlockSpec(memory_space=pltpu.VMEM)


def dot(a, b):
    return jnp.dot(a, b, preferred_element_type=F32)


def dot_t(a, b):
    return lax.dot_general(a, b, (((1,), (1,)), ((), ())), preferred_element_type=F32)


def params(others):
    return pltpu.CompilerParams(vmem_limit_bytes=(12 if others <= 4 else 48) * 1024 * 1024)


def each(count, step):
    if count <= 4:
        for i in range(count):
            step(i)
    else:
        lax.fori_loop(0, count, lambda i, c: (step(i), c)[1], 0)


def lane_ids(ids_ref, rank):
    count = ids_ref.shape[0]
    lane = lax.broadcasted_iota(jnp.int32, (1, count * rank), 1) // rank
    out = jnp.full((1, count * rank), -1, jnp.int32)
    for b in range(count):
        out = jnp.where(lane == b, ids_ref[b], out)
    return out


def split_columns(half, keep_ref, send_ref, rows, product):
    width = keep_ref.shape[2]
    for q in range(keep_ref.shape[0]):
        for side in range(2):
            at = (2 * q + side) * width
            part = product(slice(at, at + width))

            @pl.when(half == side)
            def _():
                keep_ref[q, rows, :] = part

            @pl.when(half != side)
            def _():
                send_ref[q, rows, :] = part.astype(BF16)


def side_columns(half, out_ref, rows, product):
    width = out_ref.shape[2]
    for side in range(2):

        @pl.when(half == side)
        def _():
            for q in range(out_ref.shape[0]):
                at = (2 * q + side) * width
                out_ref[q, rows, :] = product(slice(at, at + width)).astype(out_ref.dtype)


def batches(count, span):
    size = span * (count if count <= 4 else 1)

    def rows_of(step):
        return pl.ds(step * size if isinstance(step, int) else pl.multiple_of(step * size, size), size)

    return size // span, count * span // size, rows_of


def mirror_kernel(
    clusters, exc, rank, others, rows_hbm, cols_hbm, x_hbm, u_hbm, v_hbm,
    send_ref, mask_ref, lanes_ref,
    rows_ref, cols_ref, x_ref, u_ref, v_ref, sems,
):
    copies = [
        pltpu.make_async_copy(src, dst, sems.at[i])
        for i, (src, dst) in enumerate(
            [(u_hbm, u_ref), (x_hbm, x_ref), (rows_hbm, rows_ref), (cols_hbm, cols_ref), (v_hbm, v_ref)]
        )
    ]
    for copy in copies:
        copy.start()
    group = lax.axis_index("row")
    half = lax.rem(lax.axis_index("col"), 2)
    copies[2].wait()
    copies[3].wait()
    row_lane = lane_ids(rows_ref, rank)
    col_lane = lane_ids(cols_ref, rank)
    lanes_ref[0:1, :] = row_lane
    lanes_ref[1:2, :] = col_lane
    copies[0].wait()
    copies[1].wait()
    every = dot_t(x_ref[...], u_ref[...])
    coef = jnp.zeros((exc, every.shape[1]), F32)
    for c in range(clusters):
        coef += jnp.where(row_lane == group * clusters + c, every[c * exc : (c + 1) * exc], 0.0)
    coef = coef.astype(BF16).astype(F32)
    copies[4].wait()
    batch, steps, rows_of = batches(others, clusters * exc)

    def one(step):
        masked = []
        for i in range(batch):
            first = (group ^ (step * batch + i + 1)) * clusters
            masked += [jnp.where(col_lane == first + c, coef, 0.0) for c in range(clusters)]
        rows = rows_of(step)
        mask_ref[rows, :] = jnp.concatenate(masked, axis=0).astype(BF16)
        side_columns(1 - half, send_ref, rows, lambda cols: dot(mask_ref[rows, :], v_ref[:, cols]))

    each(steps, one)


def kept_kernel(clusters, exc, others, mask_ref, v_ref, keep_ref):
    half = lax.rem(lax.axis_index("col"), 2)
    _, steps, rows_of = batches(others, clusters * exc)

    def one(step):
        rows = rows_of(step)
        side_columns(half, keep_ref, rows, lambda cols: dot(mask_ref[rows, :], v_ref[:, cols]))

    each(steps, one)


def pair_kernel(split, keep_ref, recv_ref, *out_refs):
    mine = lax.axis_index("col") // 2
    for m in range(keep_ref.shape[0]):
        total = keep_ref[mine ^ m] + recv_ref[mine ^ m].astype(F32)
        out_refs[2 * m][...] = total[:split].astype(out_refs[2 * m].dtype)
        out_refs[2 * m + 1][...] = total[split:].astype(out_refs[2 * m + 1].dtype)


def near_kernel(clusters, exc, rows_ref, cols_ref, x_ref, n_ref, out_ref):
    first = lax.axis_index("row") * clusters
    out_ref[...] = jnp.zeros_like(out_ref)
    for b in range(n_ref.shape[0]):
        row = rows_ref[b] - first
        col = cols_ref[b] - first
        weight = jnp.where(row == col, 0.5, 1.0).astype(F32)
        out_ref[row] += weight * dot_t(x_ref[col], n_ref[b])
        out_ref[col] += weight * dot(x_ref[row], n_ref[b])


def coef_of(clusters, exc, aways, lanes_ref, v_ref, pieces):
    group = lax.axis_index("row")
    col_lane = lanes_ref[1:2, :]
    coef = jnp.zeros((exc, v_ref.shape[0]), F32)
    batch = len(pieces) if len(pieces) <= 4 else 1
    for n in range(0, len(pieces), batch):
        every = dot_t(jnp.concatenate(pieces[n : n + batch], axis=0), v_ref[...])
        for i in range(batch):
            first = (group ^ aways[n + i]) * clusters
            for c in range(clusters):
                at = (i * clusters + c) * exc
                coef += jnp.where(col_lane == first + c, every[at : at + exc], 0.0)
    return coef


def early_kernel(clusters, exc, count, lanes_ref, *refs):
    sources, (coef_ref, *targets) = refs[: 3 + count], refs[3 + count : 7 + count]
    pieces_ref, sems = refs[7 + count :]
    span = clusters * exc
    moves = [(sources[0], targets[0])]
    moves += [(src, pieces_ref.at[i * span : (i + 1) * span]) for i, src in enumerate(sources[3:])]
    moves += list(zip(sources[1:3], targets[1:]))
    copies = [pltpu.make_async_copy(src, dst, sems.at[i]) for i, (src, dst) in enumerate(moves)]
    for copy in copies:
        copy.start()
    half = lax.rem(lax.axis_index("col"), 2)
    for copy in copies[: 1 + count]:
        copy.wait()
    pieces = [pieces_ref[i * span : (i + 1) * span] for i in range(count)]
    aways = [1] + [2 * t + half for t in range(1, count)]
    coef_ref[...] = coef_of(clusters, exc, aways, lanes_ref, targets[0], pieces)
    for copy in copies[1 + count :]:
        copy.wait()


def forward_kernel(clusters, exc, lanes_ref, early_ref, v_ref, u_ref, near_ref, *refs):
    send_ref, keep_ref = refs[-2:]
    group = lax.axis_index("row")
    half = lax.rem(lax.axis_index("col"), 2)
    pieces = [ref[...] for ref in refs[:-2]]
    aways = [2 * t + 3 - half for t in range(len(pieces))]
    coef = early_ref[...] + coef_of(clusters, exc, aways, lanes_ref, v_ref, pieces)
    coef = coef.astype(BF16).astype(F32)
    row_lane = lanes_ref[0:1, :]
    masked = jnp.concatenate(
        [jnp.where(row_lane == group * clusters + c, coef, 0.0) for c in range(clusters)], axis=0
    ).astype(BF16)
    rows = slice(None)
    split_columns(
        half, keep_ref, send_ref, rows, lambda cols: dot(masked, u_ref[:, cols]) + near_ref[:, cols]
    )


def swap(value, axis, size, step):
    return lax.ppermute(value, axis, [(i, i ^ step) for i in range(size)])


def stage(work):
    shapes = jax.eval_shape(work)
    inside = lax.axis_index("row") < lax.axis_size("row")
    return lax.cond(inside, work, lambda: jax.tree.map(lambda a: jnp.zeros(a.shape, a.dtype), shapes))


def body(charges, near_blocks, near_rows, near_cols, far_u, far_v, far_rows, far_cols):
    clusters, exc, panels = charges.shape
    entries, rank, _ = far_u.shape
    row_count = lax.axis_size("row")
    col_count = lax.axis_size("col")
    others = row_count - 1
    pairs = col_count // 2
    width = panels // col_count
    span = clusters * exc
    place = lax.axis_index("col")
    x = charges.reshape(span, panels)
    u = far_u.reshape(entries * rank, panels)
    v = far_v.reshape(entries * rank, panels)

    def shares(count):
        return [
            jax.ShapeDtypeStruct((pairs, count * span, width), BF16),
            jax.ShapeDtypeStruct((pairs, count * span, width), F32),
        ]

    def pair_sum(send, keep):
        return keep + swap(send, "col", col_count, 1).astype(F32)

    def chunks(total):
        def chunk(m):
            return lax.dynamic_index_in_dim(total, place // 2 ^ m, 0, keepdims=False)

        return chunk(0), [chunk(m).astype(BF16) for m in range(1, pairs)]

    def col_sum(out, leaving):
        for m, part in enumerate(leaving):
            out = out + swap(part, "col", col_count, 2 * m + 2).astype(F32)
        return out

    def near_of(x_near):
        return pl.pallas_call(
            lambda *refs: near_kernel(clusters, exc, *refs),
            in_specs=[SMEM, SMEM, VMEM, VMEM],
            out_specs=VMEM,
            out_shape=jax.ShapeDtypeStruct((clusters, exc, panels), F32),
            compiler_params=params(others),
            cost_estimate=pl.CostEstimate(flops=1024, bytes_accessed=1024, transcendentals=0),
            name="near",
        )(near_rows, near_cols, x_near, near_blocks).reshape(span, panels)

    def rows_perm(distance):
        return [
            (r * col_count + c, (r ^ (distance + c % 2)) * col_count + c)
            for r in range(row_count)
            for c in range(col_count)
        ]

    whole = swap(x, "row", row_count, 1)
    got = [lax.ppermute(x, ("row", "col"), rows_perm(d)) for d in range(2, row_count, 2)]

    def local():
        send, mask, lanes = pl.pallas_call(
            lambda *refs: mirror_kernel(clusters, exc, rank, others, *refs),
            in_specs=[ANY] * 5,
            out_specs=[VMEM] * 3,
            out_shape=[
                shares(others)[0],
                jax.ShapeDtypeStruct((others * span, entries * rank), BF16),
                jax.ShapeDtypeStruct((8, entries * rank), jnp.int32),
            ],
            scratch_shapes=[
                pltpu.SMEM(far_rows.shape, jnp.int32),
                pltpu.SMEM(far_cols.shape, jnp.int32),
                pltpu.VMEM(x.shape, BF16),
                pltpu.VMEM(u.shape, BF16),
                pltpu.VMEM(v.shape, BF16),
                pltpu.SemaphoreType.DMA((5,)),
            ],
            compiler_params=params(others),
            cost_estimate=pl.CostEstimate(flops=1024, bytes_accessed=1024, transcendentals=0),
            name="mirror",
        )(far_rows, far_cols, x, u, v)
        keep = pl.pallas_call(
            lambda *refs: kept_kernel(clusters, exc, others, *refs),
            in_specs=[VMEM] * 2,
            out_specs=VMEM,
            out_shape=shares(others)[1],
            compiler_params=params(others),
            cost_estimate=pl.CostEstimate(flops=1024, bytes_accessed=1024, transcendentals=0),
            name="kept",
        )(mask, v)
        kinds = [F32] + [BF16] * (pairs - 1)
        one, far, *leaving = pl.pallas_call(
            lambda *refs: pair_kernel(span, *refs),
            in_specs=[VMEM] * 2,
            out_specs=[VMEM] * (2 * pairs),
            out_shape=[
                jax.ShapeDtypeStruct((rows * span, width), kind) for kind in kinds for rows in (1, others - 1)
            ],
            compiler_params=params(others),
            cost_estimate=pl.CostEstimate(flops=1024, bytes_accessed=1024, transcendentals=0),
            name="pair",
        )(keep, swap(send, "col", col_count, 1))
        one_leaving, leaving = leaving[::2], leaving[1::2]
        *leaving, x_near = lax.optimization_barrier((*leaving, charges))
        near = near_of(x_near)
        far = col_sum(far, leaving).astype(BF16)
        return (one, one_leaving), [far[i * span : (i + 1) * span] for i in range(others - 1)], near, lanes

    (one, one_leaving), far, near, lanes = stage(local)
    from_rows = [swap(part, "row", row_count, i + 2) for i, part in enumerate(far)]
    whole, *got, lanes = lax.optimization_barrier((whole, *got, lanes))

    def forward():
        other = [swap(piece, "col", col_count, 1) for piece in got]
        early, *fetched = pl.pallas_call(
            lambda *refs: early_kernel(clusters, exc, 1 + len(got), *refs),
            in_specs=[VMEM] + [ANY] * (4 + len(got)),
            out_specs=[VMEM] * 4,
            out_shape=[
                jax.ShapeDtypeStruct((exc, entries * rank), F32),
                jax.ShapeDtypeStruct(v.shape, BF16),
                jax.ShapeDtypeStruct(u.shape, BF16),
                jax.ShapeDtypeStruct(near.shape, F32),
            ],
            scratch_shapes=[
                pltpu.VMEM(((1 + len(got)) * span, panels), BF16),
                pltpu.SemaphoreType.DMA((4 + len(got),)),
            ],
            compiler_params=params(others),
            cost_estimate=pl.CostEstimate(flops=1024, bytes_accessed=1024, transcendentals=0),
            name="early",
        )(lanes, v, u, near, whole, *got)
        send, keep = pl.pallas_call(
            lambda *refs: forward_kernel(clusters, exc, *refs),
            in_specs=[VMEM] * (5 + len(other)),
            out_specs=[VMEM] * 2,
            out_shape=shares(1),
            compiler_params=params(others),
            cost_estimate=pl.CostEstimate(flops=1024, bytes_accessed=1024, transcendentals=0),
            name="forward",
        )(lanes, early, *fetched, *other)
        joined = col_sum(one, one_leaving).astype(BF16)
        return col_sum(*chunks(pair_sum(send, keep))) + swap(joined, "row", row_count, 1).astype(F32)

    total = stage(forward)
    for term in from_rows:
        total = total + term.astype(F32)
    return total.reshape(clusters, exc, width)


def solution(mesh):
    placed = (
        P(("parts", "row"), None, None),
        P(("parts", "row", "col"), None, None),
        P(("parts", "row", "col")),
        P(("parts", "row", "col")),
        P(("parts", "row", "col"), None, None),
        P(("parts", "row", "col"), None, None),
        P(("parts", "row", "col")),
        P(("parts", "row", "col")),
    )
    return jax.shard_map(
        body,
        mesh=mesh,
        in_specs=placed,
        out_specs=P(("parts", "row"), None, "col"),
        check_vma=False,
    )
```

```python
import jax
import jax.numpy as jnp
from jax import lax
from jax.experimental import pallas as pl
from jax.experimental.pallas import tpu as pltpu
from jax.sharding import PartitionSpec as P

F32 = jnp.float32
BF16 = jnp.bfloat16
SMEM = pl.BlockSpec(memory_space=pltpu.SMEM)
ANY = pl.BlockSpec(memory_space=pltpu.HBM)
VMEM = pl.BlockSpec(memory_space=pltpu.VMEM)


def dot(a, b):
    return jnp.dot(a, b, preferred_element_type=F32)


def dot_t(a, b):
    return lax.dot_general(a, b, (((1,), (1,)), ((), ())), preferred_element_type=F32)


def params(others):
    return pltpu.CompilerParams(vmem_limit_bytes=(12 if others <= 4 else 48) * 1024 * 1024)


def each(count, step):
    if count <= 4:
        for i in range(count):
            step(i)
    else:
        lax.fori_loop(0, count, lambda i, c: (step(i), c)[1], 0)


def lane_ids(ids_ref, rank):
    count = ids_ref.shape[0]
    lane = lax.broadcasted_iota(jnp.int32, (1, count * rank), 1) // rank
    out = jnp.full((1, count * rank), -1, jnp.int32)
    for b in range(count):
        out = jnp.where(lane == b, ids_ref[b], out)
    return out


def split_columns(half, keep_ref, send_ref, rows, product):
    width = keep_ref.shape[2]
    for q in range(keep_ref.shape[0]):
        for side in range(2):
            at = (2 * q + side) * width
            part = product(slice(at, at + width))

            @pl.when(half == side)
            def _():
                keep_ref[q, rows, :] = part

            @pl.when(half != side)
            def _():
                send_ref[q, rows, :] = part.astype(BF16)


def side_columns(half, out_ref, rows, product):
    width = out_ref.shape[2]
    for side in range(2):

        @pl.when(half == side)
        def _():
            for q in range(out_ref.shape[0]):
                at = (2 * q + side) * width
                out_ref[q, rows, :] = product(slice(at, at + width)).astype(out_ref.dtype)


def batches(count, span):
    size = span * (count if count <= 4 else 1)

    def rows_of(step):
        return pl.ds(step * size if isinstance(step, int) else pl.multiple_of(step * size, size), size)

    return size // span, count * span // size, rows_of


def mirror_kernel(
    clusters, exc, rank, others, rows_hbm, cols_hbm, x_hbm, u_hbm, v_hbm,
    send_ref, mask_ref, lanes_ref,
    rows_ref, cols_ref, x_ref, u_ref, v_ref, sems,
):
    copies = [
        pltpu.make_async_copy(src, dst, sems.at[i])
        for i, (src, dst) in enumerate(
            [(u_hbm, u_ref), (x_hbm, x_ref), (rows_hbm, rows_ref), (cols_hbm, cols_ref), (v_hbm, v_ref)]
        )
    ]
    for copy in copies:
        copy.start()
    group = lax.axis_index("row")
    half = lax.rem(lax.axis_index("col"), 2)
    copies[2].wait()
    copies[3].wait()
    row_lane = lane_ids(rows_ref, rank)
    col_lane = lane_ids(cols_ref, rank)
    lanes_ref[0:1, :] = row_lane
    lanes_ref[1:2, :] = col_lane
    copies[0].wait()
    copies[1].wait()
    every = dot_t(x_ref[...], u_ref[...])
    coef = jnp.zeros((exc, every.shape[1]), F32)
    for c in range(clusters):
        coef += jnp.where(row_lane == group * clusters + c, every[c * exc : (c + 1) * exc], 0.0)
    coef = coef.astype(BF16).astype(F32)
    copies[4].wait()
    batch, steps, rows_of = batches(others, clusters * exc)

    def one(step):
        masked = []
        for i in range(batch):
            first = (group ^ (step * batch + i + 1)) * clusters
            masked += [jnp.where(col_lane == first + c, coef, 0.0) for c in range(clusters)]
        rows = rows_of(step)
        mask_ref[rows, :] = jnp.concatenate(masked, axis=0).astype(BF16)
        side_columns(1 - half, send_ref, rows, lambda cols: dot(mask_ref[rows, :], v_ref[:, cols]))

    each(steps, one)


def kept_kernel(clusters, exc, others, mask_ref, v_ref, keep_ref):
    half = lax.rem(lax.axis_index("col"), 2)
    _, steps, rows_of = batches(others, clusters * exc)

    def one(step):
        rows = rows_of(step)
        side_columns(half, keep_ref, rows, lambda cols: dot(mask_ref[rows, :], v_ref[:, cols]))

    each(steps, one)


def pair_kernel(split, keep_ref, recv_ref, *out_refs):
    mine = lax.axis_index("col") // 2
    for m in range(keep_ref.shape[0]):
        total = keep_ref[mine ^ m] + recv_ref[mine ^ m].astype(F32)
        out_refs[2 * m][...] = total[:split].astype(out_refs[2 * m].dtype)
        out_refs[2 * m + 1][...] = total[split:].astype(out_refs[2 * m + 1].dtype)


def near_kernel(clusters, exc, rows_ref, cols_ref, x_ref, n_ref, out_ref):
    first = lax.axis_index("row") * clusters
    out_ref[...] = jnp.zeros_like(out_ref)
    for b in range(n_ref.shape[0]):
        row = rows_ref[b] - first
        col = cols_ref[b] - first
        weight = jnp.where(row == col, 0.5, 1.0).astype(F32)
        out_ref[row] += weight * dot_t(x_ref[col], n_ref[b])
        out_ref[col] += weight * dot(x_ref[row], n_ref[b])


def coef_of(clusters, exc, aways, lanes_ref, v_ref, pieces):
    group = lax.axis_index("row")
    col_lane = lanes_ref[1:2, :]
    coef = jnp.zeros((exc, v_ref.shape[0]), F32)
    batch = len(pieces) if len(pieces) <= 4 else 1
    for n in range(0, len(pieces), batch):
        every = dot_t(jnp.concatenate(pieces[n : n + batch], axis=0), v_ref[...])
        for i in range(batch):
            first = (group ^ aways[n + i]) * clusters
            for c in range(clusters):
                at = (i * clusters + c) * exc
                coef += jnp.where(col_lane == first + c, every[at : at + exc], 0.0)
    return coef


def early_kernel(clusters, exc, count, lanes_ref, *refs):
    sources, (coef_ref, *targets) = refs[: 3 + count], refs[3 + count : 7 + count]
    pieces_ref, sems = refs[7 + count :]
    span = clusters * exc
    moves = [(sources[0], targets[0])]
    moves += [(src, pieces_ref.at[i * span : (i + 1) * span]) for i, src in enumerate(sources[3:])]
    moves += list(zip(sources[1:3], targets[1:]))
    copies = [pltpu.make_async_copy(src, dst, sems.at[i]) for i, (src, dst) in enumerate(moves)]
    for copy in copies:
        copy.start()
    half = lax.rem(lax.axis_index("col"), 2)
    for copy in copies[: 1 + count]:
        copy.wait()
    pieces = [pieces_ref[i * span : (i + 1) * span] for i in range(count)]
    aways = [1] + [2 * t + half for t in range(1, count)]
    coef_ref[...] = coef_of(clusters, exc, aways, lanes_ref, targets[0], pieces)
    for copy in copies[1 + count :]:
        copy.wait()


def forward_kernel(clusters, exc, lanes_ref, early_ref, v_ref, u_ref, near_ref, *refs):
    send_ref, keep_ref = refs[-2:]
    group = lax.axis_index("row")
    half = lax.rem(lax.axis_index("col"), 2)
    pieces = [ref[...] for ref in refs[:-2]]
    aways = [2 * t + 3 - half for t in range(len(pieces))]
    coef = early_ref[...] + coef_of(clusters, exc, aways, lanes_ref, v_ref, pieces)
    coef = coef.astype(BF16).astype(F32)
    row_lane = lanes_ref[0:1, :]
    masked = jnp.concatenate(
        [jnp.where(row_lane == group * clusters + c, coef, 0.0) for c in range(clusters)], axis=0
    ).astype(BF16)
    rows = slice(None)
    split_columns(
        half, keep_ref, send_ref, rows, lambda cols: dot(masked, u_ref[:, cols]) + near_ref[:, cols]
    )


def swap(value, axis, size, step):
    return lax.ppermute(value, axis, [(i, i ^ step) for i in range(size)])


def stage(work):
    shapes = jax.eval_shape(work)
    inside = lax.axis_index("row") < lax.axis_size("row")
    return lax.cond(inside, work, lambda: jax.tree.map(lambda a: jnp.zeros(a.shape, a.dtype), shapes))


def body(charges, near_blocks, near_rows, near_cols, far_u, far_v, far_rows, far_cols):
    clusters, exc, panels = charges.shape
    entries, rank, _ = far_u.shape
    row_count = lax.axis_size("row")
    col_count = lax.axis_size("col")
    others = row_count - 1
    pairs = col_count // 2
    width = panels // col_count
    span = clusters * exc
    place = lax.axis_index("col")
    x = charges.reshape(span, panels)
    u = far_u.reshape(entries * rank, panels)
    v = far_v.reshape(entries * rank, panels)

    def shares(count):
        return [
            jax.ShapeDtypeStruct((pairs, count * span, width), BF16),
            jax.ShapeDtypeStruct((pairs, count * span, width), F32),
        ]

    def pair_sum(send, keep):
        return keep + swap(send, "col", col_count, 1).astype(F32)

    def chunks(total):
        def chunk(m):
            return lax.dynamic_index_in_dim(total, place // 2 ^ m, 0, keepdims=False)

        return chunk(0), [chunk(m).astype(BF16) for m in range(1, pairs)]

    def col_sum(out, leaving):
        for m, part in enumerate(leaving):
            out = out + swap(part, "col", col_count, 2 * m + 2).astype(F32)
        return out

    def near_of(x_near):
        return pl.pallas_call(
            lambda *refs: near_kernel(clusters, exc, *refs),
            in_specs=[SMEM, SMEM, VMEM, VMEM],
            out_specs=VMEM,
            out_shape=jax.ShapeDtypeStruct((clusters, exc, panels), F32),
            compiler_params=params(others),
            cost_estimate=pl.CostEstimate(flops=1024, bytes_accessed=1024, transcendentals=0),
            name="near",
        )(near_rows, near_cols, x_near, near_blocks).reshape(span, panels)

    def rows_perm(distance):
        return [
            (r * col_count + c, (r ^ (distance + c % 2)) * col_count + c)
            for r in range(row_count)
            for c in range(col_count)
        ]

    whole = swap(x, "row", row_count, 1)
    got = [lax.ppermute(x, ("row", "col"), rows_perm(d)) for d in range(2, row_count, 2)]

    def local():
        send, mask, lanes = pl.pallas_call(
            lambda *refs: mirror_kernel(clusters, exc, rank, others, *refs),
            in_specs=[ANY] * 5,
            out_specs=[VMEM] * 3,
            out_shape=[
                shares(others)[0],
                jax.ShapeDtypeStruct((others * span, entries * rank), BF16),
                jax.ShapeDtypeStruct((8, entries * rank), jnp.int32),
            ],
            scratch_shapes=[
                pltpu.SMEM(far_rows.shape, jnp.int32),
                pltpu.SMEM(far_cols.shape, jnp.int32),
                pltpu.VMEM(x.shape, BF16),
                pltpu.VMEM(u.shape, BF16),
                pltpu.VMEM(v.shape, BF16),
                pltpu.SemaphoreType.DMA((5,)),
            ],
            compiler_params=params(others),
            cost_estimate=pl.CostEstimate(flops=1024, bytes_accessed=1024, transcendentals=0),
            name="mirror",
        )(far_rows, far_cols, x, u, v)
        keep = pl.pallas_call(
            lambda *refs: kept_kernel(clusters, exc, others, *refs),
            in_specs=[VMEM] * 2,
            out_specs=VMEM,
            out_shape=shares(others)[1],
            compiler_params=params(others),
            cost_estimate=pl.CostEstimate(flops=1024, bytes_accessed=1024, transcendentals=0),
            name="kept",
        )(mask, v)
        kinds = [F32] + [BF16] * (pairs - 1)
        one, far, *leaving = pl.pallas_call(
            lambda *refs: pair_kernel(span, *refs),
            in_specs=[VMEM] * 2,
            out_specs=[VMEM] * (2 * pairs),
            out_shape=[
                jax.ShapeDtypeStruct((rows * span, width), kind) for kind in kinds for rows in (1, others - 1)
            ],
            compiler_params=params(others),
            cost_estimate=pl.CostEstimate(flops=1024, bytes_accessed=1024, transcendentals=0),
            name="pair",
        )(keep, swap(send, "col", col_count, 1))
        one_leaving, leaving = leaving[::2], leaving[1::2]
        *leaving, x_near = lax.optimization_barrier((*leaving, charges))
        near = near_of(x_near)
        far = col_sum(far, leaving).astype(BF16)
        return (one, one_leaving), [far[i * span : (i + 1) * span] for i in range(others - 1)], near, lanes

    (one, one_leaving), far, near, lanes = stage(local)
    from_rows = [swap(part, "row", row_count, i + 2) for i, part in enumerate(far)]
    *got, lanes = lax.optimization_barrier((*got, lanes))
    one_parts = [swap(part, "col", col_count, 2 * m + 2) for m, part in enumerate(one_leaving)]
    got, one_parts, whole = lax.optimization_barrier((got, one_parts, whole))

    def forward():
        other = [swap(piece, "col", col_count, 1) for piece in got]
        early, *fetched = pl.pallas_call(
            lambda *refs: early_kernel(clusters, exc, 1 + len(got), *refs),
            in_specs=[VMEM] + [ANY] * (4 + len(got)),
            out_specs=[VMEM] * 4,
            out_shape=[
                jax.ShapeDtypeStruct((exc, entries * rank), F32),
                jax.ShapeDtypeStruct(v.shape, BF16),
                jax.ShapeDtypeStruct(u.shape, BF16),
                jax.ShapeDtypeStruct(near.shape, F32),
            ],
            scratch_shapes=[
                pltpu.VMEM(((1 + len(got)) * span, panels), BF16),
                pltpu.SemaphoreType.DMA((4 + len(got),)),
            ],
            compiler_params=params(others),
            cost_estimate=pl.CostEstimate(flops=1024, bytes_accessed=1024, transcendentals=0),
            name="early",
        )(lanes, v, u, near, whole, *got)
        send, keep = pl.pallas_call(
            lambda *refs: forward_kernel(clusters, exc, *refs),
            in_specs=[VMEM] * (5 + len(other)),
            out_specs=[VMEM] * 2,
            out_shape=shares(1),
            compiler_params=params(others),
            cost_estimate=pl.CostEstimate(flops=1024, bytes_accessed=1024, transcendentals=0),
            name="forward",
        )(lanes, early, *fetched, *other)
        joined = sum([part.astype(F32) for part in one_parts], one).astype(BF16)
        return col_sum(*chunks(pair_sum(send, keep))) + swap(joined, "row", row_count, 1).astype(F32)

    total = stage(forward)
    for term in from_rows:
        total = total + term.astype(F32)
    return total.reshape(clusters, exc, width)


def solution(mesh):
    placed = (
        P(("parts", "row"), None, None),
        P(("parts", "row", "col"), None, None),
        P(("parts", "row", "col")),
        P(("parts", "row", "col")),
        P(("parts", "row", "col"), None, None),
        P(("parts", "row", "col"), None, None),
        P(("parts", "row", "col")),
        P(("parts", "row", "col")),
    )
    return jax.shard_map(
        body,
        mesh=mesh,
        in_specs=placed,
        out_specs=P(("parts", "row"), None, "col"),
        check_vma=False,
    )
```

```python
import jax
import jax.numpy as jnp
from jax import lax
from jax.experimental import pallas as pl
from jax.experimental.pallas import tpu as pltpu
from jax.sharding import PartitionSpec as P

F32 = jnp.float32
BF16 = jnp.bfloat16
SMEM = pl.BlockSpec(memory_space=pltpu.SMEM)
ANY = pl.BlockSpec(memory_space=pltpu.HBM)
VMEM = pl.BlockSpec(memory_space=pltpu.VMEM)


def dot(a, b):
    return jnp.dot(a, b, preferred_element_type=F32)


def dot_t(a, b):
    return lax.dot_general(a, b, (((1,), (1,)), ((), ())), preferred_element_type=F32)


def params(others):
    return pltpu.CompilerParams(vmem_limit_bytes=(12 if others <= 4 else 48) * 1024 * 1024)


def each(count, step):
    if count <= 4:
        for i in range(count):
            step(i)
    else:
        lax.fori_loop(0, count, lambda i, c: (step(i), c)[1], 0)


def lane_ids(ids_ref, rank):
    count = ids_ref.shape[0]
    lane = lax.broadcasted_iota(jnp.int32, (1, count * rank), 1) // rank
    out = jnp.full((1, count * rank), -1, jnp.int32)
    for b in range(count):
        out = jnp.where(lane == b, ids_ref[b], out)
    return out


def split_columns(half, keep_ref, send_ref, rows, product):
    width = keep_ref.shape[2]
    for q in range(keep_ref.shape[0]):
        for side in range(2):
            at = (2 * q + side) * width
            part = product(slice(at, at + width))

            @pl.when(half == side)
            def _():
                keep_ref[q, rows, :] = part

            @pl.when(half != side)
            def _():
                send_ref[q, rows, :] = part.astype(BF16)


def side_columns(half, out_ref, rows, product):
    width = out_ref.shape[2]
    for side in range(2):

        @pl.when(half == side)
        def _():
            for q in range(out_ref.shape[0]):
                at = (2 * q + side) * width
                out_ref[q, rows, :] = product(slice(at, at + width)).astype(out_ref.dtype)


def batches(count, span):
    size = span * (count if count <= 4 else 1)

    def rows_of(step):
        return pl.ds(step * size if isinstance(step, int) else pl.multiple_of(step * size, size), size)

    return size // span, count * span // size, rows_of


def mirror_kernel(
    clusters, exc, rank, others, rows_hbm, cols_hbm, x_hbm, u_hbm, v_hbm,
    send_ref, mask_ref, lanes_ref,
    rows_ref, cols_ref, x_ref, u_ref, v_ref, sems,
):
    copies = [
        pltpu.make_async_copy(src, dst, sems.at[i])
        for i, (src, dst) in enumerate(
            [(u_hbm, u_ref), (x_hbm, x_ref), (rows_hbm, rows_ref), (cols_hbm, cols_ref), (v_hbm, v_ref)]
        )
    ]
    for copy in copies:
        copy.start()
    group = lax.axis_index("row")
    half = lax.rem(lax.axis_index("col"), 2)
    copies[2].wait()
    copies[3].wait()
    row_lane = lane_ids(rows_ref, rank)
    col_lane = lane_ids(cols_ref, rank)
    lanes_ref[0:1, :] = row_lane
    lanes_ref[1:2, :] = col_lane
    copies[0].wait()
    copies[1].wait()
    every = dot_t(x_ref[...], u_ref[...])
    coef = jnp.zeros((exc, every.shape[1]), F32)
    for c in range(clusters):
        coef += jnp.where(row_lane == group * clusters + c, every[c * exc : (c + 1) * exc], 0.0)
    coef = coef.astype(BF16).astype(F32)
    copies[4].wait()
    batch, steps, rows_of = batches(others, clusters * exc)

    def one(step):
        masked = []
        for i in range(batch):
            first = (group ^ (step * batch + i + 1)) * clusters
            masked += [jnp.where(col_lane == first + c, coef, 0.0) for c in range(clusters)]
        rows = rows_of(step)
        mask_ref[rows, :] = jnp.concatenate(masked, axis=0).astype(BF16)
        side_columns(1 - half, send_ref, rows, lambda cols: dot(mask_ref[rows, :], v_ref[:, cols]))

    each(steps, one)


def kept_kernel(clusters, exc, others, mask_ref, v_ref, keep_ref):
    half = lax.rem(lax.axis_index("col"), 2)
    _, steps, rows_of = batches(others, clusters * exc)

    def one(step):
        rows = rows_of(step)
        side_columns(half, keep_ref, rows, lambda cols: dot(mask_ref[rows, :], v_ref[:, cols]))

    each(steps, one)


def pair_kernel(split, keep_ref, recv_ref, *out_refs):
    mine = lax.axis_index("col") // 2
    for m in range(keep_ref.shape[0]):
        total = keep_ref[mine ^ m] + recv_ref[mine ^ m].astype(F32)
        out_refs[2 * m][...] = total[:split].astype(out_refs[2 * m].dtype)
        out_refs[2 * m + 1][...] = total[split:].astype(out_refs[2 * m + 1].dtype)


def near_kernel(clusters, exc, rows_ref, cols_ref, x_ref, n_ref, out_ref):
    first = lax.axis_index("row") * clusters
    out_ref[...] = jnp.zeros_like(out_ref)
    for b in range(n_ref.shape[0]):
        row = rows_ref[b] - first
        col = cols_ref[b] - first
        weight = jnp.where(row == col, 0.5, 1.0).astype(F32)
        out_ref[row] += weight * dot_t(x_ref[col], n_ref[b])
        out_ref[col] += weight * dot(x_ref[row], n_ref[b])


def coef_of(clusters, exc, aways, lanes_ref, v_ref, pieces):
    group = lax.axis_index("row")
    col_lane = lanes_ref[1:2, :]
    coef = jnp.zeros((exc, v_ref.shape[0]), F32)
    batch = len(pieces) if len(pieces) <= 4 else 1
    for n in range(0, len(pieces), batch):
        every = dot_t(jnp.concatenate(pieces[n : n + batch], axis=0), v_ref[...])
        for i in range(batch):
            first = (group ^ aways[n + i]) * clusters
            for c in range(clusters):
                at = (i * clusters + c) * exc
                coef += jnp.where(col_lane == first + c, every[at : at + exc], 0.0)
    return coef


def early_kernel(clusters, exc, count, lanes_ref, *refs):
    sources, (coef_ref, *targets) = refs[: 3 + count], refs[3 + count : 7 + count]
    pieces_ref, sems = refs[7 + count :]
    span = clusters * exc
    moves = [(sources[0], targets[0])]
    moves += [(src, pieces_ref.at[i * span : (i + 1) * span]) for i, src in enumerate(sources[3:])]
    moves += list(zip(sources[1:3], targets[1:]))
    copies = [pltpu.make_async_copy(src, dst, sems.at[i]) for i, (src, dst) in enumerate(moves)]
    for copy in copies:
        copy.start()
    half = lax.rem(lax.axis_index("col"), 2)
    for copy in copies[: 1 + count]:
        copy.wait()
    pieces = [pieces_ref[i * span : (i + 1) * span] for i in range(count)]
    aways = [1] + [2 * t + half for t in range(1, count)]
    coef_ref[...] = coef_of(clusters, exc, aways, lanes_ref, targets[0], pieces)
    for copy in copies[1 + count :]:
        copy.wait()


def forward_kernel(clusters, exc, lanes_ref, early_ref, v_ref, u_ref, near_ref, *refs):
    send_ref, keep_ref = refs[-2:]
    group = lax.axis_index("row")
    half = lax.rem(lax.axis_index("col"), 2)
    pieces = [ref[...] for ref in refs[:-2]]
    aways = [2 * t + 3 - half for t in range(len(pieces))]
    coef = early_ref[...] + coef_of(clusters, exc, aways, lanes_ref, v_ref, pieces)
    coef = coef.astype(BF16).astype(F32)
    row_lane = lanes_ref[0:1, :]
    masked = jnp.concatenate(
        [jnp.where(row_lane == group * clusters + c, coef, 0.0) for c in range(clusters)], axis=0
    ).astype(BF16)
    rows = slice(None)
    split_columns(
        half, keep_ref, send_ref, rows, lambda cols: dot(masked, u_ref[:, cols]) + near_ref[:, cols]
    )


def swap(value, axis, size, step):
    return lax.ppermute(value, axis, [(i, i ^ step) for i in range(size)])


def stage(work):
    shapes = jax.eval_shape(work)
    inside = lax.axis_index("row") < lax.axis_size("row")
    return lax.cond(inside, work, lambda: jax.tree.map(lambda a: jnp.zeros(a.shape, a.dtype), shapes))


def body(charges, near_blocks, near_rows, near_cols, far_u, far_v, far_rows, far_cols):
    clusters, exc, panels = charges.shape
    entries, rank, _ = far_u.shape
    row_count = lax.axis_size("row")
    col_count = lax.axis_size("col")
    others = row_count - 1
    pairs = col_count // 2
    width = panels // col_count
    span = clusters * exc
    place = lax.axis_index("col")
    x = charges.reshape(span, panels)
    u = far_u.reshape(entries * rank, panels)
    v = far_v.reshape(entries * rank, panels)

    def shares(count):
        return [
            jax.ShapeDtypeStruct((pairs, count * span, width), BF16),
            jax.ShapeDtypeStruct((pairs, count * span, width), F32),
        ]

    def pair_sum(send, keep):
        return keep + swap(send, "col", col_count, 1).astype(F32)

    def chunks(total):
        def chunk(m):
            return lax.dynamic_index_in_dim(total, place // 2 ^ m, 0, keepdims=False)

        return chunk(0), [chunk(m).astype(BF16) for m in range(1, pairs)]

    def col_sum(out, leaving):
        for m, part in enumerate(leaving):
            out = out + swap(part, "col", col_count, 2 * m + 2).astype(F32)
        return out

    def near_of(x_near):
        return pl.pallas_call(
            lambda *refs: near_kernel(clusters, exc, *refs),
            in_specs=[SMEM, SMEM, VMEM, VMEM],
            out_specs=VMEM,
            out_shape=jax.ShapeDtypeStruct((clusters, exc, panels), F32),
            compiler_params=params(others),
            cost_estimate=pl.CostEstimate(flops=1024, bytes_accessed=1024, transcendentals=0),
            name="near",
        )(near_rows, near_cols, x_near, near_blocks).reshape(span, panels)

    def rows_perm(distance):
        return [
            (r * col_count + c, (r ^ (distance + c % 2)) * col_count + c)
            for r in range(row_count)
            for c in range(col_count)
        ]

    whole = swap(x, "row", row_count, 1)
    got = [lax.ppermute(x, ("row", "col"), rows_perm(d)) for d in range(2, row_count, 2)]

    def local():
        send, mask, lanes = pl.pallas_call(
            lambda *refs: mirror_kernel(clusters, exc, rank, others, *refs),
            in_specs=[ANY] * 5,
            out_specs=[VMEM] * 3,
            out_shape=[
                shares(others)[0],
                jax.ShapeDtypeStruct((others * span, entries * rank), BF16),
                jax.ShapeDtypeStruct((8, entries * rank), jnp.int32),
            ],
            scratch_shapes=[
                pltpu.SMEM(far_rows.shape, jnp.int32),
                pltpu.SMEM(far_cols.shape, jnp.int32),
                pltpu.VMEM(x.shape, BF16),
                pltpu.VMEM(u.shape, BF16),
                pltpu.VMEM(v.shape, BF16),
                pltpu.SemaphoreType.DMA((5,)),
            ],
            compiler_params=params(others),
            cost_estimate=pl.CostEstimate(flops=1024, bytes_accessed=1024, transcendentals=0),
            name="mirror",
        )(far_rows, far_cols, x, u, v)
        keep = pl.pallas_call(
            lambda *refs: kept_kernel(clusters, exc, others, *refs),
            in_specs=[VMEM] * 2,
            out_specs=VMEM,
            out_shape=shares(others)[1],
            compiler_params=params(others),
            cost_estimate=pl.CostEstimate(flops=1024, bytes_accessed=1024, transcendentals=0),
            name="kept",
        )(mask, v)
        kinds = [F32] + [BF16] * (pairs - 1)
        one, far, *leaving = pl.pallas_call(
            lambda *refs: pair_kernel(span, *refs),
            in_specs=[VMEM] * 2,
            out_specs=[VMEM] * (2 * pairs),
            out_shape=[
                jax.ShapeDtypeStruct((rows * span, width), kind) for kind in kinds for rows in (1, others - 1)
            ],
            compiler_params=params(others),
            cost_estimate=pl.CostEstimate(flops=1024, bytes_accessed=1024, transcendentals=0),
            name="pair",
        )(keep, swap(send, "col", col_count, 1))
        one_leaving, leaving = leaving[::2], leaving[1::2]
        *leaving, x_near = lax.optimization_barrier((*leaving, charges))
        near = near_of(x_near)
        far = col_sum(far, leaving).astype(BF16)
        return (one, one_leaving), [far[i * span : (i + 1) * span] for i in range(others - 1)], near, lanes

    (one, one_leaving), far, near, lanes = stage(local)
    from_rows = [swap(part, "row", row_count, i + 2) for i, part in enumerate(far)]
    *got, lanes = lax.optimization_barrier((*got, lanes))
    whole, *got = lax.optimization_barrier((whole, *got))

    def forward():
        other = [swap(piece, "col", col_count, 1) for piece in got]
        early, *fetched = pl.pallas_call(
            lambda *refs: early_kernel(clusters, exc, 1 + len(got), *refs),
            in_specs=[VMEM] + [ANY] * (4 + len(got)),
            out_specs=[VMEM] * 4,
            out_shape=[
                jax.ShapeDtypeStruct((exc, entries * rank), F32),
                jax.ShapeDtypeStruct(v.shape, BF16),
                jax.ShapeDtypeStruct(u.shape, BF16),
                jax.ShapeDtypeStruct(near.shape, F32),
            ],
            scratch_shapes=[
                pltpu.VMEM(((1 + len(got)) * span, panels), BF16),
                pltpu.SemaphoreType.DMA((4 + len(got),)),
            ],
            compiler_params=params(others),
            cost_estimate=pl.CostEstimate(flops=1024, bytes_accessed=1024, transcendentals=0),
            name="early",
        )(lanes, v, u, near, whole, *got)
        send, keep = pl.pallas_call(
            lambda *refs: forward_kernel(clusters, exc, *refs),
            in_specs=[VMEM] * (5 + len(other)),
            out_specs=[VMEM] * 2,
            out_shape=shares(1),
            compiler_params=params(others),
            cost_estimate=pl.CostEstimate(flops=1024, bytes_accessed=1024, transcendentals=0),
            name="forward",
        )(lanes, early, *fetched, *other)
        joined = col_sum(one, one_leaving).astype(BF16)
        return col_sum(*chunks(pair_sum(send, keep))) + swap(joined, "row", row_count, 1).astype(F32)

    total = stage(forward)
    for term in from_rows:
        total = total + term.astype(F32)
    return total.reshape(clusters, exc, width)


def solution(mesh):
    placed = (
        P(("parts", "row"), None, None),
        P(("parts", "row", "col"), None, None),
        P(("parts", "row", "col")),
        P(("parts", "row", "col")),
        P(("parts", "row", "col"), None, None),
        P(("parts", "row", "col"), None, None),
        P(("parts", "row", "col")),
        P(("parts", "row", "col")),
    )
    return jax.shard_map(
        body,
        mesh=mesh,
        in_specs=placed,
        out_specs=P(("parts", "row"), None, "col"),
        check_vma=False,
    )
```

```python
import jax
import jax.numpy as jnp
from jax import lax
from jax.experimental import pallas as pl
from jax.experimental.pallas import tpu as pltpu
from jax.sharding import PartitionSpec as P

F32 = jnp.float32
BF16 = jnp.bfloat16
SMEM = pl.BlockSpec(memory_space=pltpu.SMEM)
ANY = pl.BlockSpec(memory_space=pltpu.HBM)
VMEM = pl.BlockSpec(memory_space=pltpu.VMEM)


def dot(a, b):
    return jnp.dot(a, b, preferred_element_type=F32)


def dot_t(a, b):
    return lax.dot_general(a, b, (((1,), (1,)), ((), ())), preferred_element_type=F32)


def params(others):
    return pltpu.CompilerParams(vmem_limit_bytes=(12 if others <= 4 else 48) * 1024 * 1024)


def each(count, step):
    if count <= 4:
        for i in range(count):
            step(i)
    else:
        lax.fori_loop(0, count, lambda i, c: (step(i), c)[1], 0)


def lane_ids(ids_ref, rank):
    count = ids_ref.shape[0]
    lane = lax.broadcasted_iota(jnp.int32, (1, count * rank), 1) // rank
    out = jnp.full((1, count * rank), -1, jnp.int32)
    for b in range(count):
        out = jnp.where(lane == b, ids_ref[b], out)
    return out


def split_columns(half, keep_ref, send_ref, rows, product):
    width = keep_ref.shape[2]
    for q in range(keep_ref.shape[0]):
        for side in range(2):
            at = (2 * q + side) * width
            part = product(slice(at, at + width))

            @pl.when(half == side)
            def _():
                keep_ref[q, rows, :] = part

            @pl.when(half != side)
            def _():
                send_ref[q, rows, :] = part.astype(BF16)


def side_columns(half, out_ref, rows, product):
    width = out_ref.shape[2]
    for side in range(2):

        @pl.when(half == side)
        def _():
            for q in range(out_ref.shape[0]):
                at = (2 * q + side) * width
                out_ref[q, rows, :] = product(slice(at, at + width)).astype(out_ref.dtype)


def batches(count, span):
    size = span * (count if count <= 4 else 1)

    def rows_of(step):
        return pl.ds(step * size if isinstance(step, int) else pl.multiple_of(step * size, size), size)

    return size // span, count * span // size, rows_of


def mirror_kernel(
    clusters, exc, rank, others, rows_hbm, cols_hbm, x_hbm, u_hbm, v_hbm,
    send_ref, mask_ref, lanes_ref,
    rows_ref, cols_ref, x_ref, u_ref, v_ref, sems,
):
    copies = [
        pltpu.make_async_copy(src, dst, sems.at[i])
        for i, (src, dst) in enumerate(
            [(u_hbm, u_ref), (x_hbm, x_ref), (rows_hbm, rows_ref), (cols_hbm, cols_ref), (v_hbm, v_ref)]
        )
    ]
    for copy in copies:
        copy.start()
    group = lax.axis_index("row")
    half = lax.rem(lax.axis_index("col"), 2)
    copies[2].wait()
    copies[3].wait()
    row_lane = lane_ids(rows_ref, rank)
    col_lane = lane_ids(cols_ref, rank)
    lanes_ref[0:1, :] = row_lane
    lanes_ref[1:2, :] = col_lane
    copies[0].wait()
    copies[1].wait()
    every = dot_t(x_ref[...], u_ref[...])
    coef = jnp.zeros((exc, every.shape[1]), F32)
    for c in range(clusters):
        coef += jnp.where(row_lane == group * clusters + c, every[c * exc : (c + 1) * exc], 0.0)
    coef = coef.astype(BF16).astype(F32)
    copies[4].wait()
    batch, steps, rows_of = batches(others, clusters * exc)

    def one(step):
        masked = []
        for i in range(batch):
            first = (group ^ (step * batch + i + 1)) * clusters
            masked += [jnp.where(col_lane == first + c, coef, 0.0) for c in range(clusters)]
        rows = rows_of(step)
        mask_ref[rows, :] = jnp.concatenate(masked, axis=0).astype(BF16)
        side_columns(1 - half, send_ref, rows, lambda cols: dot(mask_ref[rows, :], v_ref[:, cols]))

    each(steps, one)


def kept_kernel(clusters, exc, others, mask_ref, v_ref, keep_ref):
    half = lax.rem(lax.axis_index("col"), 2)
    _, steps, rows_of = batches(others, clusters * exc)

    def one(step):
        rows = rows_of(step)
        side_columns(half, keep_ref, rows, lambda cols: dot(mask_ref[rows, :], v_ref[:, cols]))

    each(steps, one)


def pair_kernel(split, keep_ref, recv_ref, *out_refs):
    mine = lax.axis_index("col") // 2
    for m in range(keep_ref.shape[0]):
        total = keep_ref[mine ^ m] + recv_ref[mine ^ m].astype(F32)
        out_refs[2 * m][...] = total[:split].astype(out_refs[2 * m].dtype)
        out_refs[2 * m + 1][...] = total[split:].astype(out_refs[2 * m + 1].dtype)


def near_kernel(clusters, exc, rows_ref, cols_ref, x_ref, n_ref, out_ref):
    first = lax.axis_index("row") * clusters
    out_ref[...] = jnp.zeros_like(out_ref)
    for b in range(n_ref.shape[0]):
        row = rows_ref[b] - first
        col = cols_ref[b] - first
        weight = jnp.where(row == col, 0.5, 1.0).astype(F32)
        out_ref[row] += weight * dot_t(x_ref[col], n_ref[b])
        out_ref[col] += weight * dot(x_ref[row], n_ref[b])


def coef_of(clusters, exc, aways, lanes_ref, v_ref, pieces):
    group = lax.axis_index("row")
    col_lane = lanes_ref[1:2, :]
    coef = jnp.zeros((exc, v_ref.shape[0]), F32)
    batch = len(pieces) if len(pieces) <= 4 else 1
    for n in range(0, len(pieces), batch):
        every = dot_t(jnp.concatenate(pieces[n : n + batch], axis=0), v_ref[...])
        for i in range(batch):
            first = (group ^ aways[n + i]) * clusters
            for c in range(clusters):
                at = (i * clusters + c) * exc
                coef += jnp.where(col_lane == first + c, every[at : at + exc], 0.0)
    return coef


def early_kernel(clusters, exc, count, lanes_ref, *refs):
    sources, (coef_ref, *targets) = refs[: 3 + count], refs[3 + count : 7 + count]
    pieces_ref, sems = refs[7 + count :]
    span = clusters * exc
    moves = [(sources[0], targets[0])]
    moves += [(src, pieces_ref.at[i * span : (i + 1) * span]) for i, src in enumerate(sources[3:])]
    moves += list(zip(sources[1:3], targets[1:]))
    copies = [pltpu.make_async_copy(src, dst, sems.at[i]) for i, (src, dst) in enumerate(moves)]
    for copy in copies:
        copy.start()
    half = lax.rem(lax.axis_index("col"), 2)
    for copy in copies[: 1 + count]:
        copy.wait()
    pieces = [pieces_ref[i * span : (i + 1) * span] for i in range(count)]
    aways = [1] + [2 * t + half for t in range(1, count)]
    coef_ref[...] = coef_of(clusters, exc, aways, lanes_ref, targets[0], pieces)
    for copy in copies[1 + count :]:
        copy.wait()


def forward_kernel(clusters, exc, lanes_ref, early_ref, v_ref, u_ref, near_ref, *refs):
    send_ref, keep_ref = refs[-2:]
    group = lax.axis_index("row")
    half = lax.rem(lax.axis_index("col"), 2)
    pieces = [ref[...] for ref in refs[:-2]]
    aways = [2 * t + 3 - half for t in range(len(pieces))]
    coef = early_ref[...] + coef_of(clusters, exc, aways, lanes_ref, v_ref, pieces)
    coef = coef.astype(BF16).astype(F32)
    row_lane = lanes_ref[0:1, :]
    masked = jnp.concatenate(
        [jnp.where(row_lane == group * clusters + c, coef, 0.0) for c in range(clusters)], axis=0
    ).astype(BF16)
    rows = slice(None)
    split_columns(
        half, keep_ref, send_ref, rows, lambda cols: dot(masked, u_ref[:, cols]) + near_ref[:, cols]
    )


def swap(value, axis, size, step):
    return lax.ppermute(value, axis, [(i, i ^ step) for i in range(size)])


def stage(work):
    shapes = jax.eval_shape(work)
    inside = lax.axis_index("row") < lax.axis_size("row")
    return lax.cond(inside, work, lambda: jax.tree.map(lambda a: jnp.zeros(a.shape, a.dtype), shapes))


def body(charges, near_blocks, near_rows, near_cols, far_u, far_v, far_rows, far_cols):
    clusters, exc, panels = charges.shape
    entries, rank, _ = far_u.shape
    row_count = lax.axis_size("row")
    col_count = lax.axis_size("col")
    others = row_count - 1
    pairs = col_count // 2
    width = panels // col_count
    span = clusters * exc
    place = lax.axis_index("col")
    x = charges.reshape(span, panels)
    u = far_u.reshape(entries * rank, panels)
    v = far_v.reshape(entries * rank, panels)

    def shares(count):
        return [
            jax.ShapeDtypeStruct((pairs, count * span, width), BF16),
            jax.ShapeDtypeStruct((pairs, count * span, width), F32),
        ]

    def pair_sum(send, keep):
        return keep + swap(send, "col", col_count, 1).astype(F32)

    def chunks(total):
        def chunk(m):
            return lax.dynamic_index_in_dim(total, place // 2 ^ m, 0, keepdims=False)

        return chunk(0), [chunk(m).astype(BF16) for m in range(1, pairs)]

    def col_sum(out, leaving):
        for m, part in enumerate(leaving):
            out = out + swap(part, "col", col_count, 2 * m + 2).astype(F32)
        return out

    def near_of(x_near):
        return pl.pallas_call(
            lambda *refs: near_kernel(clusters, exc, *refs),
            in_specs=[SMEM, SMEM, VMEM, VMEM],
            out_specs=VMEM,
            out_shape=jax.ShapeDtypeStruct((clusters, exc, panels), F32),
            compiler_params=params(others),
            cost_estimate=pl.CostEstimate(flops=1024, bytes_accessed=1024, transcendentals=0),
            name="near",
        )(near_rows, near_cols, x_near, near_blocks).reshape(span, panels)

    def rows_perm(distance):
        return [
            (r * col_count + c, (r ^ (distance + c % 2)) * col_count + c)
            for r in range(row_count)
            for c in range(col_count)
        ]

    whole = swap(x, "row", row_count, 1)
    got = [lax.ppermute(x, ("row", "col"), rows_perm(d)) for d in range(2, row_count, 2)]

    def local():
        send, mask, lanes = pl.pallas_call(
            lambda *refs: mirror_kernel(clusters, exc, rank, others, *refs),
            in_specs=[ANY] * 5,
            out_specs=[VMEM] * 3,
            out_shape=[
                shares(others)[0],
                jax.ShapeDtypeStruct((others * span, entries * rank), BF16),
                jax.ShapeDtypeStruct((8, entries * rank), jnp.int32),
            ],
            scratch_shapes=[
                pltpu.SMEM(far_rows.shape, jnp.int32),
                pltpu.SMEM(far_cols.shape, jnp.int32),
                pltpu.VMEM(x.shape, BF16),
                pltpu.VMEM(u.shape, BF16),
                pltpu.VMEM(v.shape, BF16),
                pltpu.SemaphoreType.DMA((5,)),
            ],
            compiler_params=params(others),
            cost_estimate=pl.CostEstimate(flops=1024, bytes_accessed=1024, transcendentals=0),
            name="mirror",
        )(far_rows, far_cols, x, u, v)
        keep = pl.pallas_call(
            lambda *refs: kept_kernel(clusters, exc, others, *refs),
            in_specs=[VMEM] * 2,
            out_specs=VMEM,
            out_shape=shares(others)[1],
            compiler_params=params(others),
            cost_estimate=pl.CostEstimate(flops=1024, bytes_accessed=1024, transcendentals=0),
            name="kept",
        )(mask, v)
        kinds = [F32] + [BF16] * (pairs - 1)
        one, far, *leaving = pl.pallas_call(
            lambda *refs: pair_kernel(span, *refs),
            in_specs=[VMEM] * 2,
            out_specs=[VMEM] * (2 * pairs),
            out_shape=[
                jax.ShapeDtypeStruct((rows * span, width), kind) for kind in kinds for rows in (1, others - 1)
            ],
            compiler_params=params(others),
            cost_estimate=pl.CostEstimate(flops=1024, bytes_accessed=1024, transcendentals=0),
            name="pair",
        )(keep, swap(send, "col", col_count, 1))
        one_leaving, leaving = leaving[::2], leaving[1::2]
        *leaving, x_near = lax.optimization_barrier((*leaving, charges))
        near = near_of(x_near)
        far = col_sum(far, leaving).astype(BF16)
        return (one, one_leaving), [far[i * span : (i + 1) * span] for i in range(others - 1)], near, lanes

    (one, one_leaving), far, near, lanes = stage(local)
    from_rows = [swap(part, "row", row_count, i + 2) for i, part in enumerate(far)]
    *got, lanes = lax.optimization_barrier((*got, lanes))
    whole, *got = lax.optimization_barrier((whole, *got))

    def forward():
        other = [swap(piece, "col", col_count, 1) for piece in got]
        early, *fetched = pl.pallas_call(
            lambda *refs: early_kernel(clusters, exc, 1 + len(got), *refs),
            in_specs=[VMEM] + [ANY] * (4 + len(got)),
            out_specs=[VMEM] * 4,
            out_shape=[
                jax.ShapeDtypeStruct((exc, entries * rank), F32),
                jax.ShapeDtypeStruct(v.shape, BF16),
                jax.ShapeDtypeStruct(u.shape, BF16),
                jax.ShapeDtypeStruct(near.shape, F32),
            ],
            scratch_shapes=[
                pltpu.VMEM(((1 + len(got)) * span, panels), BF16),
                pltpu.SemaphoreType.DMA((4 + len(got),)),
            ],
            compiler_params=params(others),
            cost_estimate=pl.CostEstimate(flops=1024, bytes_accessed=1024, transcendentals=0),
            name="early",
        )(lanes, v, u, near, whole, *got)
        send, keep = pl.pallas_call(
            lambda *refs: forward_kernel(clusters, exc, *refs),
            in_specs=[VMEM] * (5 + len(other)),
            out_specs=[VMEM] * 2,
            out_shape=shares(1),
            compiler_params=params(others),
            cost_estimate=pl.CostEstimate(flops=1024, bytes_accessed=1024, transcendentals=0),
            name="forward",
        )(lanes, early, *fetched, *other)
        send, mine = lax.optimization_barrier((send, one))
        joined = col_sum(mine, one_leaving).astype(BF16)
        send, joined = lax.optimization_barrier((send, joined))
        summed = lax.optimization_barrier(col_sum(*chunks(pair_sum(send, keep))))
        return summed + swap(joined, "row", row_count, 1).astype(F32)

    total = stage(forward)
    for term in from_rows:
        total = total + term.astype(F32)
    return total.reshape(clusters, exc, width)


def solution(mesh):
    placed = (
        P(("parts", "row"), None, None),
        P(("parts", "row", "col"), None, None),
        P(("parts", "row", "col")),
        P(("parts", "row", "col")),
        P(("parts", "row", "col"), None, None),
        P(("parts", "row", "col"), None, None),
        P(("parts", "row", "col")),
        P(("parts", "row", "col")),
    )
    return jax.shard_map(
        body,
        mesh=mesh,
        in_specs=placed,
        out_specs=P(("parts", "row"), None, "col"),
        check_vma=False,
    )
```

```python
import jax
import jax.numpy as jnp
from jax import lax
from jax.experimental import pallas as pl
from jax.experimental.pallas import tpu as pltpu
from jax.sharding import PartitionSpec as P

F32 = jnp.float32
BF16 = jnp.bfloat16
SMEM = pl.BlockSpec(memory_space=pltpu.SMEM)
ANY = pl.BlockSpec(memory_space=pltpu.HBM)
VMEM = pl.BlockSpec(memory_space=pltpu.VMEM)


def dot(a, b):
    return jnp.dot(a, b, preferred_element_type=F32)


def dot_t(a, b):
    return lax.dot_general(a, b, (((1,), (1,)), ((), ())), preferred_element_type=F32)


def params(others):
    return pltpu.CompilerParams(vmem_limit_bytes=(12 if others <= 4 else 48) * 1024 * 1024)


def each(count, step):
    if count <= 4:
        for i in range(count):
            step(i)
    else:
        lax.fori_loop(0, count, lambda i, c: (step(i), c)[1], 0)


def lane_ids(ids_ref, rank):
    count = ids_ref.shape[0]
    lane = lax.broadcasted_iota(jnp.int32, (1, count * rank), 1) // rank
    out = jnp.full((1, count * rank), -1, jnp.int32)
    for b in range(count):
        out = jnp.where(lane == b, ids_ref[b], out)
    return out


def split_columns(half, keep_ref, send_ref, rows, product):
    width = keep_ref.shape[2]
    for q in range(keep_ref.shape[0]):
        for side in range(2):
            at = (2 * q + side) * width
            part = product(slice(at, at + width))

            @pl.when(half == side)
            def _():
                keep_ref[q, rows, :] = part

            @pl.when(half != side)
            def _():
                send_ref[q, rows, :] = part.astype(BF16)


def side_columns(half, out_ref, rows, product):
    width = out_ref.shape[2]
    for side in range(2):

        @pl.when(half == side)
        def _():
            for q in range(out_ref.shape[0]):
                at = (2 * q + side) * width
                out_ref[q, rows, :] = product(slice(at, at + width)).astype(out_ref.dtype)


def batches(count, span):
    size = span * (count if count <= 4 else 1)

    def rows_of(step):
        return pl.ds(step * size if isinstance(step, int) else pl.multiple_of(step * size, size), size)

    return size // span, count * span // size, rows_of


def mirror_kernel(
    clusters, exc, rank, others, rows_hbm, cols_hbm, x_hbm, u_hbm, v_hbm,
    send_ref, mask_ref, lanes_ref,
    rows_ref, cols_ref, x_ref, u_ref, v_ref, sems,
):
    copies = [
        pltpu.make_async_copy(src, dst, sems.at[i])
        for i, (src, dst) in enumerate(
            [(u_hbm, u_ref), (x_hbm, x_ref), (rows_hbm, rows_ref), (cols_hbm, cols_ref), (v_hbm, v_ref)]
        )
    ]
    for copy in copies:
        copy.start()
    group = lax.axis_index("row")
    half = lax.rem(lax.axis_index("col"), 2)
    copies[2].wait()
    copies[3].wait()
    row_lane = lane_ids(rows_ref, rank)
    col_lane = lane_ids(cols_ref, rank)
    lanes_ref[0:1, :] = row_lane
    lanes_ref[1:2, :] = col_lane
    copies[0].wait()
    copies[1].wait()
    every = dot_t(x_ref[...], u_ref[...])
    coef = jnp.zeros((exc, every.shape[1]), F32)
    for c in range(clusters):
        coef += jnp.where(row_lane == group * clusters + c, every[c * exc : (c + 1) * exc], 0.0)
    coef = coef.astype(BF16).astype(F32)
    copies[4].wait()
    batch, steps, rows_of = batches(others, clusters * exc)

    def one(step):
        masked = []
        for i in range(batch):
            first = (group ^ (step * batch + i + 1)) * clusters
            masked += [jnp.where(col_lane == first + c, coef, 0.0) for c in range(clusters)]
        rows = rows_of(step)
        mask_ref[rows, :] = jnp.concatenate(masked, axis=0).astype(BF16)
        side_columns(1 - half, send_ref, rows, lambda cols: dot(mask_ref[rows, :], v_ref[:, cols]))

    each(steps, one)


def kept_kernel(clusters, exc, others, mask_ref, v_ref, keep_ref):
    half = lax.rem(lax.axis_index("col"), 2)
    _, steps, rows_of = batches(others, clusters * exc)

    def one(step):
        rows = rows_of(step)
        side_columns(half, keep_ref, rows, lambda cols: dot(mask_ref[rows, :], v_ref[:, cols]))

    each(steps, one)


def pair_kernel(split, keep_ref, recv_ref, *out_refs):
    mine = lax.axis_index("col") // 2
    for m in range(keep_ref.shape[0]):
        total = keep_ref[mine ^ m] + recv_ref[mine ^ m].astype(F32)
        out_refs[2 * m][...] = total[:split].astype(out_refs[2 * m].dtype)
        out_refs[2 * m + 1][...] = total[split:].astype(out_refs[2 * m + 1].dtype)


def near_kernel(clusters, exc, rows_ref, cols_ref, x_ref, n_ref, out_ref):
    first = lax.axis_index("row") * clusters
    out_ref[...] = jnp.zeros_like(out_ref)
    for b in range(n_ref.shape[0]):
        row = rows_ref[b] - first
        col = cols_ref[b] - first
        weight = jnp.where(row == col, 0.5, 1.0).astype(F32)
        out_ref[row] += weight * dot_t(x_ref[col], n_ref[b])
        out_ref[col] += weight * dot(x_ref[row], n_ref[b])


def coef_of(clusters, exc, aways, lanes_ref, v_ref, pieces):
    group = lax.axis_index("row")
    col_lane = lanes_ref[1:2, :]
    coef = jnp.zeros((exc, v_ref.shape[0]), F32)
    batch = len(pieces) if len(pieces) <= 4 else 1
    for n in range(0, len(pieces), batch):
        every = dot_t(jnp.concatenate(pieces[n : n + batch], axis=0), v_ref[...])
        for i in range(batch):
            first = (group ^ aways[n + i]) * clusters
            for c in range(clusters):
                at = (i * clusters + c) * exc
                coef += jnp.where(col_lane == first + c, every[at : at + exc], 0.0)
    return coef


def early_kernel(clusters, exc, count, lanes_ref, *refs):
    sources, (coef_ref, *targets) = refs[: 3 + count], refs[3 + count : 7 + count]
    pieces_ref, sems = refs[7 + count :]
    span = clusters * exc
    moves = [(sources[0], targets[0])]
    moves += [(src, pieces_ref.at[i * span : (i + 1) * span]) for i, src in enumerate(sources[3:])]
    moves += list(zip(sources[1:3], targets[1:]))
    copies = [pltpu.make_async_copy(src, dst, sems.at[i]) for i, (src, dst) in enumerate(moves)]
    for copy in copies:
        copy.start()
    half = lax.rem(lax.axis_index("col"), 2)
    for copy in copies[: 1 + count]:
        copy.wait()
    pieces = [pieces_ref[i * span : (i + 1) * span] for i in range(count)]
    aways = [1] + [2 * t + half for t in range(1, count)]
    coef_ref[...] = coef_of(clusters, exc, aways, lanes_ref, targets[0], pieces)
    for copy in copies[1 + count :]:
        copy.wait()


def forward_kernel(clusters, exc, lanes_ref, early_ref, v_ref, u_ref, near_ref, *refs):
    send_ref, keep_ref = refs[-2:]
    group = lax.axis_index("row")
    half = lax.rem(lax.axis_index("col"), 2)
    pieces = [ref[...] for ref in refs[:-2]]
    aways = [2 * t + 3 - half for t in range(len(pieces))]
    coef = early_ref[...] + coef_of(clusters, exc, aways, lanes_ref, v_ref, pieces)
    coef = coef.astype(BF16).astype(F32)
    row_lane = lanes_ref[0:1, :]
    masked = jnp.concatenate(
        [jnp.where(row_lane == group * clusters + c, coef, 0.0) for c in range(clusters)], axis=0
    ).astype(BF16)
    rows = slice(None)
    split_columns(
        half, keep_ref, send_ref, rows, lambda cols: dot(masked, u_ref[:, cols]) + near_ref[:, cols]
    )


def swap(value, axis, size, step):
    return lax.ppermute(value, axis, [(i, i ^ step) for i in range(size)])


def stage(work):
    shapes = jax.eval_shape(work)
    inside = lax.axis_index("row") < lax.axis_size("row")
    return lax.cond(inside, work, lambda: jax.tree.map(lambda a: jnp.zeros(a.shape, a.dtype), shapes))


def body(charges, near_blocks, near_rows, near_cols, far_u, far_v, far_rows, far_cols):
    clusters, exc, panels = charges.shape
    entries, rank, _ = far_u.shape
    row_count = lax.axis_size("row")
    col_count = lax.axis_size("col")
    others = row_count - 1
    pairs = col_count // 2
    width = panels // col_count
    span = clusters * exc
    place = lax.axis_index("col")
    x = charges.reshape(span, panels)
    u = far_u.reshape(entries * rank, panels)
    v = far_v.reshape(entries * rank, panels)

    def shares(count):
        return [
            jax.ShapeDtypeStruct((pairs, count * span, width), BF16),
            jax.ShapeDtypeStruct((pairs, count * span, width), F32),
        ]

    def pair_sum(send, keep):
        return keep + swap(send, "col", col_count, 1).astype(F32)

    def chunks(total):
        def chunk(m):
            return lax.dynamic_index_in_dim(total, place // 2 ^ m, 0, keepdims=False)

        return chunk(0), [chunk(m).astype(BF16) for m in range(1, pairs)]

    def col_sum(out, leaving):
        for m, part in enumerate(leaving):
            out = out + swap(part, "col", col_count, 2 * m + 2).astype(F32)
        return out

    def near_of(x_near):
        return pl.pallas_call(
            lambda *refs: near_kernel(clusters, exc, *refs),
            in_specs=[SMEM, SMEM, VMEM, VMEM],
            out_specs=VMEM,
            out_shape=jax.ShapeDtypeStruct((clusters, exc, panels), F32),
            compiler_params=params(others),
            cost_estimate=pl.CostEstimate(flops=1024, bytes_accessed=1024, transcendentals=0),
            name="near",
        )(near_rows, near_cols, x_near, near_blocks).reshape(span, panels)

    def rows_perm(distance):
        return [
            (r * col_count + c, (r ^ (distance + c % 2)) * col_count + c)
            for r in range(row_count)
            for c in range(col_count)
        ]

    whole = swap(x, "row", row_count, 1)
    got = [lax.ppermute(x, ("row", "col"), rows_perm(d)) for d in range(2, row_count, 2)]

    def local():
        send, mask, lanes = pl.pallas_call(
            lambda *refs: mirror_kernel(clusters, exc, rank, others, *refs),
            in_specs=[ANY] * 5,
            out_specs=[VMEM] * 3,
            out_shape=[
                shares(others)[0],
                jax.ShapeDtypeStruct((others * span, entries * rank), BF16),
                jax.ShapeDtypeStruct((8, entries * rank), jnp.int32),
            ],
            scratch_shapes=[
                pltpu.SMEM(far_rows.shape, jnp.int32),
                pltpu.SMEM(far_cols.shape, jnp.int32),
                pltpu.VMEM(x.shape, BF16),
                pltpu.VMEM(u.shape, BF16),
                pltpu.VMEM(v.shape, BF16),
                pltpu.SemaphoreType.DMA((5,)),
            ],
            compiler_params=params(others),
            cost_estimate=pl.CostEstimate(flops=1024, bytes_accessed=1024, transcendentals=0),
            name="mirror",
        )(far_rows, far_cols, x, u, v)
        keep = pl.pallas_call(
            lambda *refs: kept_kernel(clusters, exc, others, *refs),
            in_specs=[VMEM] * 2,
            out_specs=VMEM,
            out_shape=shares(others)[1],
            compiler_params=params(others),
            cost_estimate=pl.CostEstimate(flops=1024, bytes_accessed=1024, transcendentals=0),
            name="kept",
        )(mask, v)
        kinds = [F32] + [BF16] * (pairs - 1)
        one, far, *leaving = pl.pallas_call(
            lambda *refs: pair_kernel(span, *refs),
            in_specs=[VMEM] * 2,
            out_specs=[VMEM] * (2 * pairs),
            out_shape=[
                jax.ShapeDtypeStruct((rows * span, width), kind) for kind in kinds for rows in (1, others - 1)
            ],
            compiler_params=params(others),
            cost_estimate=pl.CostEstimate(flops=1024, bytes_accessed=1024, transcendentals=0),
            name="pair",
        )(keep, swap(send, "col", col_count, 1))
        one_leaving, leaving = leaving[::2], leaving[1::2]
        *leaving, x_near = lax.optimization_barrier((*leaving, charges))
        near = near_of(x_near)
        far = col_sum(far, leaving).astype(BF16)
        return (one, one_leaving), [far[i * span : (i + 1) * span] for i in range(others - 1)], near, lanes

    (one, one_leaving), far, near, lanes = stage(local)
    from_rows = [swap(part, "row", row_count, i + 2) for i, part in enumerate(far)]
    *got, lanes = lax.optimization_barrier((*got, lanes))
    whole, *got = lax.optimization_barrier((whole, *got))

    def forward():
        other = [swap(piece, "col", col_count, 1) for piece in got]
        early, *fetched = pl.pallas_call(
            lambda *refs: early_kernel(clusters, exc, 1 + len(got), *refs),
            in_specs=[VMEM] + [ANY] * (4 + len(got)),
            out_specs=[VMEM] * 4,
            out_shape=[
                jax.ShapeDtypeStruct((exc, entries * rank), F32),
                jax.ShapeDtypeStruct(v.shape, BF16),
                jax.ShapeDtypeStruct(u.shape, BF16),
                jax.ShapeDtypeStruct(near.shape, F32),
            ],
            scratch_shapes=[
                pltpu.VMEM(((1 + len(got)) * span, panels), BF16),
                pltpu.SemaphoreType.DMA((4 + len(got),)),
            ],
            compiler_params=params(others),
            cost_estimate=pl.CostEstimate(flops=1024, bytes_accessed=1024, transcendentals=0),
            name="early",
        )(lanes, v, u, near, whole, *got)
        send, keep = pl.pallas_call(
            lambda *refs: forward_kernel(clusters, exc, *refs),
            in_specs=[VMEM] * (5 + len(other)),
            out_specs=[VMEM] * 2,
            out_shape=shares(1),
            compiler_params=params(others),
            cost_estimate=pl.CostEstimate(flops=1024, bytes_accessed=1024, transcendentals=0),
            name="forward",
        )(lanes, early, *fetched, *other)
        joined = col_sum(one, one_leaving).astype(BF16)
        return col_sum(*chunks(pair_sum(send, keep))) + swap(joined, "row", row_count, 1).astype(F32)

    total = stage(forward)
    for term in from_rows[:-1]:
        total = total + term.astype(F32)
    total = lax.optimization_barrier(total) + from_rows[-1].astype(F32)
    return total.reshape(clusters, exc, width)


def solution(mesh):
    placed = (
        P(("parts", "row"), None, None),
        P(("parts", "row", "col"), None, None),
        P(("parts", "row", "col")),
        P(("parts", "row", "col")),
        P(("parts", "row", "col"), None, None),
        P(("parts", "row", "col"), None, None),
        P(("parts", "row", "col")),
        P(("parts", "row", "col")),
    )
    return jax.shard_map(
        body,
        mesh=mesh,
        in_specs=placed,
        out_specs=P(("parts", "row"), None, "col"),
        check_vma=False,
    )
```

```python
import jax
import jax.numpy as jnp
from jax import lax
from jax.experimental import pallas as pl
from jax.experimental.pallas import tpu as pltpu
from jax.sharding import PartitionSpec as P

F32 = jnp.float32
BF16 = jnp.bfloat16
SMEM = pl.BlockSpec(memory_space=pltpu.SMEM)
ANY = pl.BlockSpec(memory_space=pltpu.HBM)
VMEM = pl.BlockSpec(memory_space=pltpu.VMEM)


def dot(a, b):
    return jnp.dot(a, b, preferred_element_type=F32)


def dot_t(a, b):
    return lax.dot_general(a, b, (((1,), (1,)), ((), ())), preferred_element_type=F32)


def params(others):
    return pltpu.CompilerParams(vmem_limit_bytes=(12 if others <= 4 else 48) * 1024 * 1024)


def each(count, step):
    if count <= 4:
        for i in range(count):
            step(i)
    else:
        lax.fori_loop(0, count, lambda i, c: (step(i), c)[1], 0)


def lane_ids(ids_ref, rank):
    count = ids_ref.shape[0]
    lane = lax.broadcasted_iota(jnp.int32, (1, count * rank), 1) // rank
    out = jnp.full((1, count * rank), -1, jnp.int32)
    for b in range(count):
        out = jnp.where(lane == b, ids_ref[b], out)
    return out


def split_columns(half, keep_ref, send_ref, rows, product):
    width = keep_ref.shape[2]
    for q in range(keep_ref.shape[0]):
        for side in range(2):
            at = (2 * q + side) * width
            part = product(slice(at, at + width))

            @pl.when(half == side)
            def _():
                keep_ref[q, rows, :] = part

            @pl.when(half != side)
            def _():
                send_ref[q, rows, :] = part.astype(BF16)


def side_columns(half, out_ref, rows, product):
    width = out_ref.shape[2]
    for side in range(2):

        @pl.when(half == side)
        def _():
            for q in range(out_ref.shape[0]):
                at = (2 * q + side) * width
                out_ref[q, rows, :] = product(slice(at, at + width)).astype(out_ref.dtype)


def batches(count, span):
    size = span * (count if count <= 4 else 1)

    def rows_of(step):
        return pl.ds(step * size if isinstance(step, int) else pl.multiple_of(step * size, size), size)

    return size // span, count * span // size, rows_of


def mirror_kernel(
    clusters, exc, rank, others, rows_hbm, cols_hbm, x_hbm, u_hbm, v_hbm,
    send_ref, mask_ref, lanes_ref,
    rows_ref, cols_ref, x_ref, u_ref, v_ref, sems,
):
    copies = [
        pltpu.make_async_copy(src, dst, sems.at[i])
        for i, (src, dst) in enumerate(
            [(u_hbm, u_ref), (x_hbm, x_ref), (rows_hbm, rows_ref), (cols_hbm, cols_ref), (v_hbm, v_ref)]
        )
    ]
    for copy in copies:
        copy.start()
    group = lax.axis_index("row")
    half = lax.rem(lax.axis_index("col"), 2)
    copies[2].wait()
    copies[3].wait()
    row_lane = lane_ids(rows_ref, rank)
    col_lane = lane_ids(cols_ref, rank)
    lanes_ref[0:1, :] = row_lane
    lanes_ref[1:2, :] = col_lane
    copies[0].wait()
    copies[1].wait()
    every = dot_t(x_ref[...], u_ref[...])
    coef = jnp.zeros((exc, every.shape[1]), F32)
    for c in range(clusters):
        coef += jnp.where(row_lane == group * clusters + c, every[c * exc : (c + 1) * exc], 0.0)
    coef = coef.astype(BF16).astype(F32)
    copies[4].wait()
    batch, steps, rows_of = batches(others, clusters * exc)

    def one(step):
        masked = []
        for i in range(batch):
            first = (group ^ (step * batch + i + 1)) * clusters
            masked += [jnp.where(col_lane == first + c, coef, 0.0) for c in range(clusters)]
        rows = rows_of(step)
        mask_ref[rows, :] = jnp.concatenate(masked, axis=0).astype(BF16)
        side_columns(1 - half, send_ref, rows, lambda cols: dot(mask_ref[rows, :], v_ref[:, cols]))

    each(steps, one)


def kept_kernel(clusters, exc, others, mask_ref, v_ref, keep_ref):
    half = lax.rem(lax.axis_index("col"), 2)
    _, steps, rows_of = batches(others, clusters * exc)

    def one(step):
        rows = rows_of(step)
        side_columns(half, keep_ref, rows, lambda cols: dot(mask_ref[rows, :], v_ref[:, cols]))

    each(steps, one)


def pair_kernel(split, keep_ref, recv_ref, *out_refs):
    mine = lax.axis_index("col") // 2
    for m in range(keep_ref.shape[0]):
        total = keep_ref[mine ^ m] + recv_ref[mine ^ m].astype(F32)
        out_refs[2 * m][...] = total[:split].astype(out_refs[2 * m].dtype)
        out_refs[2 * m + 1][...] = total[split:].astype(out_refs[2 * m + 1].dtype)


def near_kernel(clusters, exc, rows_ref, cols_ref, x_ref, n_ref, out_ref):
    first = lax.axis_index("row") * clusters
    out_ref[...] = jnp.zeros_like(out_ref)
    for b in range(n_ref.shape[0]):
        row = rows_ref[b] - first
        col = cols_ref[b] - first
        weight = jnp.where(row == col, 0.5, 1.0).astype(F32)
        out_ref[row] += weight * dot_t(x_ref[col], n_ref[b])
        out_ref[col] += weight * dot(x_ref[row], n_ref[b])


def coef_of(clusters, exc, aways, lanes_ref, v_ref, pieces):
    group = lax.axis_index("row")
    col_lane = lanes_ref[1:2, :]
    coef = jnp.zeros((exc, v_ref.shape[0]), F32)
    batch = len(pieces) if len(pieces) <= 4 else 1
    for n in range(0, len(pieces), batch):
        every = dot_t(jnp.concatenate(pieces[n : n + batch], axis=0), v_ref[...])
        for i in range(batch):
            first = (group ^ aways[n + i]) * clusters
            for c in range(clusters):
                at = (i * clusters + c) * exc
                coef += jnp.where(col_lane == first + c, every[at : at + exc], 0.0)
    return coef


def early_kernel(clusters, exc, count, lanes_ref, *refs):
    sources, (coef_ref, *targets) = refs[: 4 + count], refs[4 + count : 9 + count]
    pieces_ref, sems = refs[9 + count :]
    span = clusters * exc
    moves = [(sources[0], targets[0])]
    moves += [(src, pieces_ref.at[i * span : (i + 1) * span]) for i, src in enumerate(sources[4:])]
    moves += list(zip(sources[1:4], targets[1:]))
    copies = [pltpu.make_async_copy(src, dst, sems.at[i]) for i, (src, dst) in enumerate(moves)]
    for copy in copies:
        copy.start()
    half = lax.rem(lax.axis_index("col"), 2)
    for copy in copies[: 1 + count]:
        copy.wait()
    pieces = [pieces_ref[i * span : (i + 1) * span] for i in range(count)]
    aways = [2 * t + half for t in range(1, count + 1)]
    coef_ref[...] = coef_of(clusters, exc, aways, lanes_ref, targets[0], pieces)
    for copy in copies[1 + count :]:
        copy.wait()


def forward_kernel(clusters, exc, lanes_ref, early_ref, v_ref, u_ref, near_ref, *refs):
    send_ref, keep_ref = refs[-2:]
    group = lax.axis_index("row")
    half = lax.rem(lax.axis_index("col"), 2)
    pieces = [ref[...] for ref in refs[:-2]]
    aways = [1] + [2 * t + 1 - half for t in range(1, len(pieces))]
    coef = early_ref[...] + coef_of(clusters, exc, aways, lanes_ref, v_ref, pieces)
    coef = coef.astype(BF16).astype(F32)
    row_lane = lanes_ref[0:1, :]
    masked = jnp.concatenate(
        [jnp.where(row_lane == group * clusters + c, coef, 0.0) for c in range(clusters)], axis=0
    ).astype(BF16)
    rows = slice(None)
    split_columns(
        half, keep_ref, send_ref, rows, lambda cols: dot(masked, u_ref[:, cols]) + near_ref[:, cols]
    )


def swap(value, axis, size, step):
    return lax.ppermute(value, axis, [(i, i ^ step) for i in range(size)])


def stage(work):
    shapes = jax.eval_shape(work)
    inside = lax.axis_index("row") < lax.axis_size("row")
    return lax.cond(inside, work, lambda: jax.tree.map(lambda a: jnp.zeros(a.shape, a.dtype), shapes))


def body(charges, near_blocks, near_rows, near_cols, far_u, far_v, far_rows, far_cols):
    clusters, exc, panels = charges.shape
    entries, rank, _ = far_u.shape
    row_count = lax.axis_size("row")
    col_count = lax.axis_size("col")
    others = row_count - 1
    pairs = col_count // 2
    width = panels // col_count
    span = clusters * exc
    place = lax.axis_index("col")
    x = charges.reshape(span, panels)
    u = far_u.reshape(entries * rank, panels)
    v = far_v.reshape(entries * rank, panels)

    def shares(count):
        return [
            jax.ShapeDtypeStruct((pairs, count * span, width), BF16),
            jax.ShapeDtypeStruct((pairs, count * span, width), F32),
        ]

    def pair_sum(send, keep):
        return keep + swap(send, "col", col_count, 1).astype(F32)

    def chunks(total):
        def chunk(m):
            return lax.dynamic_index_in_dim(total, place // 2 ^ m, 0, keepdims=False)

        return chunk(0), [chunk(m).astype(BF16) for m in range(1, pairs)]

    def col_sum(out, leaving):
        for m, part in enumerate(leaving):
            out = out + swap(part, "col", col_count, 2 * m + 2).astype(F32)
        return out

    def near_of(x_near):
        return pl.pallas_call(
            lambda *refs: near_kernel(clusters, exc, *refs),
            in_specs=[SMEM, SMEM, VMEM, VMEM],
            out_specs=VMEM,
            out_shape=jax.ShapeDtypeStruct((clusters, exc, panels), F32),
            compiler_params=params(others),
            cost_estimate=pl.CostEstimate(flops=1024, bytes_accessed=1024, transcendentals=0),
            name="near",
        )(near_rows, near_cols, x_near, near_blocks).reshape(span, panels)

    def rows_perm(distance):
        return [
            (r * col_count + c, (r ^ (distance + c % 2)) * col_count + c)
            for r in range(row_count)
            for c in range(col_count)
        ]

    whole = swap(x, "row", row_count, 1)
    got = [lax.ppermute(x, ("row", "col"), rows_perm(d)) for d in range(2, row_count, 2)]

    def local():
        send, mask, lanes = pl.pallas_call(
            lambda *refs: mirror_kernel(clusters, exc, rank, others, *refs),
            in_specs=[ANY] * 5,
            out_specs=[VMEM] * 3,
            out_shape=[
                shares(others)[0],
                jax.ShapeDtypeStruct((others * span, entries * rank), BF16),
                jax.ShapeDtypeStruct((8, entries * rank), jnp.int32),
            ],
            scratch_shapes=[
                pltpu.SMEM(far_rows.shape, jnp.int32),
                pltpu.SMEM(far_cols.shape, jnp.int32),
                pltpu.VMEM(x.shape, BF16),
                pltpu.VMEM(u.shape, BF16),
                pltpu.VMEM(v.shape, BF16),
                pltpu.SemaphoreType.DMA((5,)),
            ],
            compiler_params=params(others),
            cost_estimate=pl.CostEstimate(flops=1024, bytes_accessed=1024, transcendentals=0),
            name="mirror",
        )(far_rows, far_cols, x, u, v)
        keep = pl.pallas_call(
            lambda *refs: kept_kernel(clusters, exc, others, *refs),
            in_specs=[VMEM] * 2,
            out_specs=VMEM,
            out_shape=shares(others)[1],
            compiler_params=params(others),
            cost_estimate=pl.CostEstimate(flops=1024, bytes_accessed=1024, transcendentals=0),
            name="kept",
        )(mask, v)
        kinds = [F32] + [BF16] * (pairs - 1)
        one, far, *leaving = pl.pallas_call(
            lambda *refs: pair_kernel(span, *refs),
            in_specs=[VMEM] * 2,
            out_specs=[VMEM] * (2 * pairs),
            out_shape=[
                jax.ShapeDtypeStruct((rows * span, width), kind) for kind in kinds for rows in (1, others - 1)
            ],
            compiler_params=params(others),
            cost_estimate=pl.CostEstimate(flops=1024, bytes_accessed=1024, transcendentals=0),
            name="pair",
        )(keep, swap(send, "col", col_count, 1))
        one_leaving, leaving = leaving[::2], leaving[1::2]
        *leaving, x_near = lax.optimization_barrier((*leaving, charges))
        near = near_of(x_near)
        far = col_sum(far, leaving).astype(BF16)
        return (one, one_leaving), [far[i * span : (i + 1) * span] for i in range(others - 1)], near, lanes

    (one, one_leaving), far, near, lanes = stage(local)
    from_rows = [swap(part, "row", row_count, i + 2) for i, part in enumerate(far)]
    *got, lanes = lax.optimization_barrier((*got, lanes))
    whole, *got = lax.optimization_barrier((whole, *got))

    def forward():
        other = [swap(piece, "col", col_count, 1) for piece in got]
        early, *fetched = pl.pallas_call(
            lambda *refs: early_kernel(clusters, exc, len(got), *refs),
            in_specs=[VMEM] + [ANY] * (4 + len(got)),
            out_specs=[VMEM] * 5,
            out_shape=[
                jax.ShapeDtypeStruct((exc, entries * rank), F32),
                jax.ShapeDtypeStruct(v.shape, BF16),
                jax.ShapeDtypeStruct(u.shape, BF16),
                jax.ShapeDtypeStruct(near.shape, F32),
                jax.ShapeDtypeStruct(x.shape, BF16),
            ],
            scratch_shapes=[
                pltpu.VMEM((len(got) * span, panels), BF16),
                pltpu.SemaphoreType.DMA((4 + len(got),)),
            ],
            compiler_params=params(others),
            cost_estimate=pl.CostEstimate(flops=1024, bytes_accessed=1024, transcendentals=0),
            name="early",
        )(lanes, v, u, near, whole, *got)
        send, keep = pl.pallas_call(
            lambda *refs: forward_kernel(clusters, exc, *refs),
            in_specs=[VMEM] * (6 + len(other)),
            out_specs=[VMEM] * 2,
            out_shape=shares(1),
            compiler_params=params(others),
            cost_estimate=pl.CostEstimate(flops=1024, bytes_accessed=1024, transcendentals=0),
            name="forward",
        )(lanes, early, *fetched, *other)
        joined = col_sum(one, one_leaving).astype(BF16)
        return col_sum(*chunks(pair_sum(send, keep))) + swap(joined, "row", row_count, 1).astype(F32)

    total = stage(forward)
    for term in from_rows[:-1]:
        total = total + term.astype(F32)
    total = lax.optimization_barrier(total) + from_rows[-1].astype(F32)
    return total.reshape(clusters, exc, width)


def solution(mesh):
    placed = (
        P(("parts", "row"), None, None),
        P(("parts", "row", "col"), None, None),
        P(("parts", "row", "col")),
        P(("parts", "row", "col")),
        P(("parts", "row", "col"), None, None),
        P(("parts", "row", "col"), None, None),
        P(("parts", "row", "col")),
        P(("parts", "row", "col")),
    )
    return jax.shard_map(
        body,
        mesh=mesh,
        in_specs=placed,
        out_specs=P(("parts", "row"), None, "col"),
        check_vma=False,
    )
```
